32 devices in a mesh: rows: 4 (over z), segment: 4 (over y, x), tm: 2 (over core).
Axes of the slice: x: 2, y: 2, z: 4, core: 2. Of those that a mesh axis runs over, the one named last changes fastest.
Arguments:
- latents: bfloat16 [4, 8, 8, 128, 128], P(None, 'tm', 'rows'), may hold values from -40 to 40
- conv_first: bfloat16 [4, 3, 3, 3, 128, 128], P('segment'), may hold values from -0.109375 to 0.109375
- conv_second: bfloat16 [4, 3, 3, 3, 128, 128], P('segment'), may hold values from -0.109375 to 0.109375
- gain_first: bfloat16 [4, 128], P('segment'), may hold values from 0.099609375 to 1.8984375
- bias_first: bfloat16 [4, 128], P('segment'), may hold values from -1 to 1
- gain_second: bfloat16 [4, 128], P('segment'), may hold values from 0.099609375 to 1.8984375
- bias_second: bfloat16 [4, 128], P('segment'), may hold values from -1 to 1
Outputs:
- decoded: bfloat16 [4, 8, 8, 128, 128], P('segment', 'tm', 'rows')
The draws below stay inside these ranges and needn't reach their ends.
All inputs are finite; a program needn't handle non-finite values.
Results may differ from the reference program's by a relative error of at most 0.022.
Values may be sent and summed in bfloat16 or wider, within the bound.
A program may use at most 64 MiB of HBM per device.

```python
import jax
import jax.numpy as jnp
from jax import lax

C = 128
GROUPS = 32
F = 4
W = 128
MICRO = 4
FRAMES = 8
HEIGHT = 8
LAYERS = 4
N_TM = 2


def draw_latents(key, part):
    key_base, key_rows, key_cols, key_amp, key_spread, key_offset = jax.random.split(key, 6)
    shape = (MICRO, FRAMES, HEIGHT, W, C)
    row_scale = jnp.exp(jax.random.uniform(key_rows, (MICRO, HEIGHT), jnp.float32, -1.1513, 1.1513))
    col_scale = jnp.exp(jax.random.uniform(key_cols, (MICRO, W), jnp.float32, -1.1513, 1.1513))
    amplitude = jnp.exp(jax.random.uniform(key_amp, (MICRO,), jnp.float32, -1.1513, 1.1513))
    spread = jax.random.uniform(key_spread, (MICRO,), jnp.float32, 0.0, 3.0)
    offset = jax.random.normal(key_offset, (MICRO, C), jnp.float32) * spread[:, None]
    heights = jnp.arange(HEIGHT, dtype=jnp.float32) / HEIGHT - 0.5
    rising = jnp.exp(heights * 1.0986123)
    base = jax.random.normal(key_base, shape, jnp.float32)
    base = base + offset[:, None, None, None, :]
    factor = (row_scale * rising[None, :])[:, None, :, None, None] * col_scale[:, None, None, :, None]
    factor = factor * amplitude[:, None, None, None, None] * 0.05
    return jnp.clip(base * factor, -40.0, 40.0).astype(jnp.bfloat16)


def shard_levels(own_key, shape, cuts, low, high):
    def one(dim, parts):
        draws = jax.random.uniform(jax.random.fold_in(jax.random.fold_in(own_key, 6), dim), (parts,), jnp.float32, low / len(cuts), high / len(cuts))
        return jnp.repeat(jnp.exp(draws), shape[dim] // parts).reshape((-1,) + (1,) * (len(shape) - dim - 1))

    factor_of = one(*cuts[0])
    for cut in cuts[1:]:
        factor_of = factor_of * one(*cut)
    return factor_of


def noise(key, dims, scale, reach, cuts=(), kind=jnp.bfloat16):
    values = scale * jax.random.normal(key, dims, jnp.float32)
    if cuts:
        values = values * shard_levels(key, dims, cuts, -0.22, 0.18)
    return jnp.clip(values, -reach, reach).astype(kind)


def setup_inputs(seed: int = 0) -> dict:
    arg_keys = jax.random.split(jax.random.key(seed), 8)
    latents = draw_latents(jax.random.fold_in(arg_keys[7], 71), 0)
    conv_first = noise(arg_keys[1], (LAYERS, 3, 3, 3, C, C), (27 * C) ** -0.5, 0.109375, ((0, 4),))
    conv_second = noise(arg_keys[2], (LAYERS, 3, 3, 3, C, C), (27 * C) ** -0.5, 0.109375, ((0, 4),))
    gain_first = jnp.clip(1.0 + 0.18 * jax.random.normal(arg_keys[3], (LAYERS, C), jnp.float32), 0.099609375, 1.8984375).astype(jnp.bfloat16)
    bias_first = jnp.clip(jax.random.uniform(arg_keys[4], (LAYERS, C), jnp.float32, -1.0, 1.0) * shard_levels(arg_keys[4], (LAYERS, C), ((0, 4),), -0.4, 0.0), -1.0, 1.0).astype(jnp.bfloat16)
    gain_second = jnp.clip(1.0 + 0.18 * jax.random.normal(arg_keys[5], (LAYERS, C), jnp.float32), 0.099609375, 1.8984375).astype(jnp.bfloat16)
    bias_second = jnp.clip(jax.random.uniform(arg_keys[6], (LAYERS, C), jnp.float32, -1.0, 1.0) * shard_levels(arg_keys[6], (LAYERS, C), ((0, 4),), -0.4, 0.0), -1.0, 1.0).astype(jnp.bfloat16)
    return dict(latents=latents, conv_first=conv_first, conv_second=conv_second, gain_first=gain_first, bias_first=bias_first, gain_second=gain_second, bias_second=bias_second)


EPS = 1e-06

def normalize(values, norm_gain, norm_bias):
    width_group = C // GROUPS
    grouped = values.astype(jnp.float32).reshape(N_TM, F, HEIGHT, W, GROUPS, width_group)
    members = F * HEIGHT * W * width_group
    average = lax.optimization_barrier(jnp.sum(grouped, axis=(1, 2, 3, 5))) / members
    squares = lax.optimization_barrier(jnp.sum(grouped * grouped, axis=(1, 2, 3, 5))) / members
    inverse = lax.rsqrt(squares - average * average + EPS)
    scaled = (grouped - average[:, None, None, None, :, None]) * inverse[:, None, None, None, :, None]
    scaled = scaled.reshape(values.shape) * norm_gain.astype(jnp.float32) + norm_bias.astype(jnp.float32)
    return jax.nn.silu(scaled).astype(jnp.bfloat16)

def convolve(active, kernel):
    result = lax.conv_general_dilated(active[None], kernel, (1, 1, 1), ((2, 0), (1, 1), (1, 1)), dimension_numbers=('NDHWC', 'DHWIO', 'NDHWC'), preferred_element_type=jnp.float32)
    return result[0]

def reference(latents, conv_first, conv_second, gain_first, bias_first, gain_second, bias_second):

    def decode(values):
        for layer_index in range(LAYERS):
            active = normalize(values, gain_first[layer_index], bias_first[layer_index])
            hidden = convolve(active, conv_first[layer_index]).astype(jnp.bfloat16)
            active = normalize(hidden, gain_second[layer_index], bias_second[layer_index])
            values = (values.astype(jnp.float32) + convolve(active, conv_second[layer_index])).astype(jnp.bfloat16)
        return values
    return lax.map(decode, latents)
```

```python
import functools

import jax
import jax.numpy as jnp
from jax import lax
from jax.experimental import pallas as pl
from jax.experimental.pallas import tpu as pltpu
from jax.sharding import PartitionSpec as P

GROUPS = 32


EPS = 1e-06


def passed_along(value, axis, steps):
    count = lax.axis_size(axis)
    initial, last = (max(0, -steps), min(count, count - steps))
    return lax.ppermute(value, axis, [(source, source + steps) for source in range(initial, last)])


def padded_2(block, sides, width):
    for axis, dim in sides:
        count = lax.axis_size(axis)
        forward = [(i, i + 1) for i in range(count - 1)]
        backward = [(target, source) for source, target in forward]
        low = lax.ppermute(
            lax.slice_in_dim(block, block.shape[dim] - width, None, axis=dim), axis, forward
        )
        high = lax.ppermute(lax.slice_in_dim(block, 0, width, axis=dim), axis, backward)
        block = jnp.concatenate([low, block, high], axis=dim)
    return block


def normalize(values, norm_gain, norm_bias):
    frames, rows_here, columns, channels = values.shape
    width_group = channels // GROUPS
    grouped = values.astype(jnp.float32).reshape(frames, rows_here, columns, GROUPS, width_group)
    totals = lax.psum(
        (jnp.sum(grouped, axis=(0, 1, 2, 4)), jnp.sum(grouped * grouped, axis=(0, 1, 2, 4))), "rows"
    )
    members = frames * rows_here * lax.axis_size("rows") * columns * width_group
    average = totals[0] / members
    squares = totals[1] / members
    inverse = lax.rsqrt(squares - average * average + EPS)
    scaled = (grouped - average[:, None]) * inverse[:, None]
    scaled = scaled.reshape(values.shape) * norm_gain.astype(jnp.float32) + norm_bias.astype(
        jnp.float32
    )
    return jax.nn.silu(scaled).astype(jnp.bfloat16)


def convolve(active, kernel):
    previous = passed_along(active[-2:], "tm", 1)
    extended = jnp.concatenate([previous, active], axis=0)
    padded = padded_2(extended, (("rows", 1),), 1)
    padded = jnp.pad(padded, ((0, 0), (0, 0), (1, 1), (0, 0)))
    result = lax.conv_general_dilated(
        padded[None],
        kernel,
        (1, 1, 1),
        "VALID",
        dimension_numbers=("NDHWC", "DHWIO", "NDHWC"),
        preferred_element_type=jnp.float32,
    )
    return result[0]


def residual_block(values, params):
    first, second, gain_one, bias_one, gain_two, bias_two = params
    active = normalize(values, gain_one, bias_one)
    hidden = convolve(active, first).astype(jnp.bfloat16)
    active = normalize(hidden, gain_two, bias_two)
    return (values.astype(jnp.float32) + convolve(active, second)).astype(jnp.bfloat16)


def plain_body(latents, conv_first, conv_second, gain_first, bias_first, gain_second, bias_second):
    segments = lax.axis_size("segment")
    micro = latents.shape[0]
    per_segment = micro // segments
    position = lax.axis_index("segment")
    small = jnp.stack([gain_first, bias_first, gain_second, bias_second], axis=1)
    small = lax.all_gather(small, "segment", axis=0, tiled=True)
    first = lax.all_gather(conv_first, "segment", axis=0, tiled=True)
    second = lax.all_gather(conv_second, "segment", axis=0, tiled=True)
    outs = []
    for index in range(per_segment):
        values = lax.dynamic_index_in_dim(
            latents, position * per_segment + index, 0, keepdims=False
        )
        for layer in range(first.shape[0]):
            gains = small[layer]
            values = residual_block(
                values, (first[layer], second[layer], gains[0], gains[1], gains[2], gains[3])
            )
        outs.append(values)
    return jnp.stack(outs)


MESH = pl.DeviceIdType.MESH
ROWS = 16


def group_sums(values):
    lanes = values.shape[-1]
    lane = lax.broadcasted_iota(jnp.int32, values.shape, 1)
    values = values + jnp.where(
        lax.rem(lane, 2) == 0, pltpu.roll(values, lanes - 1, 1), pltpu.roll(values, 1, 1)
    )
    return values + jnp.where(
        lax.rem(lane, 4) < 2, pltpu.roll(values, lanes - 2, 1), pltpu.roll(values, 2, 1)
    )


def tap_block(weights, dt, dy, dx, channels):
    if dt < 0 or dt > 2:
        return jnp.zeros((channels, channels), jnp.bfloat16)
    return weights[dt, dy, dx]


def decode_kernel(
    count,
    latents,
    first,
    second,
    small,
    out,
    staged,
    turned,
    values,
    hidden,
    sibling,
    edges,
    stats,
    active,
    own_sem,
    in_send,
    in_recv,
    stat_send,
    stat_recv,
    edge_send,
    edge_recv,
    sib_send,
    sib_recv,
    out_send,
    out_recv,
    free_sem,
):
    frames, height, width, channels = staged.shape
    local_rows = height // count
    both = 2 * height
    row = lax.axis_index("rows")
    segment = lax.axis_index("segment")
    span = lax.axis_index("tm")
    members = frames * height * width * count * (channels // GROUPS)

    def at(rows_index, tm_index):
        return {"rows": rows_index, "tm": tm_index}

    barrier = pltpu.get_barrier_semaphore()
    for k in range(count):
        other = lax.rem(row + k, count)
        if k:
            pl.semaphore_signal(barrier, inc=1, device_id=at(other, span), device_id_type=MESH)
        pl.semaphore_signal(barrier, inc=1, device_id=at(other, 1 - span), device_id_type=MESH)
    pl.semaphore_wait(barrier, 2 * count - 1)

    def incoming(k, me, to):
        return pltpu.make_async_remote_copy(
            src_ref=latents.at[segment, :, :, pl.ds(pl.multiple_of(to * width, width), width)],
            dst_ref=staged.at[:, pl.ds(me * local_rows, local_rows)],
            send_sem=in_send.at[k],
            recv_sem=in_recv.at[me],
            device_id=at(to, span),
            device_id_type=MESH,
        )

    for k in range(1, count):
        incoming(k, row, lax.rem(row + k, count)).start()
    own = pltpu.make_async_copy(
        latents.at[segment, :, :, pl.ds(pl.multiple_of(row * width, width), width)],
        staged.at[:, pl.ds(row * local_rows, local_rows)],
        own_sem,
    )
    own.start()
    own.wait()
    for k in range(1, count):
        other = lax.rem(row + k, count)
        incoming(k, other, row).wait_recv()

    for f in range(frames):
        turned[f] = staged[f].astype(jnp.float32).reshape(height * width, channels)
    zero = jnp.zeros((height, channels), jnp.float32)

    def turn(x, carry):
        total, squares = carry
        for q in range(2):
            tile = jnp.concatenate(
                [turned[q + 2 * p, pl.ds(x, height, stride=width)] for p in range(2)], axis=0
            )
            values[q, x] = tile.astype(jnp.bfloat16)
            total = total + tile[:height] + tile[height:]
            tile = tile * tile
            squares = squares + tile[:height] + tile[height:]
        return total, squares

    partial = lax.fori_loop(0, width, turn, (zero, zero), unroll=4)
    for k in range(1, count):
        incoming(k, row, lax.rem(row + k, count)).wait_send()

    def stat_copy(par, k, me, to, tm_from, tm_to):
        slot = tm_from * count + me
        cross = 0 if tm_from is tm_to else count
        return pltpu.make_async_remote_copy(
            src_ref=stats.at[par, slot],
            dst_ref=stats.at[par, slot],
            send_sem=stat_send.at[par, k + cross],
            recv_sem=stat_recv.at[par, slot],
            device_id=at(to, tm_to),
            device_id_type=MESH,
        )

    def edge_copy(par, source, side, tm_from, tm_to, to):
        return pltpu.make_async_remote_copy(
            src_ref=source.at[:, width - 1 if side == 0 else 0],
            dst_ref=edges.at[par, side, tm_from],
            send_sem=edge_send.at[par, side, tm_to],
            recv_sem=edge_recv.at[par, side, tm_from],
            device_id=at(to, tm_to),
            device_id_type=MESH,
        )

    def sib_copy(par, source):
        return pltpu.make_async_remote_copy(
            src_ref=source,
            dst_ref=sibling.at[par],
            send_sem=sib_send.at[par],
            recv_sem=sib_recv.at[par],
            device_id=at(row, 1),
            device_id_type=MESH,
        )

    def each_send(par, source, act):
        for k in range(1, count):
            act(stat_copy(par, k, row, lax.rem(row + k, count), span, span))

        @pl.when(span == 0)
        def _():
            for k in range(count):
                act(stat_copy(par, k, row, lax.rem(row + k, count), 0, 1))

        for side, there in ((0, row < count - 1), (1, row > 0)):

            @pl.when(there)
            def _(side=side):
                to = row + 1 if side == 0 else row - 1
                act(edge_copy(par, source, side, span, span, to))

                @pl.when(span == 0)
                def _():
                    act(edge_copy(par, source, side, 0, 1, to))

        @pl.when(span == 0)
        def _():
            act(sib_copy(par, source))

    def exchange(par, source, partial):
        index = lax.broadcasted_iota(jnp.int32, (8, channels), 0)
        total = jnp.sum(partial[0], axis=0, keepdims=True)
        squares = jnp.sum(partial[1], axis=0, keepdims=True)
        stats[par, span * count + row] = jnp.where(
            index == 0, total, jnp.where(index == 1, squares, 0.0)
        )
        each_send(par, source, lambda copy: copy.start())

    def finish_sends(par, source):
        each_send(par, source, lambda copy: copy.wait_send())

    def receive(par, source):
        for side, there in ((0, row > 0), (1, row < count - 1)):

            @pl.when(there)
            def _(side=side):
                edge_copy(par, source, side, span, span, row).wait_recv()

                @pl.when(span == 1)
                def _():
                    edge_copy(par, source, side, 0, 1, row).wait_recv()

        @pl.when(span == 1)
        def _():
            sib_copy(par, source).wait_recv()
            for k in range(count):
                stat_copy(par, k, lax.rem(row + k, count), row, 0, 1).wait_recv()

        for k in range(1, count):
            stat_copy(par, k, lax.rem(row + k, count), row, span, span).wait_recv()

    def moments(par, base, gain):
        total = stats[par, base]
        for k in range(1, count):
            total = total + stats[par, base + k]
        total = group_sums(total) / members
        average = total[0:1]
        return average, lax.rsqrt(total[1:2] - average * average + EPS) * gain

    def activate(par, source, gain, bias):
        mine = moments(par, span * count, gain)
        before = moments(par, 0, gain)
        later = span > 0
        index = lax.broadcasted_iota(jnp.int32, (1, height, channels), 1)

        def silu(tile, moment):
            half = ((tile - moment[0]) * moment[1] + bias) * 0.5
            return half + half * jnp.tanh(half)

        def shifted(a, dy):
            if dy == 0:
                return jnp.where(index == 0, 0.0, pltpu.roll(a, 1, 1))
            if dy == 2:
                return jnp.where(index == height - 1, 0.0, pltpu.roll(a, height - 1, 1))
            return a

        def put(q, where, size, tile, older, valid):
            a = silu(tile.astype(jnp.float32), mine).reshape(2 * size, height, channels)
            b = silu(older.astype(jnp.float32)[:, height:], before)
            b = jnp.where(later, b, 0.0)
            if valid is not None:
                a = jnp.where(valid, a, 0.0)
                b = jnp.where(valid, b, 0.0)
            for dy in range(3):
                now = shifted(a, dy).reshape(size, both, channels)
                old = shifted(b, dy)
                active[2 + q, dy, where] = now.astype(jnp.bfloat16)
                active[q, dy, where] = jnp.concatenate([old, now[:, :height]], axis=1).astype(
                    jnp.bfloat16
                )

        step = min(8, width)

        @pl.loop(0, width // step)
        def _(i):
            x = i * step
            for q in range(2):
                put(
                    q,
                    pl.ds(x + 1, step),
                    step,
                    source[q, pl.ds(x, step)],
                    sibling[par, q, pl.ds(x, step)],
                    None,
                )

        for side, there in ((0, row > 0), (1, row < count - 1)):
            for q in range(2):
                put(
                    q,
                    pl.ds(0 if side == 0 else width + 1, 1),
                    1,
                    edges[par, side, span, q][None],
                    edges[par, side, 0, q][None],
                    there,
                )

    def convolution(weights, store):
        step = width
        partial = None
        for x in range(0, width, step):
            left, right = [], []
            for dy in range(3):
                for dx in range(3):
                    for k in (1, 2, 0, 3):
                        left.append(
                            active[k, dy, x + dx : x + dx + step].reshape(step * both, channels)
                        )
                        right.append(
                            jnp.concatenate(
                                [
                                    tap_block(weights, k - q, dy, dx, channels)
                                    for q in range(2)
                                ],
                                axis=1,
                            )
                        )
            result = jnp.dot(
                jnp.concatenate(left, axis=1),
                jnp.concatenate(right, axis=0),
                preferred_element_type=jnp.float32,
            )
            for q in range(2):
                tile = store(
                    q, x, step, result[:, q * channels : (q + 1) * channels].reshape(
                        step, both, channels
                    )
                )
                tile = tile.astype(jnp.float32).reshape(-1, height, channels)
                total, squares = jnp.sum(tile, axis=0), jnp.sum(tile * tile, axis=0)
                if partial is None:
                    partial = (total, squares)
                else:
                    partial = (partial[0] + total, partial[1] + squares)
        return partial

    def store_hidden(q, x, step, tile):
        tile = tile.astype(jnp.bfloat16)
        hidden[q, x : x + step] = tile
        return tile

    def store_values(q, x, step, tile):
        tile = (values[q, x : x + step].astype(jnp.float32) + tile).astype(jnp.bfloat16)
        values[q, x : x + step] = tile
        return tile

    def give(when):
        @pl.when((span == 1) & when)
        def _():
            pl.semaphore_signal(free_sem, inc=1, device_id=at(row, 0), device_id_type=MESH)

    def take(when):
        @pl.when((span == 0) & when)
        def _():
            pl.semaphore_wait(free_sem, 1)

    layers = first.shape[0]
    exchange(0, values, partial)

    @pl.loop(0, layers)
    def _(layer):
        receive(0, values)
        give(layer > 0)
        activate(0, values, small[layer, 0:1], small[layer, 1:2])
        partial = convolution(first.at[layer], store_hidden)
        finish_sends(0, values)
        take(layer > 0)
        exchange(1, hidden, partial)
        receive(1, hidden)
        give(layer < layers - 1)
        activate(1, hidden, small[layer, 2:3], small[layer, 3:4])
        partial = convolution(second.at[layer], store_values)
        finish_sends(1, hidden)

        @pl.when(layer < layers - 1)
        def _():
            take(layer >= 0)
            exchange(0, values, partial)

    for q in range(2):
        whole = values[q].astype(jnp.float32)
        for p in range(2):
            turned[q + 2 * p] = whole[:, p * height : (p + 1) * height].reshape(
                height * width, channels
            )
    for f in range(frames):
        for y in range(height):
            staged[f, y] = turned[f, pl.ds(y, width, stride=height)].astype(jnp.bfloat16)

    def outgoing(k, me, to):
        return pltpu.make_async_remote_copy(
            src_ref=staged.at[:, pl.ds(to * local_rows, local_rows)],
            dst_ref=out.at[0, :, :, pl.ds(pl.multiple_of(me * width, width), width)],
            send_sem=out_send.at[k],
            recv_sem=out_recv.at[me],
            device_id=at(to, span),
            device_id_type=MESH,
        )

    for k in range(1, count):
        outgoing(k, row, lax.rem(row + k, count)).start()
    own = pltpu.make_async_copy(
        staged.at[:, pl.ds(row * local_rows, local_rows)],
        out.at[0, :, :, pl.ds(pl.multiple_of(row * width, width), width)],
        own_sem,
    )
    own.start()
    own.wait()
    for k in range(1, count):
        other = lax.rem(row + k, count)
        outgoing(k, other, row).wait_recv()
        outgoing(k, row, other).wait_send()


def body(latents, conv_first, conv_second, gain_first, bias_first, gain_second, bias_second):
    micro, frames, local_rows, columns, channels = latents.shape
    count = lax.axis_size("rows")
    width = columns // count
    height = local_rows * count
    small = jnp.stack([gain_first, bias_first, gain_second, bias_second], axis=1)
    small = lax.all_gather(small, "segment", axis=0, tiled=True).astype(jnp.float32)
    first = lax.all_gather(conv_first, "segment", axis=0, tiled=True)
    second = lax.all_gather(conv_second, "segment", axis=0, tiled=True)
    both = 2 * height
    dma = pltpu.SemaphoreType.DMA
    return pl.pallas_call(
        functools.partial(decode_kernel, count),
        out_shape=jax.ShapeDtypeStruct((1, frames, local_rows, columns, channels), jnp.bfloat16),
        in_specs=[pl.BlockSpec(memory_space=pl.ANY)]
        + [pl.BlockSpec(memory_space=pltpu.VMEM)] * 3,
        out_specs=pl.BlockSpec(memory_space=pltpu.VMEM),
        scratch_shapes=[
            pltpu.VMEM((frames, height, width, channels), jnp.bfloat16),
            pltpu.VMEM((frames, height * width, channels), jnp.float32),
            pltpu.VMEM((2, width, both, channels), jnp.bfloat16),
            pltpu.VMEM((2, width, both, channels), jnp.bfloat16),
            pltpu.VMEM((2, 2, width, both, channels), jnp.bfloat16),
            pltpu.VMEM((2, 2, 2, 2, both, channels), jnp.bfloat16),
            pltpu.VMEM((2, 2 * count, 8, channels), jnp.float32),
            pltpu.VMEM((4, 3, width + 2, both, channels), jnp.bfloat16),
            dma,
            dma((count,)),
            dma((count,)),
            dma((2, 2 * count)),
            dma((2, 2 * count)),
            dma((2, 2, 2)),
            dma((2, 2, 2)),
            dma((2,)),
            dma((2,)),
            dma((count,)),
            dma((count,)),
            pltpu.SemaphoreType.REGULAR,
        ],
        compiler_params=pltpu.CompilerParams(
            collective_id=0, has_side_effects=True, vmem_limit_bytes=48 * 2**20
        ),
    )(latents, first, second, small)


def solution(mesh):
    in_specs = (
        P(None, "tm", "rows", None, None),
        P("segment", None, None, None, None, None),
        P("segment", None, None, None, None, None),
        P("segment", None),
        P("segment", None),
        P("segment", None),
        P("segment", None),
    )
    out_specs = P("segment", "tm", "rows", None, None)
    sizes = dict(mesh.shape)

    def run(latents, *params):
        micro, frames, height, columns, channels = latents.shape
        count = sizes["rows"]
        fits = (
            micro == sizes["segment"]
            and sizes["tm"] == 2
            and frames == 8
            and height % (8 * 1) == 0
            and columns % (count * ROWS) == 0
            and channels == 4 * GROUPS
        )
        inner = body if fits else plain_body
        return jax.shard_map(
            inner, mesh=mesh, in_specs=in_specs, out_specs=out_specs, check_vma=False
        )(latents, *params)

    return run
```

```python
import functools

import jax
import jax.numpy as jnp
from jax import lax
from jax.experimental import pallas as pl
from jax.experimental.pallas import tpu as pltpu
from jax.sharding import PartitionSpec as P

GROUPS = 32


EPS = 1e-06


def passed_along(value, axis, steps):
    count = lax.axis_size(axis)
    initial, last = (max(0, -steps), min(count, count - steps))
    return lax.ppermute(value, axis, [(source, source + steps) for source in range(initial, last)])


def padded_2(block, sides, width):
    for axis, dim in sides:
        count = lax.axis_size(axis)
        forward = [(i, i + 1) for i in range(count - 1)]
        backward = [(target, source) for source, target in forward]
        low = lax.ppermute(
            lax.slice_in_dim(block, block.shape[dim] - width, None, axis=dim), axis, forward
        )
        high = lax.ppermute(lax.slice_in_dim(block, 0, width, axis=dim), axis, backward)
        block = jnp.concatenate([low, block, high], axis=dim)
    return block


def normalize(values, norm_gain, norm_bias):
    frames, rows_here, columns, channels = values.shape
    width_group = channels // GROUPS
    grouped = values.astype(jnp.float32).reshape(frames, rows_here, columns, GROUPS, width_group)
    totals = lax.psum(
        (jnp.sum(grouped, axis=(0, 1, 2, 4)), jnp.sum(grouped * grouped, axis=(0, 1, 2, 4))), "rows"
    )
    members = frames * rows_here * lax.axis_size("rows") * columns * width_group
    average = totals[0] / members
    squares = totals[1] / members
    inverse = lax.rsqrt(squares - average * average + EPS)
    scaled = (grouped - average[:, None]) * inverse[:, None]
    scaled = scaled.reshape(values.shape) * norm_gain.astype(jnp.float32) + norm_bias.astype(
        jnp.float32
    )
    return jax.nn.silu(scaled).astype(jnp.bfloat16)


def convolve(active, kernel):
    previous = passed_along(active[-2:], "tm", 1)
    extended = jnp.concatenate([previous, active], axis=0)
    padded = padded_2(extended, (("rows", 1),), 1)
    padded = jnp.pad(padded, ((0, 0), (0, 0), (1, 1), (0, 0)))
    result = lax.conv_general_dilated(
        padded[None],
        kernel,
        (1, 1, 1),
        "VALID",
        dimension_numbers=("NDHWC", "DHWIO", "NDHWC"),
        preferred_element_type=jnp.float32,
    )
    return result[0]


def residual_block(values, params):
    first, second, gain_one, bias_one, gain_two, bias_two = params
    active = normalize(values, gain_one, bias_one)
    hidden = convolve(active, first).astype(jnp.bfloat16)
    active = normalize(hidden, gain_two, bias_two)
    return (values.astype(jnp.float32) + convolve(active, second)).astype(jnp.bfloat16)


def plain_body(latents, conv_first, conv_second, gain_first, bias_first, gain_second, bias_second):
    segments = lax.axis_size("segment")
    micro = latents.shape[0]
    per_segment = micro // segments
    position = lax.axis_index("segment")
    small = jnp.stack([gain_first, bias_first, gain_second, bias_second], axis=1)
    small = lax.all_gather(small, "segment", axis=0, tiled=True)
    first = lax.all_gather(conv_first, "segment", axis=0, tiled=True)
    second = lax.all_gather(conv_second, "segment", axis=0, tiled=True)
    outs = []
    for index in range(per_segment):
        values = lax.dynamic_index_in_dim(
            latents, position * per_segment + index, 0, keepdims=False
        )
        for layer in range(first.shape[0]):
            gains = small[layer]
            values = residual_block(
                values, (first[layer], second[layer], gains[0], gains[1], gains[2], gains[3])
            )
        outs.append(values)
    return jnp.stack(outs)


MESH = pl.DeviceIdType.MESH
ROWS = 16


def group_sums(values):
    lanes = values.shape[-1]
    lane = lax.broadcasted_iota(jnp.int32, values.shape, 1)
    values = values + jnp.where(
        lax.rem(lane, 2) == 0, pltpu.roll(values, lanes - 1, 1), pltpu.roll(values, 1, 1)
    )
    return values + jnp.where(
        lax.rem(lane, 4) < 2, pltpu.roll(values, lanes - 2, 1), pltpu.roll(values, 2, 1)
    )


def tap_block(weights, dt, dy, dx, channels):
    if dt < 0 or dt > 2:
        return jnp.zeros((channels, channels), jnp.bfloat16)
    return weights[dt, dy, dx]


def decode_kernel(
    count,
    latents,
    first,
    second,
    gain_first,
    bias_first,
    gain_second,
    bias_second,
    out,
    staged,
    turned,
    values,
    hidden,
    sibling,
    edges,
    stats,
    active,
    own_sem,
    in_send,
    in_recv,
    stat_send,
    stat_recv,
    edge_send,
    edge_recv,
    sib_send,
    sib_recv,
    out_send,
    out_recv,
    free_sem,
    kernels,
    small,
    param_send,
    param_recv,
    load_sem,
    w_send,
    w_recv,
    half_send,
    half_recv,
):
    frames, height, width, channels = staged.shape
    local_rows = height // count
    both = 2 * height
    row = lax.axis_index("rows")
    segment = lax.axis_index("segment")
    span = lax.axis_index("tm")
    members = frames * height * width * count * (channels // GROUPS)

    def at(rows_index, tm_index):
        return {"rows": rows_index, "tm": tm_index}

    barrier = pltpu.get_barrier_semaphore()
    for k in range(count):
        other = lax.rem(row + k, count)
        if k:
            pl.semaphore_signal(barrier, inc=1, device_id=at(other, span), device_id_type=MESH)
        pl.semaphore_signal(barrier, inc=1, device_id=at(other, 1 - span), device_id_type=MESH)
    for k in range(1, 4):
        pl.semaphore_signal(
            barrier, inc=1, device_id={"segment": segment ^ k}, device_id_type=MESH
        )
    pl.semaphore_wait(barrier, 2 * count + 2)

    given = (first, second)
    layers = kernels.shape[0] // 2
    depth = channels // 2

    def tensor_part(ref, half, chunk, chunks):
        rows = pl.ds(pl.multiple_of(half * depth, depth), depth)
        size = 3 // chunks
        return ref.at[pl.ds(chunk * size, size), :, :, rows]

    def chunks_of(j):
        return 3 if j < 2 else 1

    def remote_half(j, chunk, source, to, slot):
        return pltpu.make_async_remote_copy(
            src_ref=tensor_part(source, span, chunk, chunks_of(j)),
            dst_ref=tensor_part(kernels.at[j], span, chunk, chunks_of(j)),
            send_sem=w_send.at[j, slot, chunk],
            recv_sem=w_recv.at[j, chunk],
            device_id={"segment": to},
            device_id_type=MESH,
        )

    def core_half(j, chunk, half):
        return pltpu.make_async_remote_copy(
            src_ref=tensor_part(kernels.at[j], half, chunk, chunks_of(j)),
            dst_ref=tensor_part(kernels.at[j], half, chunk, chunks_of(j)),
            send_sem=half_send.at[j, chunk],
            recv_sem=half_recv.at[j, chunk],
            device_id={"tm": 1 - span},
            device_id_type=MESH,
        )

    def move(name):
        kind, j = name[0], int(name[1])
        away = segment ^ (j // 2)
        source = given[j % 2].at[0]
        first_to = segment ^ (1 + span)
        second_to = segment ^ (2 - span)
        passes = away == 1 + span
        each = range(chunks_of(j))
        if kind == "P":

            @pl.when(away == 0)
            def _():
                for c in each:
                    remote_half(j, c, source, first_to, 0).start()

        if kind == "S":

            @pl.when(away == 0)
            def _():
                for c in each:
                    remote_half(j, c, source, first_to, 0).wait_send()
                for c in each:
                    remote_half(j, c, source, second_to, 1).start()

        if kind == "F":

            @pl.when(passes)
            def _():
                for c in each:
                    remote_half(j, c, kernels.at[j], second_to, 0).wait_recv()
                    remote_half(j, c, kernels.at[j], second_to, 0).start()
                    core_half(j, c, span).start()

        if kind == "R":

            @pl.when((away > 0) & jnp.logical_not(passes))
            def _():
                for c in each:
                    remote_half(j, c, kernels.at[j], second_to, 0).wait_recv()
                    core_half(j, c, span).start()

        if kind == "G":

            @pl.when(away > 0)
            def _():
                for c in each:
                    core_half(j, c, 1 - span).wait_recv()

            @pl.when(away == 0)
            def _():
                pltpu.make_async_copy(source, kernels.at[j], load_sem.at[j]).wait()

        if kind == "W":

            @pl.when(away == 0)
            def _():
                for c in each:
                    remote_half(j, c, source, second_to, 1).wait_send()

            @pl.when(passes)
            def _():
                for c in each:
                    remote_half(j, c, kernels.at[j], second_to, 0).wait_send()

            @pl.when(away > 0)
            def _():
                for c in each:
                    core_half(j, c, span).wait_send()

    plan = {
        "start": ("P0", "P2", "P4", "P6",),
        "early": ("F0", "S0",),
        "a0": ("R0", "P1", "S2", "S4", "S6",),
        "b0": ("S1", "G0",),
        "a1": ("F1", "P7",),
        "b1": ("F2", "P3", "P5", "R1", "G1",),
        "a2": ("S3", "S5", "S7", "F4",),
        "b2": ("R2", "F3", "G2",),
        "a3": ("F5", "F6",),
        "b3": ("R3", "R4", "G3",),
        "a4": ("F7",),
        "b4": ("R5", "R6", "G4",),
        "a5": ("R7",),
        "b5": ("G5",),
        "b6": ("G6",),
        "b7": ("G7",),
        "end": ("W0", "W1", "W2", "W3", "W4", "W5", "W6", "W7",),
    }

    def moves(point):
        for name in plan.get(point, ()):
            move(name)

    def moves_at(letter, which, layer):
        for known in range(layers):
            point = letter + str(2 * known + which)
            if point in plan:

                @pl.when(layer == known)
                def _(point=point):
                    moves(point)

    def incoming(k, me, to):
        return pltpu.make_async_remote_copy(
            src_ref=latents.at[segment, :, :, pl.ds(pl.multiple_of(to * width, width), width)],
            dst_ref=staged.at[:, pl.ds(me * local_rows, local_rows)],
            send_sem=in_send.at[k],
            recv_sem=in_recv.at[me],
            device_id=at(to, span),
            device_id_type=MESH,
        )

    moves("start")
    for k in range(1, count):
        incoming(k, row, lax.rem(row + k, count)).start()
    for j in range(2 * layers):

        @pl.when(segment == j // 2)
        def _(j=j):
            pltpu.make_async_copy(given[j % 2].at[0], kernels.at[j], load_sem.at[j]).start()

    index = lax.broadcasted_iota(jnp.int32, (8, channels), 0)
    packed = jnp.zeros((8, channels), jnp.float32)
    for k, ref in enumerate((gain_first, bias_first, gain_second, bias_second)):
        packed = jnp.where(index == k, ref[...].astype(jnp.float32), packed)
    small[segment] = packed

    def param_copy(k, me):
        return pltpu.make_async_remote_copy(
            src_ref=small.at[me],
            dst_ref=small.at[me],
            send_sem=param_send.at[k],
            recv_sem=param_recv.at[me],
            device_id={"segment": segment ^ k},
            device_id_type=MESH,
        )

    for k in range(1, 4):
        param_copy(k, segment).start()
    own = pltpu.make_async_copy(
        latents.at[segment, :, :, pl.ds(pl.multiple_of(row * width, width), width)],
        staged.at[:, pl.ds(row * local_rows, local_rows)],
        own_sem,
    )
    own.start()
    moves("early")
    own.wait()
    for k in range(1, count):
        other = lax.rem(row + k, count)
        incoming(k, other, row).wait_recv()

    for f in range(frames):
        turned[f] = staged[f].astype(jnp.float32).reshape(height * width, channels)
    zero = jnp.zeros((height, channels), jnp.float32)

    def turn(x, carry):
        total, squares = carry
        for q in range(2):
            tile = jnp.concatenate(
                [turned[q + 2 * p, pl.ds(x, height, stride=width)] for p in range(2)], axis=0
            )
            values[q, x] = tile.astype(jnp.bfloat16)
            total = total + tile[:height] + tile[height:]
            tile = tile * tile
            squares = squares + tile[:height] + tile[height:]
        return total, squares

    partial = lax.fori_loop(0, width, turn, (zero, zero), unroll=4)
    for k in range(1, count):
        incoming(k, row, lax.rem(row + k, count)).wait_send()

    def stat_copy(par, k, me, to, tm_from, tm_to):
        slot = tm_from * count + me
        cross = 0 if tm_from is tm_to else count
        return pltpu.make_async_remote_copy(
            src_ref=stats.at[par, slot],
            dst_ref=stats.at[par, slot],
            send_sem=stat_send.at[par, k + cross],
            recv_sem=stat_recv.at[par, slot],
            device_id=at(to, tm_to),
            device_id_type=MESH,
        )

    def edge_copy(par, source, side, tm_from, tm_to, to):
        return pltpu.make_async_remote_copy(
            src_ref=source.at[:, width - 1 if side == 0 else 0],
            dst_ref=edges.at[par, side, tm_from],
            send_sem=edge_send.at[par, side, tm_to],
            recv_sem=edge_recv.at[par, side, tm_from],
            device_id=at(to, tm_to),
            device_id_type=MESH,
        )

    def sib_copy(par, source):
        return pltpu.make_async_remote_copy(
            src_ref=source,
            dst_ref=sibling.at[par],
            send_sem=sib_send.at[par],
            recv_sem=sib_recv.at[par],
            device_id=at(row, 1),
            device_id_type=MESH,
        )

    def each_send(par, source, act):
        for k in range(1, count):
            act(stat_copy(par, k, row, lax.rem(row + k, count), span, span))

        @pl.when(span == 0)
        def _():
            for k in range(count):
                act(stat_copy(par, k, row, lax.rem(row + k, count), 0, 1))

        for side, there in ((0, row < count - 1), (1, row > 0)):

            @pl.when(there)
            def _(side=side):
                to = row + 1 if side == 0 else row - 1
                act(edge_copy(par, source, side, span, span, to))

                @pl.when(span == 0)
                def _():
                    act(edge_copy(par, source, side, 0, 1, to))

        @pl.when(span == 0)
        def _():
            act(sib_copy(par, source))

    def exchange(par, source, partial):
        index = lax.broadcasted_iota(jnp.int32, (8, channels), 0)
        total = jnp.sum(partial[0], axis=0, keepdims=True)
        squares = jnp.sum(partial[1], axis=0, keepdims=True)
        stats[par, span * count + row] = jnp.where(
            index == 0, total, jnp.where(index == 1, squares, 0.0)
        )
        each_send(par, source, lambda copy: copy.start())

    def finish_sends(par, source):
        each_send(par, source, lambda copy: copy.wait_send())

    def receive(par, source):
        for side, there in ((0, row > 0), (1, row < count - 1)):

            @pl.when(there)
            def _(side=side):
                edge_copy(par, source, side, span, span, row).wait_recv()

                @pl.when(span == 1)
                def _():
                    edge_copy(par, source, side, 0, 1, row).wait_recv()

        @pl.when(span == 1)
        def _():
            sib_copy(par, source).wait_recv()
            for k in range(count):
                stat_copy(par, k, lax.rem(row + k, count), row, 0, 1).wait_recv()

        for k in range(1, count):
            stat_copy(par, k, lax.rem(row + k, count), row, span, span).wait_recv()

    def moments(par, base, gain):
        total = stats[par, base]
        for k in range(1, count):
            total = total + stats[par, base + k]
        total = group_sums(total) / members
        average = total[0:1]
        return average, lax.rsqrt(total[1:2] - average * average + EPS) * gain

    def activate(par, source, gain, bias):
        mine = moments(par, span * count, gain)
        before = moments(par, 0, gain)
        later = span > 0
        index = lax.broadcasted_iota(jnp.int32, (1, height, channels), 1)

        def silu(tile, moment):
            half = ((tile - moment[0]) * moment[1] + bias) * 0.5
            return half + half * jnp.tanh(half)

        def shifted(a, dy):
            if dy == 0:
                return jnp.where(index == 0, 0.0, pltpu.roll(a, 1, 1))
            if dy == 2:
                return jnp.where(index == height - 1, 0.0, pltpu.roll(a, height - 1, 1))
            return a

        def put(q, where, size, tile, older, valid):
            a = silu(tile.astype(jnp.float32), mine).reshape(2 * size, height, channels)
            b = silu(older.astype(jnp.float32)[:, height:], before)
            b = jnp.where(later, b, 0.0)
            if valid is not None:
                a = jnp.where(valid, a, 0.0)
                b = jnp.where(valid, b, 0.0)
            for dy in range(3):
                now = shifted(a, dy).reshape(size, both, channels)
                old = shifted(b, dy)
                active[2 + q, dy, where] = now.astype(jnp.bfloat16)
                active[q, dy, where] = jnp.concatenate([old, now[:, :height]], axis=1).astype(
                    jnp.bfloat16
                )

        step = min(8, width)

        @pl.loop(0, width // step)
        def _(i):
            x = i * step
            for q in range(2):
                put(
                    q,
                    pl.ds(x + 1, step),
                    step,
                    source[q, pl.ds(x, step)],
                    sibling[par, q, pl.ds(x, step)],
                    None,
                )

        for side, there in ((0, row > 0), (1, row < count - 1)):
            for q in range(2):
                put(
                    q,
                    pl.ds(0 if side == 0 else width + 1, 1),
                    1,
                    edges[par, side, span, q][None],
                    edges[par, side, 0, q][None],
                    there,
                )

    def convolution(weights, store):
        step = width
        partial = None
        for x in range(0, width, step):
            left, right = [], []
            for dy in range(3):
                for dx in range(3):
                    for k in (1, 2, 0, 3):
                        left.append(
                            active[k, dy, x + dx : x + dx + step].reshape(step * both, channels)
                        )
                        right.append(
                            jnp.concatenate(
                                [
                                    tap_block(weights, k - q, dy, dx, channels)
                                    for q in range(2)
                                ],
                                axis=1,
                            )
                        )
            result = jnp.dot(
                jnp.concatenate(left, axis=1),
                jnp.concatenate(right, axis=0),
                preferred_element_type=jnp.float32,
            )
            for q in range(2):
                tile = store(
                    q, x, step, result[:, q * channels : (q + 1) * channels].reshape(
                        step, both, channels
                    )
                )
                tile = tile.astype(jnp.float32).reshape(-1, height, channels)
                total, squares = jnp.sum(tile, axis=0), jnp.sum(tile * tile, axis=0)
                if partial is None:
                    partial = (total, squares)
                else:
                    partial = (partial[0] + total, partial[1] + squares)
        return partial

    def store_hidden(q, x, step, tile):
        tile = tile.astype(jnp.bfloat16)
        hidden[q, x : x + step] = tile
        return tile

    def store_values(q, x, step, tile):
        tile = (values[q, x : x + step].astype(jnp.float32) + tile).astype(jnp.bfloat16)
        values[q, x : x + step] = tile
        return tile

    def give(when):
        @pl.when((span == 1) & when)
        def _():
            pl.semaphore_signal(free_sem, inc=1, device_id=at(row, 0), device_id_type=MESH)

    def take(when):
        @pl.when((span == 0) & when)
        def _():
            pl.semaphore_wait(free_sem, 1)

    exchange(0, values, partial)
    for k in range(1, 4):
        param_copy(k, segment ^ k).wait_recv()

    @pl.loop(0, layers)
    def _(layer):
        moves_at("a", 0, layer)
        receive(0, values)
        give(layer > 0)
        activate(0, values, small[layer, 0:1], small[layer, 1:2])
        moves_at("b", 0, layer)
        partial = convolution(kernels.at[2 * layer], store_hidden)
        finish_sends(0, values)
        take(layer > 0)
        exchange(1, hidden, partial)
        moves_at("a", 1, layer)
        receive(1, hidden)
        give(layer < layers - 1)
        activate(1, hidden, small[layer, 2:3], small[layer, 3:4])
        moves_at("b", 1, layer)
        partial = convolution(kernels.at[2 * layer + 1], store_values)
        finish_sends(1, hidden)

        @pl.when(layer < layers - 1)
        def _():
            take(layer >= 0)
            exchange(0, values, partial)

    for q in range(2):
        whole = values[q].astype(jnp.float32)
        for p in range(2):
            turned[q + 2 * p] = whole[:, p * height : (p + 1) * height].reshape(
                height * width, channels
            )
    for f in range(frames):
        for y in range(height):
            staged[f, y] = turned[f, pl.ds(y, width, stride=height)].astype(jnp.bfloat16)

    def outgoing(k, me, to):
        return pltpu.make_async_remote_copy(
            src_ref=staged.at[:, pl.ds(to * local_rows, local_rows)],
            dst_ref=out.at[0, :, :, pl.ds(pl.multiple_of(me * width, width), width)],
            send_sem=out_send.at[k],
            recv_sem=out_recv.at[me],
            device_id=at(to, span),
            device_id_type=MESH,
        )

    for k in range(1, count):
        outgoing(k, row, lax.rem(row + k, count)).start()
    own = pltpu.make_async_copy(
        staged.at[:, pl.ds(row * local_rows, local_rows)],
        out.at[0, :, :, pl.ds(pl.multiple_of(row * width, width), width)],
        own_sem,
    )
    own.start()
    own.wait()
    moves("end")
    for k in range(1, 4):
        param_copy(k, segment).wait_send()
    for k in range(1, count):
        other = lax.rem(row + k, count)
        outgoing(k, other, row).wait_recv()
        outgoing(k, row, other).wait_send()


def body(latents, conv_first, conv_second, gain_first, bias_first, gain_second, bias_second):
    micro, frames, local_rows, columns, channels = latents.shape
    count = lax.axis_size("rows")
    width = columns // count
    height = local_rows * count
    both = 2 * height
    dma = pltpu.SemaphoreType.DMA
    return pl.pallas_call(
        functools.partial(decode_kernel, count),
        out_shape=jax.ShapeDtypeStruct((1, frames, local_rows, columns, channels), jnp.bfloat16),
        in_specs=[pl.BlockSpec(memory_space=pl.ANY)] * 3
        + [pl.BlockSpec(memory_space=pltpu.VMEM)] * 4,
        out_specs=pl.BlockSpec(memory_space=pltpu.VMEM),
        scratch_shapes=[
            pltpu.VMEM((frames, height, width, channels), jnp.bfloat16),
            pltpu.VMEM((frames, height * width, channels), jnp.float32),
            pltpu.VMEM((2, width, both, channels), jnp.bfloat16),
            pltpu.VMEM((2, width, both, channels), jnp.bfloat16),
            pltpu.VMEM((2, 2, width, both, channels), jnp.bfloat16),
            pltpu.VMEM((2, 2, 2, 2, both, channels), jnp.bfloat16),
            pltpu.VMEM((2, 2 * count, 8, channels), jnp.float32),
            pltpu.VMEM((4, 3, width + 2, both, channels), jnp.bfloat16),
            dma,
            dma((count,)),
            dma((count,)),
            dma((2, 2 * count)),
            dma((2, 2 * count)),
            dma((2, 2, 2)),
            dma((2, 2, 2)),
            dma((2,)),
            dma((2,)),
            dma((count,)),
            dma((count,)),
            pltpu.SemaphoreType.REGULAR,
            pltpu.VMEM((8,) + conv_first.shape[1:], jnp.bfloat16),
            pltpu.VMEM((4, 8, channels), jnp.float32),
            dma((4,)),
            dma((4,)),
            dma((8,)),
            dma((8, 2, 3)),
            dma((8, 3)),
            dma((8, 3)),
            dma((8, 3)),
        ],
        compiler_params=pltpu.CompilerParams(
            collective_id=0, has_side_effects=True, vmem_limit_bytes=48 * 2**20
        ),
    )(latents, conv_first, conv_second, gain_first, bias_first, gain_second, bias_second)


def solution(mesh):
    in_specs = (
        P(None, "tm", "rows", None, None),
        P("segment", None, None, None, None, None),
        P("segment", None, None, None, None, None),
        P("segment", None),
        P("segment", None),
        P("segment", None),
        P("segment", None),
    )
    out_specs = P("segment", "tm", "rows", None, None)
    sizes = dict(mesh.shape)

    def run(latents, *params):
        micro, frames, height, columns, channels = latents.shape
        count = sizes["rows"]
        fits = (
            micro == sizes["segment"] == 4
            and params[0].shape == (4, 3, 3, 3, channels, channels)
            and count < 8
            and sizes["tm"] == 2
            and frames == 8
            and height % (8 * 1) == 0
            and columns % (count * ROWS) == 0
            and channels == 4 * GROUPS
        )
        inner = body if fits else plain_body
        return jax.shard_map(
            inner, mesh=mesh, in_specs=in_specs, out_specs=out_specs, check_vma=False
        )(latents, *params)

    return run
```

```python
import functools

import jax
import jax.numpy as jnp
from jax import lax
from jax.experimental import pallas as pl
from jax.experimental.pallas import tpu as pltpu
from jax.sharding import PartitionSpec as P

GROUPS = 32


EPS = 1e-06


def passed_along(value, axis, steps):
    count = lax.axis_size(axis)
    initial, last = (max(0, -steps), min(count, count - steps))
    return lax.ppermute(value, axis, [(source, source + steps) for source in range(initial, last)])


def padded_2(block, sides, width):
    for axis, dim in sides:
        count = lax.axis_size(axis)
        forward = [(i, i + 1) for i in range(count - 1)]
        backward = [(target, source) for source, target in forward]
        low = lax.ppermute(
            lax.slice_in_dim(block, block.shape[dim] - width, None, axis=dim), axis, forward
        )
        high = lax.ppermute(lax.slice_in_dim(block, 0, width, axis=dim), axis, backward)
        block = jnp.concatenate([low, block, high], axis=dim)
    return block


def normalize(values, norm_gain, norm_bias):
    frames, rows_here, columns, channels = values.shape
    width_group = channels // GROUPS
    grouped = values.astype(jnp.float32).reshape(frames, rows_here, columns, GROUPS, width_group)
    totals = lax.psum(
        (jnp.sum(grouped, axis=(0, 1, 2, 4)), jnp.sum(grouped * grouped, axis=(0, 1, 2, 4))), "rows"
    )
    members = frames * rows_here * lax.axis_size("rows") * columns * width_group
    average = totals[0] / members
    squares = totals[1] / members
    inverse = lax.rsqrt(squares - average * average + EPS)
    scaled = (grouped - average[:, None]) * inverse[:, None]
    scaled = scaled.reshape(values.shape) * norm_gain.astype(jnp.float32) + norm_bias.astype(
        jnp.float32
    )
    return jax.nn.silu(scaled).astype(jnp.bfloat16)


def convolve(active, kernel):
    previous = passed_along(active[-2:], "tm", 1)
    extended = jnp.concatenate([previous, active], axis=0)
    padded = padded_2(extended, (("rows", 1),), 1)
    padded = jnp.pad(padded, ((0, 0), (0, 0), (1, 1), (0, 0)))
    result = lax.conv_general_dilated(
        padded[None],
        kernel,
        (1, 1, 1),
        "VALID",
        dimension_numbers=("NDHWC", "DHWIO", "NDHWC"),
        preferred_element_type=jnp.float32,
    )
    return result[0]


def residual_block(values, params):
    first, second, gain_one, bias_one, gain_two, bias_two = params
    active = normalize(values, gain_one, bias_one)
    hidden = convolve(active, first).astype(jnp.bfloat16)
    active = normalize(hidden, gain_two, bias_two)
    return (values.astype(jnp.float32) + convolve(active, second)).astype(jnp.bfloat16)


def plain_body(latents, conv_first, conv_second, gain_first, bias_first, gain_second, bias_second):
    segments = lax.axis_size("segment")
    micro = latents.shape[0]
    per_segment = micro // segments
    position = lax.axis_index("segment")
    small = jnp.stack([gain_first, bias_first, gain_second, bias_second], axis=1)
    small = lax.all_gather(small, "segment", axis=0, tiled=True)
    first = lax.all_gather(conv_first, "segment", axis=0, tiled=True)
    second = lax.all_gather(conv_second, "segment", axis=0, tiled=True)
    outs = []
    for index in range(per_segment):
        values = lax.dynamic_index_in_dim(
            latents, position * per_segment + index, 0, keepdims=False
        )
        for layer in range(first.shape[0]):
            gains = small[layer]
            values = residual_block(
                values, (first[layer], second[layer], gains[0], gains[1], gains[2], gains[3])
            )
        outs.append(values)
    return jnp.stack(outs)


MESH = pl.DeviceIdType.MESH
ROWS = 16


def group_sums(values):
    lanes = values.shape[-1]
    lane = lax.broadcasted_iota(jnp.int32, values.shape, 1)
    values = values + jnp.where(
        lax.rem(lane, 2) == 0, pltpu.roll(values, lanes - 1, 1), pltpu.roll(values, 1, 1)
    )
    return values + jnp.where(
        lax.rem(lane, 4) < 2, pltpu.roll(values, lanes - 2, 1), pltpu.roll(values, 2, 1)
    )


def tap_block(weights, dt, dy, dx, channels):
    if dt < 0 or dt > 2:
        return jnp.zeros((channels, channels), jnp.bfloat16)
    return weights[dt, dy, dx]


def decode_kernel(
    count,
    latents,
    first,
    second,
    gain_first,
    bias_first,
    gain_second,
    bias_second,
    out,
    staged,
    turned,
    values,
    hidden,
    sibling,
    edges,
    stats,
    active,
    own_sem,
    in_send,
    in_recv,
    stat_send,
    stat_recv,
    edge_send,
    edge_recv,
    sib_send,
    sib_recv,
    out_send,
    out_recv,
    free_sem,
    kernels,
    small,
    param_send,
    param_recv,
    load_sem,
    w_send,
    w_recv,
    half_send,
    half_recv,
    raw_params,
    raw_sem,
):
    frames, height, width, channels = staged.shape
    local_rows = height // count
    both = 2 * height
    row = lax.axis_index("rows")
    segment = lax.axis_index("segment")
    span = lax.axis_index("tm")
    members = frames * height * width * count * (channels // GROUPS)

    def at(rows_index, tm_index):
        return {"rows": rows_index, "tm": tm_index}

    barrier = pltpu.get_barrier_semaphore()
    for k in range(count):
        other = lax.rem(row + k, count)
        if k:
            pl.semaphore_signal(barrier, inc=1, device_id=at(other, span), device_id_type=MESH)
        pl.semaphore_signal(barrier, inc=1, device_id=at(other, 1 - span), device_id_type=MESH)
    for k in range(1, 4):
        pl.semaphore_signal(
            barrier, inc=1, device_id={"segment": segment ^ k}, device_id_type=MESH
        )
    pl.semaphore_wait(barrier, 2 * count + 2)

    given = (first, second)
    layers = kernels.shape[0] // 2
    depth = channels // 2

    def tensor_part(ref, half, chunk, chunks):
        rows = pl.ds(pl.multiple_of(half * depth, depth), depth)
        size = 3 // chunks
        return ref.at[pl.ds(chunk * size, size), :, :, rows]

    def chunks_of(j):
        return 3 if j < 2 else 1

    def remote_half(j, chunk, source, to, slot):
        return pltpu.make_async_remote_copy(
            src_ref=tensor_part(source, span, chunk, chunks_of(j)),
            dst_ref=tensor_part(kernels.at[j], span, chunk, chunks_of(j)),
            send_sem=w_send.at[j, slot, chunk],
            recv_sem=w_recv.at[j, chunk],
            device_id={"segment": to},
            device_id_type=MESH,
        )

    def core_half(j, chunk, half):
        return pltpu.make_async_remote_copy(
            src_ref=tensor_part(kernels.at[j], half, chunk, chunks_of(j)),
            dst_ref=tensor_part(kernels.at[j], half, chunk, chunks_of(j)),
            send_sem=half_send.at[j, chunk],
            recv_sem=half_recv.at[j, chunk],
            device_id={"tm": 1 - span},
            device_id_type=MESH,
        )

    def move(name):
        kind, j = name[0], int(name[1])
        away = segment ^ (j // 2)
        source = given[j % 2].at[0]
        first_to = segment ^ (1 + span)
        second_to = segment ^ (2 - span)
        passes = away == 1 + span
        each = range(chunks_of(j))
        if kind == "P":

            @pl.when(away == 0)
            def _():
                for c in each:
                    remote_half(j, c, source, first_to, 0).start()

        if kind == "S":

            @pl.when(away == 0)
            def _():
                for c in each:
                    if j == 0:
                        remote_half(j, c, source, first_to, 0).wait_send()
                    remote_half(j, c, source, second_to, 1).start()

        if kind == "F":

            @pl.when(passes)
            def _():
                for c in each:
                    remote_half(j, c, kernels.at[j], second_to, 0).wait_recv()
                    remote_half(j, c, kernels.at[j], second_to, 0).start()
                    core_half(j, c, span).start()

        if kind == "R":

            @pl.when((away > 0) & jnp.logical_not(passes))
            def _():
                for c in each:
                    remote_half(j, c, kernels.at[j], second_to, 0).wait_recv()
                    core_half(j, c, span).start()

        if kind == "G":

            @pl.when(away > 0)
            def _():
                for c in each:
                    core_half(j, c, 1 - span).wait_recv()

            @pl.when(away == 0)
            def _():
                pltpu.make_async_copy(source, kernels.at[j], load_sem.at[j]).wait()

        if kind == "W":

            @pl.when(away == 0)
            def _():
                for c in each:
                    if j > 0:
                        remote_half(j, c, source, first_to, 0).wait_send()
                    remote_half(j, c, source, second_to, 1).wait_send()

            @pl.when(passes)
            def _():
                for c in each:
                    remote_half(j, c, kernels.at[j], second_to, 0).wait_send()

            @pl.when(away > 0)
            def _():
                for c in each:
                    core_half(j, c, span).wait_send()

    plan = {
        "start": ("P0", "P2", "P4", "P6"),
        "early": ("F0", "S0"),
        "mid": ("P1",),
        "a0": ("R0", "S2", "S4", "S6"),
        "b0": ("S1", "G0"),
        "a1": ("F1",),
        "r1": ("F2",),
        "b1": ("P3", "P5", "R1", "G1"),
        "a2": ("F3", "S3", "S5", "F4"),
        "b2": ("P7", "R2", "G2"),
        "a3": ("F5", "F6"),
        "b3": ("S7", "R3", "R4", "G3"),
        "a4": ("F7",),
        "b4": ("R5", "R6", "G4"),
        "a5": ("R7",),
        "b5": ("G5",),
        "b6": ("G6",),
        "b7": ("G7",),
        "end": ("W0", "W1", "W2", "W3", "W4", "W5", "W6", "W7"),
    }

    def moves(point):
        for name in plan.get(point, ()):
            move(name)

    def moves_at(letter, which, layer):
        for known in range(layers):
            point = letter + str(2 * known + which)
            if point in plan:

                @pl.when(layer == known)
                def _(point=point):
                    moves(point)

    def incoming(k, me, to):
        return pltpu.make_async_remote_copy(
            src_ref=latents.at[segment, :, :, pl.ds(pl.multiple_of(to * width, width), width)],
            dst_ref=staged.at[:, pl.ds(me * local_rows, local_rows)],
            send_sem=in_send.at[k],
            recv_sem=in_recv.at[me],
            device_id=at(to, span),
            device_id_type=MESH,
        )

    moves("start")
    for k in range(1, count):
        incoming(k, row, lax.rem(row + k, count)).start()
    for j in range(2 * layers):

        @pl.when(segment == j // 2)
        def _(j=j):
            pltpu.make_async_copy(given[j % 2].at[0], kernels.at[j], load_sem.at[j]).start()

    index = lax.broadcasted_iota(jnp.int32, (8, channels), 0)
    raw = [
        pltpu.make_async_copy(ref, raw_params.at[k], raw_sem.at[k])
        for k, ref in enumerate((gain_first, bias_first, gain_second, bias_second))
    ]
    for copy in raw:
        copy.start()
    for copy in raw:
        copy.wait()
    packed = jnp.zeros((8, channels), jnp.float32)
    for k in range(4):
        packed = jnp.where(index == k, raw_params[k].astype(jnp.float32), packed)
    small[segment] = packed

    def param_copy(k, me):
        return pltpu.make_async_remote_copy(
            src_ref=small.at[me],
            dst_ref=small.at[me],
            send_sem=param_send.at[k],
            recv_sem=param_recv.at[me],
            device_id={"segment": segment ^ k},
            device_id_type=MESH,
        )

    for k in range(1, 4):
        param_copy(k, segment).start()
    own = pltpu.make_async_copy(
        latents.at[segment, :, :, pl.ds(pl.multiple_of(row * width, width), width)],
        staged.at[:, pl.ds(row * local_rows, local_rows)],
        own_sem,
    )
    own.start()
    moves("early")
    own.wait()
    for k in range(1, count):
        other = lax.rem(row + k, count)
        incoming(k, other, row).wait_recv()
    moves("mid")

    for f in range(frames):
        turned[f] = staged[f].astype(jnp.float32).reshape(height * width, channels)
    zero = jnp.zeros((height, channels), jnp.float32)

    def turn(x, carry):
        total, squares = carry
        for q in range(2):
            tile = jnp.concatenate(
                [turned[q + 2 * p, pl.ds(x, height, stride=width)] for p in range(2)], axis=0
            )
            values[q, x] = tile.astype(jnp.bfloat16)
            total = total + tile[:height] + tile[height:]
            tile = tile * tile
            squares = squares + tile[:height] + tile[height:]
        return total, squares

    partial = lax.fori_loop(0, width, turn, (zero, zero), unroll=4)
    for k in range(1, count):
        incoming(k, row, lax.rem(row + k, count)).wait_send()

    def stat_copy(par, k, me, to, tm_from, tm_to):
        slot = tm_from * count + me
        cross = 0 if tm_from is tm_to else count
        return pltpu.make_async_remote_copy(
            src_ref=stats.at[par, slot],
            dst_ref=stats.at[par, slot],
            send_sem=stat_send.at[par, k + cross],
            recv_sem=stat_recv.at[par, slot],
            device_id=at(to, tm_to),
            device_id_type=MESH,
        )

    def edge_copy(par, source, side, tm_from, tm_to, to):
        return pltpu.make_async_remote_copy(
            src_ref=source.at[:, width - 1 if side == 0 else 0],
            dst_ref=edges.at[par, side, tm_from],
            send_sem=edge_send.at[par, side, tm_to],
            recv_sem=edge_recv.at[par, side, tm_from],
            device_id=at(to, tm_to),
            device_id_type=MESH,
        )

    def sib_copy(par, source):
        return pltpu.make_async_remote_copy(
            src_ref=source,
            dst_ref=sibling.at[par],
            send_sem=sib_send.at[par],
            recv_sem=sib_recv.at[par],
            device_id=at(row, 1),
            device_id_type=MESH,
        )

    def each_send(par, source, act):
        for k in range(1, count):
            act(stat_copy(par, k, row, lax.rem(row + k, count), span, span))

        @pl.when(span == 0)
        def _():
            for k in range(count):
                act(stat_copy(par, k, row, lax.rem(row + k, count), 0, 1))

        for side, there in ((0, row < count - 1), (1, row > 0)):

            @pl.when(there)
            def _(side=side):
                to = row + 1 if side == 0 else row - 1
                act(edge_copy(par, source, side, span, span, to))

                @pl.when(span == 0)
                def _():
                    act(edge_copy(par, source, side, 0, 1, to))

        @pl.when(span == 0)
        def _():
            act(sib_copy(par, source))

    def exchange(par, source, partial):
        index = lax.broadcasted_iota(jnp.int32, (8, channels), 0)
        total = jnp.sum(partial[0], axis=0, keepdims=True)
        squares = jnp.sum(partial[1], axis=0, keepdims=True)
        stats[par, span * count + row] = jnp.where(
            index == 0, total, jnp.where(index == 1, squares, 0.0)
        )
        each_send(par, source, lambda copy: copy.start())

    def finish_sends(par, source):
        each_send(par, source, lambda copy: copy.wait_send())

    def receive(par, source):
        for side, there in ((0, row > 0), (1, row < count - 1)):

            @pl.when(there)
            def _(side=side):
                edge_copy(par, source, side, span, span, row).wait_recv()

                @pl.when(span == 1)
                def _():
                    edge_copy(par, source, side, 0, 1, row).wait_recv()

        @pl.when(span == 1)
        def _():
            sib_copy(par, source).wait_recv()
            for k in range(count):
                stat_copy(par, k, lax.rem(row + k, count), row, 0, 1).wait_recv()

        for k in range(1, count):
            stat_copy(par, k, lax.rem(row + k, count), row, span, span).wait_recv()

    def moments(par, base, gain):
        total = stats[par, base]
        for k in range(1, count):
            total = total + stats[par, base + k]
        total = group_sums(total) / members
        average = total[0:1]
        return average, lax.rsqrt(total[1:2] - average * average + EPS) * gain

    def activate(par, source, gain, bias):
        mine = moments(par, span * count, gain)
        before = moments(par, 0, gain)
        later = span > 0
        index = lax.broadcasted_iota(jnp.int32, (1, height, channels), 1)

        def silu(tile, moment):
            half = ((tile - moment[0]) * moment[1] + bias) * 0.5
            return half + half * jnp.tanh(half)

        def shifted(a, dy):
            if dy == 0:
                return jnp.where(index == 0, 0.0, pltpu.roll(a, 1, 1))
            if dy == 2:
                return jnp.where(index == height - 1, 0.0, pltpu.roll(a, height - 1, 1))
            return a

        def put(q, where, size, tile, older, valid):
            a = silu(tile.astype(jnp.float32), mine).reshape(2 * size, height, channels)
            b = silu(older.astype(jnp.float32)[:, height:], before)
            b = jnp.where(later, b, 0.0)
            if valid is not None:
                a = jnp.where(valid, a, 0.0)
                b = jnp.where(valid, b, 0.0)
            for dy in range(3):
                now = shifted(a, dy).reshape(size, both, channels)
                old = shifted(b, dy)
                active[2 + q, dy, where] = now.astype(jnp.bfloat16)
                active[q, dy, where] = jnp.concatenate([old, now[:, :height]], axis=1).astype(
                    jnp.bfloat16
                )

        step = min(8, width)

        @pl.loop(0, width // step)
        def _(i):
            x = i * step
            for q in range(2):
                put(
                    q,
                    pl.ds(x + 1, step),
                    step,
                    source[q, pl.ds(x, step)],
                    sibling[par, q, pl.ds(x, step)],
                    None,
                )

        for side, there in ((0, row > 0), (1, row < count - 1)):
            for q in range(2):
                put(
                    q,
                    pl.ds(0 if side == 0 else width + 1, 1),
                    1,
                    edges[par, side, span, q][None],
                    edges[par, side, 0, q][None],
                    there,
                )

    def convolution(weights, store):
        step = width // 2
        partial = None
        for x in range(0, width, step):
            left, right = [], []
            for dy in range(3):
                for dx in range(3):
                    for k in (1, 2, 0, 3):
                        left.append(
                            active[k, dy, x + dx : x + dx + step].reshape(step * both, channels)
                        )
                        right.append(
                            jnp.concatenate(
                                [
                                    tap_block(weights, k - q, dy, dx, channels)
                                    for q in range(2)
                                ],
                                axis=1,
                            )
                        )
            result = jnp.dot(
                jnp.concatenate(left, axis=1),
                jnp.concatenate(right, axis=0),
                preferred_element_type=jnp.float32,
            )
            for q in range(2):
                tile = store(
                    q, x, step, result[:, q * channels : (q + 1) * channels].reshape(
                        step, both, channels
                    )
                )
                tile = tile.astype(jnp.float32).reshape(-1, height, channels)
                total, squares = jnp.sum(tile, axis=0), jnp.sum(tile * tile, axis=0)
                if partial is None:
                    partial = (total, squares)
                else:
                    partial = (partial[0] + total, partial[1] + squares)
        return partial

    def store_hidden(q, x, step, tile):
        tile = tile.astype(jnp.bfloat16)
        hidden[q, x : x + step] = tile
        return tile

    def store_values(q, x, step, tile):
        tile = (values[q, x : x + step].astype(jnp.float32) + tile).astype(jnp.bfloat16)
        values[q, x : x + step] = tile
        return tile

    def give(when):
        @pl.when((span == 1) & when)
        def _():
            pl.semaphore_signal(free_sem, inc=1, device_id=at(row, 0), device_id_type=MESH)

    def take(when):
        @pl.when((span == 0) & when)
        def _():
            pl.semaphore_wait(free_sem, 1)

    exchange(0, values, partial)
    for k in range(1, 4):
        param_copy(k, segment ^ k).wait_recv()

    @pl.loop(0, layers)
    def _(layer):
        moves_at("a", 0, layer)
        receive(0, values)
        moves_at("r", 0, layer)
        give(layer > 0)
        activate(0, values, small[layer, 0:1], small[layer, 1:2])
        moves_at("b", 0, layer)
        partial = convolution(kernels.at[2 * layer], store_hidden)
        finish_sends(0, values)
        take(layer > 0)
        exchange(1, hidden, partial)
        moves_at("a", 1, layer)
        receive(1, hidden)
        moves_at("r", 1, layer)
        give(layer < layers - 1)
        activate(1, hidden, small[layer, 2:3], small[layer, 3:4])
        moves_at("b", 1, layer)
        partial = convolution(kernels.at[2 * layer + 1], store_values)
        finish_sends(1, hidden)

        @pl.when(layer < layers - 1)
        def _():
            take(layer >= 0)
            exchange(0, values, partial)

    for q in range(2):
        whole = values[q].astype(jnp.float32)
        for p in range(2):
            turned[q + 2 * p] = whole[:, p * height : (p + 1) * height].reshape(
                height * width, channels
            )
    for f in range(frames):
        for y in range(height):
            staged[f, y] = turned[f, pl.ds(y, width, stride=height)].astype(jnp.bfloat16)

    def outgoing(k, me, to):
        return pltpu.make_async_remote_copy(
            src_ref=staged.at[:, pl.ds(to * local_rows, local_rows)],
            dst_ref=out.at[0, :, :, pl.ds(pl.multiple_of(me * width, width), width)],
            send_sem=out_send.at[k],
            recv_sem=out_recv.at[me],
            device_id=at(to, span),
            device_id_type=MESH,
        )

    for k in range(1, count):
        outgoing(k, row, lax.rem(row + k, count)).start()
    own = pltpu.make_async_copy(
        staged.at[:, pl.ds(row * local_rows, local_rows)],
        out.at[0, :, :, pl.ds(pl.multiple_of(row * width, width), width)],
        own_sem,
    )
    own.start()
    own.wait()
    moves("end")
    for k in range(1, 4):
        param_copy(k, segment).wait_send()
    for k in range(1, count):
        other = lax.rem(row + k, count)
        outgoing(k, other, row).wait_recv()
        outgoing(k, row, other).wait_send()


def body(latents, conv_first, conv_second, gain_first, bias_first, gain_second, bias_second):
    micro, frames, local_rows, columns, channels = latents.shape
    count = lax.axis_size("rows")
    width = columns // count
    height = local_rows * count
    both = 2 * height
    dma = pltpu.SemaphoreType.DMA
    return pl.pallas_call(
        functools.partial(decode_kernel, count),
        out_shape=jax.ShapeDtypeStruct((1, frames, local_rows, columns, channels), jnp.bfloat16),
        in_specs=[pl.BlockSpec(memory_space=pltpu.HBM)] * 7,
        out_specs=pl.BlockSpec(memory_space=pltpu.VMEM),
        scratch_shapes=[
            pltpu.VMEM((frames, height, width, channels), jnp.bfloat16),
            pltpu.VMEM((frames, height * width, channels), jnp.float32),
            pltpu.VMEM((2, width, both, channels), jnp.bfloat16),
            pltpu.VMEM((2, width, both, channels), jnp.bfloat16),
            pltpu.VMEM((2, 2, width, both, channels), jnp.bfloat16),
            pltpu.VMEM((2, 2, 2, 2, both, channels), jnp.bfloat16),
            pltpu.VMEM((2, 2 * count, 8, channels), jnp.float32),
            pltpu.VMEM((4, 3, width + 2, both, channels), jnp.bfloat16),
            dma,
            dma((count,)),
            dma((count,)),
            dma((2, 2 * count)),
            dma((2, 2 * count)),
            dma((2, 2, 2)),
            dma((2, 2, 2)),
            dma((2,)),
            dma((2,)),
            dma((count,)),
            dma((count,)),
            pltpu.SemaphoreType.REGULAR,
            pltpu.VMEM((8,) + conv_first.shape[1:], jnp.bfloat16),
            pltpu.VMEM((4, 8, channels), jnp.float32),
            dma((4,)),
            dma((4,)),
            dma((8,)),
            dma((8, 2, 3)),
            dma((8, 3)),
            dma((8, 3)),
            dma((8, 3)),
            pltpu.VMEM((4, 1, channels), jnp.bfloat16),
            dma((4,)),
        ],
        compiler_params=pltpu.CompilerParams(
            collective_id=0, has_side_effects=True, vmem_limit_bytes=64 * 2**20 - 2**17
        ),
    )(latents, conv_first, conv_second, gain_first, bias_first, gain_second, bias_second)


def solution(mesh):
    in_specs = (
        P(None, "tm", "rows", None, None),
        P("segment", None, None, None, None, None),
        P("segment", None, None, None, None, None),
        P("segment", None),
        P("segment", None),
        P("segment", None),
        P("segment", None),
    )
    out_specs = P("segment", "tm", "rows", None, None)
    sizes = dict(mesh.shape)

    def run(latents, *params):
        micro, frames, height, columns, channels = latents.shape
        count = sizes["rows"]
        fits = (
            micro == sizes["segment"] == 4
            and params[0].shape == (4, 3, 3, 3, channels, channels)
            and count < 8
            and sizes["tm"] == 2
            and frames == 8
            and height % (8 * 1) == 0
            and columns % (count * ROWS) == 0
            and channels == 4 * GROUPS
        )
        inner = body if fits else plain_body
        return jax.shard_map(
            inner, mesh=mesh, in_specs=in_specs, out_specs=out_specs, check_vma=False
        )(latents, *params)

    return run
```

```python
import functools

import jax
import jax.numpy as jnp
from jax import lax
from jax.experimental import pallas as pl
from jax.experimental.pallas import tpu as pltpu
from jax.sharding import PartitionSpec as P

GROUPS = 32


EPS = 1e-06


def passed_along(value, axis, steps):
    count = lax.axis_size(axis)
    initial, last = (max(0, -steps), min(count, count - steps))
    return lax.ppermute(value, axis, [(source, source + steps) for source in range(initial, last)])


def padded_2(block, sides, width):
    for axis, dim in sides:
        count = lax.axis_size(axis)
        forward = [(i, i + 1) for i in range(count - 1)]
        backward = [(target, source) for source, target in forward]
        low = lax.ppermute(
            lax.slice_in_dim(block, block.shape[dim] - width, None, axis=dim), axis, forward
        )
        high = lax.ppermute(lax.slice_in_dim(block, 0, width, axis=dim), axis, backward)
        block = jnp.concatenate([low, block, high], axis=dim)
    return block


def normalize(values, norm_gain, norm_bias):
    frames, rows_here, columns, channels = values.shape
    width_group = channels // GROUPS
    grouped = values.astype(jnp.float32).reshape(frames, rows_here, columns, GROUPS, width_group)
    totals = lax.psum(
        (jnp.sum(grouped, axis=(0, 1, 2, 4)), jnp.sum(grouped * grouped, axis=(0, 1, 2, 4))), "rows"
    )
    members = frames * rows_here * lax.axis_size("rows") * columns * width_group
    average = totals[0] / members
    squares = totals[1] / members
    inverse = lax.rsqrt(squares - average * average + EPS)
    scaled = (grouped - average[:, None]) * inverse[:, None]
    scaled = scaled.reshape(values.shape) * norm_gain.astype(jnp.float32) + norm_bias.astype(
        jnp.float32
    )
    return jax.nn.silu(scaled).astype(jnp.bfloat16)


def convolve(active, kernel):
    previous = passed_along(active[-2:], "tm", 1)
    extended = jnp.concatenate([previous, active], axis=0)
    padded = padded_2(extended, (("rows", 1),), 1)
    padded = jnp.pad(padded, ((0, 0), (0, 0), (1, 1), (0, 0)))
    result = lax.conv_general_dilated(
        padded[None],
        kernel,
        (1, 1, 1),
        "VALID",
        dimension_numbers=("NDHWC", "DHWIO", "NDHWC"),
        preferred_element_type=jnp.float32,
    )
    return result[0]


def residual_block(values, params):
    first, second, gain_one, bias_one, gain_two, bias_two = params
    active = normalize(values, gain_one, bias_one)
    hidden = convolve(active, first).astype(jnp.bfloat16)
    active = normalize(hidden, gain_two, bias_two)
    return (values.astype(jnp.float32) + convolve(active, second)).astype(jnp.bfloat16)


def plain_body(latents, conv_first, conv_second, gain_first, bias_first, gain_second, bias_second):
    segments = lax.axis_size("segment")
    micro = latents.shape[0]
    per_segment = micro // segments
    position = lax.axis_index("segment")
    small = jnp.stack([gain_first, bias_first, gain_second, bias_second], axis=1)
    small = lax.all_gather(small, "segment", axis=0, tiled=True)
    first = lax.all_gather(conv_first, "segment", axis=0, tiled=True)
    second = lax.all_gather(conv_second, "segment", axis=0, tiled=True)
    outs = []
    for index in range(per_segment):
        values = lax.dynamic_index_in_dim(
            latents, position * per_segment + index, 0, keepdims=False
        )
        for layer in range(first.shape[0]):
            gains = small[layer]
            values = residual_block(
                values, (first[layer], second[layer], gains[0], gains[1], gains[2], gains[3])
            )
        outs.append(values)
    return jnp.stack(outs)


MESH = pl.DeviceIdType.MESH
ROWS = 16


def group_sums(values):
    lanes = values.shape[-1]
    lane = lax.broadcasted_iota(jnp.int32, values.shape, 1)
    values = values + jnp.where(
        lax.rem(lane, 2) == 0, pltpu.roll(values, lanes - 1, 1), pltpu.roll(values, 1, 1)
    )
    return values + jnp.where(
        lax.rem(lane, 4) < 2, pltpu.roll(values, lanes - 2, 1), pltpu.roll(values, 2, 1)
    )


def tap_block(weights, dt, dy, dx, channels):
    if dt < 0 or dt > 2:
        return jnp.zeros((channels, channels), jnp.bfloat16)
    return weights[dt, dy, dx]


def decode_kernel(
    count,
    latents,
    first,
    second,
    gain_first,
    bias_first,
    gain_second,
    bias_second,
    out,
    staged,
    turned,
    values,
    hidden,
    sibling,
    edges,
    stats,
    active,
    own_sem,
    in_send,
    in_recv,
    stat_send,
    stat_recv,
    edge_send,
    edge_recv,
    sib_send,
    sib_recv,
    out_send,
    out_recv,
    free_sem,
    kernels,
    small,
    param_send,
    param_recv,
    load_sem,
    w_send,
    w_recv,
    half_send,
    half_recv,
    raw_params,
    raw_sem,
):
    frames, height, width, channels = staged.shape
    local_rows = height // count
    both = 2 * height
    row = lax.axis_index("rows")
    segment = lax.axis_index("segment")
    span = lax.axis_index("tm")
    members = frames * height * width * count * (channels // GROUPS)

    def at(rows_index, tm_index):
        return {"rows": rows_index, "tm": tm_index}

    barrier = pltpu.get_barrier_semaphore()
    for k in range(count):
        other = lax.rem(row + k, count)
        if k:
            pl.semaphore_signal(barrier, inc=1, device_id=at(other, span), device_id_type=MESH)
        pl.semaphore_signal(barrier, inc=1, device_id=at(other, 1 - span), device_id_type=MESH)
    for k in range(1, 4):
        pl.semaphore_signal(
            barrier, inc=1, device_id={"segment": segment ^ k}, device_id_type=MESH
        )
    pl.semaphore_wait(barrier, 2 * count + 2)

    given = (first, second)
    layers = kernels.shape[0] // 2
    depth = channels // 2

    def tensor_part(ref, half, chunk, chunks):
        rows = pl.ds(pl.multiple_of(half * depth, depth), depth)
        size = 3 // chunks
        return ref.at[pl.ds(chunk * size, size), :, :, rows]

    def chunks_of(j):
        return 3 if j < 2 else 1

    def remote_half(j, chunk, source, to, slot):
        return pltpu.make_async_remote_copy(
            src_ref=tensor_part(source, span, chunk, chunks_of(j)),
            dst_ref=tensor_part(kernels.at[j], span, chunk, chunks_of(j)),
            send_sem=w_send.at[j, slot, chunk],
            recv_sem=w_recv.at[j, chunk],
            device_id={"rows": row ^ 1} if to is None else {"segment": to},
            device_id_type=MESH,
        )

    def core_half(j, chunk, half):
        return pltpu.make_async_remote_copy(
            src_ref=tensor_part(kernels.at[j], half, chunk, chunks_of(j)),
            dst_ref=tensor_part(kernels.at[j], half, chunk, chunks_of(j)),
            send_sem=half_send.at[j, chunk],
            recv_sem=half_recv.at[j, chunk],
            device_id={"tm": 1 - span},
            device_id_type=MESH,
        )

    routes = "ZZVXVVVV"

    def move(name):
        kind, j = name[0], int(name[1])
        route = routes[j]
        away = segment ^ (j // 2)
        source = given[j % 2].at[0]
        each = range(chunks_of(j))
        if route == "X":
            first_to = segment ^ 1
            second_to = pass_to = segment ^ 2
            passes = away == 1
        else:
            turn = lax.rem(row + span, 2) if route == "Z" else span
            first_to = segment ^ (1 + turn)
            second_to = pass_to = segment ^ (2 - turn)
            passes = away == 1 + turn
        here = kernels.at[j]
        if kind == "P":

            @pl.when(away == 0)
            def _():
                for c in each:
                    remote_half(j, c, source, first_to, 0).start()

        if kind == "Q":

            @pl.when(away == 0)
            def _():
                for c in each:
                    remote_half(j - 1, c, given[(j - 1) % 2].at[0], first_to, 0).wait_send()
                    remote_half(j, c, source, first_to, 0).start()

        if kind == "S":

            @pl.when(away == 0)
            def _():
                for c in each:
                    remote_half(j, c, source, second_to, 1).start()

        if kind == "F":

            @pl.when(passes)
            def _():
                for c in each:
                    remote_half(j, c, here, pass_to, 0).wait_recv()
                    remote_half(j, c, here, pass_to, 0).start()
                    if route == "Z":
                        remote_half(j, c, here, None, 1).start()
                    core_half(j, c, span).start()

        if kind == "R":

            @pl.when((away > 0) & jnp.logical_not(passes))
            def _():
                for c in each:
                    remote_half(j, c, here, pass_to, 0).wait_recv()
                    core_half(j, c, span).start()

        if kind == "G":

            @pl.when(away > 0)
            def _():
                for c in each:
                    core_half(j, c, 1 - span).wait_recv()

            @pl.when(away == 0)
            def _():
                pltpu.make_async_copy(source, kernels.at[j], load_sem.at[j]).wait()

        if kind == "W":

            @pl.when(away == 0)
            def _():
                for c in each:
                    if j > 0:
                        remote_half(j, c, source, first_to, 0).wait_send()
                    if route != "Z":
                        remote_half(j, c, source, second_to, 1).wait_send()

            @pl.when(passes)
            def _():
                for c in each:
                    remote_half(j, c, here, pass_to, 0).wait_send()
                    if route == "Z":
                        remote_half(j, c, here, None, 1).wait_send()

            @pl.when(away > 0)
            def _():
                for c in each:
                    core_half(j, c, span).wait_send()

    plan = {
        "start": ("P0", "P2", "P4", "P6"),
        "early": ("Q1", "F0"),
        "a0": ("P3", "F1", "R0"),
        "r0": ("F2", "S2", "S4"),
        "b0": ("G0",),
        "a1": ("S3", "S6", "F4", "R1"),
        "b1": ("G1",),
        "a2": ("F3", "P5", "R2", "F6"),
        "b2": ("G2",),
        "a3": ("S5", "P7", "R4", "R3"),
        "r3": ("F5",),
        "b3": ("G3",),
        "a4": ("S7", "R6"),
        "b4": ("G4",),
        "a5": ("F7", "R5"),
        "b5": ("G5",),
        "r6": ("R7",),
        "b6": ("G6",),
        "b7": ("G7",),
        "end": ("W0", "W1", "W2", "W3", "W4", "W5", "W6", "W7"),
    }

    def moves(point):
        for name in plan.get(point, ()):
            move(name)

    def moves_at(letter, which, layer):
        for known in range(layers):
            point = letter + str(2 * known + which)
            if point in plan:

                @pl.when(layer == known)
                def _(point=point):
                    moves(point)

    def incoming(k, me, to):
        return pltpu.make_async_remote_copy(
            src_ref=latents.at[segment, :, :, pl.ds(pl.multiple_of(to * width, width), width)],
            dst_ref=staged.at[:, pl.ds(me * local_rows, local_rows)],
            send_sem=in_send.at[k],
            recv_sem=in_recv.at[me],
            device_id=at(to, span),
            device_id_type=MESH,
        )

    moves("start")
    for k in range(1, count):
        incoming(k, row, lax.rem(row + k, count)).start()
    for j in range(2 * layers):

        @pl.when(segment == j // 2)
        def _(j=j):
            pltpu.make_async_copy(given[j % 2].at[0], kernels.at[j], load_sem.at[j]).start()

    index = lax.broadcasted_iota(jnp.int32, (8, channels), 0)
    raw = [
        pltpu.make_async_copy(ref, raw_params.at[k], raw_sem.at[k])
        for k, ref in enumerate((gain_first, bias_first, gain_second, bias_second))
    ]
    for copy in raw:
        copy.start()
    for copy in raw:
        copy.wait()
    packed = jnp.zeros((8, channels), jnp.float32)
    for k in range(4):
        packed = jnp.where(index == k, raw_params[k].astype(jnp.float32), packed)
    small[segment] = packed

    def param_copy(k, me):
        return pltpu.make_async_remote_copy(
            src_ref=small.at[me],
            dst_ref=small.at[me],
            send_sem=param_send.at[k],
            recv_sem=param_recv.at[me],
            device_id={"segment": segment ^ k},
            device_id_type=MESH,
        )

    for k in range(1, 4):
        param_copy(k, segment).start()
    own = pltpu.make_async_copy(
        latents.at[segment, :, :, pl.ds(pl.multiple_of(row * width, width), width)],
        staged.at[:, pl.ds(row * local_rows, local_rows)],
        own_sem,
    )
    own.start()
    moves("early")
    own.wait()
    for k in range(1, count):
        other = lax.rem(row + k, count)
        incoming(k, other, row).wait_recv()

    for f in range(frames):
        turned[f] = staged[f].astype(jnp.float32).reshape(height * width, channels)
    zero = jnp.zeros((height, channels), jnp.float32)

    def turn(x, carry):
        total, squares = carry
        for q in range(2):
            tile = jnp.concatenate(
                [turned[q + 2 * p, pl.ds(x, height, stride=width)] for p in range(2)], axis=0
            )
            values[q, x] = tile.astype(jnp.bfloat16)
            total = total + tile[:height] + tile[height:]
            tile = tile * tile
            squares = squares + tile[:height] + tile[height:]
        return total, squares

    partial = lax.fori_loop(0, width, turn, (zero, zero), unroll=4)
    for k in range(1, count):
        incoming(k, row, lax.rem(row + k, count)).wait_send()

    def stat_copy(par, k, me, to, tm_from, tm_to):
        slot = tm_from * count + me
        cross = 0 if tm_from is tm_to else count
        return pltpu.make_async_remote_copy(
            src_ref=stats.at[par, slot],
            dst_ref=stats.at[par, slot],
            send_sem=stat_send.at[par, k + cross],
            recv_sem=stat_recv.at[par, slot],
            device_id=at(to, tm_to),
            device_id_type=MESH,
        )

    def edge_copy(par, source, side, tm_from, tm_to, to):
        return pltpu.make_async_remote_copy(
            src_ref=source.at[:, width - 1 if side == 0 else 0],
            dst_ref=edges.at[par, side, tm_from],
            send_sem=edge_send.at[par, side, tm_to],
            recv_sem=edge_recv.at[par, side, tm_from],
            device_id=at(to, tm_to),
            device_id_type=MESH,
        )

    def sib_copy(par, source):
        return pltpu.make_async_remote_copy(
            src_ref=source,
            dst_ref=sibling.at[par],
            send_sem=sib_send.at[par],
            recv_sem=sib_recv.at[par],
            device_id=at(row, 1),
            device_id_type=MESH,
        )

    def each_send(par, source, act):
        for k in range(1, count):
            act(stat_copy(par, k, row, lax.rem(row + k, count), span, span))

        @pl.when(span == 0)
        def _():
            for k in range(count):
                act(stat_copy(par, k, row, lax.rem(row + k, count), 0, 1))

        for side, there in ((0, row < count - 1), (1, row > 0)):

            @pl.when(there)
            def _(side=side):
                to = row + 1 if side == 0 else row - 1
                act(edge_copy(par, source, side, span, span, to))

                @pl.when(span == 0)
                def _():
                    act(edge_copy(par, source, side, 0, 1, to))

        @pl.when(span == 0)
        def _():
            act(sib_copy(par, source))

    def exchange(par, source, partial):
        index = lax.broadcasted_iota(jnp.int32, (8, channels), 0)
        total = jnp.sum(partial[0], axis=0, keepdims=True)
        squares = jnp.sum(partial[1], axis=0, keepdims=True)
        stats[par, span * count + row] = jnp.where(
            index == 0, total, jnp.where(index == 1, squares, 0.0)
        )
        each_send(par, source, lambda copy: copy.start())

    def finish_sends(par, source):
        each_send(par, source, lambda copy: copy.wait_send())

    def receive(par, source):
        for side, there in ((0, row > 0), (1, row < count - 1)):

            @pl.when(there)
            def _(side=side):
                edge_copy(par, source, side, span, span, row).wait_recv()

                @pl.when(span == 1)
                def _():
                    edge_copy(par, source, side, 0, 1, row).wait_recv()

        @pl.when(span == 1)
        def _():
            sib_copy(par, source).wait_recv()
            for k in range(count):
                stat_copy(par, k, lax.rem(row + k, count), row, 0, 1).wait_recv()

        for k in range(1, count):
            stat_copy(par, k, lax.rem(row + k, count), row, span, span).wait_recv()

    def moments(par, base, gain):
        total = stats[par, base]
        for k in range(1, count):
            total = total + stats[par, base + k]
        total = group_sums(total) / members
        average = total[0:1]
        return average, lax.rsqrt(total[1:2] - average * average + EPS) * gain

    def activate(par, source, gain, bias):
        mine = moments(par, span * count, gain)
        before = moments(par, 0, gain)
        later = span > 0
        index = lax.broadcasted_iota(jnp.int32, (1, height, channels), 1)

        def silu(tile, moment):
            half = ((tile - moment[0]) * moment[1] + bias) * 0.5
            return half + half * jnp.tanh(half)

        def shifted(a, dy):
            if dy == 0:
                return jnp.where(index == 0, 0.0, pltpu.roll(a, 1, 1))
            if dy == 2:
                return jnp.where(index == height - 1, 0.0, pltpu.roll(a, height - 1, 1))
            return a

        def put(q, where, size, tile, older, valid):
            a = silu(tile.astype(jnp.float32), mine).reshape(2 * size, height, channels)
            b = silu(older.astype(jnp.float32)[:, height:], before)
            b = jnp.where(later, b, 0.0)
            if valid is not None:
                a = jnp.where(valid, a, 0.0)
                b = jnp.where(valid, b, 0.0)
            for dy in range(3):
                now = shifted(a, dy).reshape(size, both, channels)
                old = shifted(b, dy)
                active[2 + q, dy, where] = now.astype(jnp.bfloat16)
                active[q, dy, where] = jnp.concatenate([old, now[:, :height]], axis=1).astype(
                    jnp.bfloat16
                )

        step = min(8, width)

        @pl.loop(0, width // step)
        def _(i):
            x = i * step
            for q in range(2):
                put(
                    q,
                    pl.ds(x + 1, step),
                    step,
                    source[q, pl.ds(x, step)],
                    sibling[par, q, pl.ds(x, step)],
                    None,
                )

        for side, there in ((0, row > 0), (1, row < count - 1)):
            for q in range(2):
                put(
                    q,
                    pl.ds(0 if side == 0 else width + 1, 1),
                    1,
                    edges[par, side, span, q][None],
                    edges[par, side, 0, q][None],
                    there,
                )

    def convolution(weights, store):
        step = width // 2
        partial = None
        for x in range(0, width, step):
            left, right = [], []
            for dy in range(3):
                for dx in range(3):
                    for k in (1, 2, 0, 3):
                        left.append(
                            active[k, dy, x + dx : x + dx + step].reshape(step * both, channels)
                        )
                        right.append(
                            jnp.concatenate(
                                [
                                    tap_block(weights, k - q, dy, dx, channels)
                                    for q in range(2)
                                ],
                                axis=1,
                            )
                        )
            result = jnp.dot(
                jnp.concatenate(left, axis=1),
                jnp.concatenate(right, axis=0),
                preferred_element_type=jnp.float32,
            )
            for q in range(2):
                tile = store(
                    q, x, step, result[:, q * channels : (q + 1) * channels].reshape(
                        step, both, channels
                    )
                )
                tile = tile.astype(jnp.float32).reshape(-1, height, channels)
                total, squares = jnp.sum(tile, axis=0), jnp.sum(tile * tile, axis=0)
                if partial is None:
                    partial = (total, squares)
                else:
                    partial = (partial[0] + total, partial[1] + squares)
        return partial

    def store_hidden(q, x, step, tile):
        tile = tile.astype(jnp.bfloat16)
        hidden[q, x : x + step] = tile
        return tile

    def store_values(q, x, step, tile):
        tile = (values[q, x : x + step].astype(jnp.float32) + tile).astype(jnp.bfloat16)
        values[q, x : x + step] = tile
        return tile

    def give(when):
        @pl.when((span == 1) & when)
        def _():
            pl.semaphore_signal(free_sem, inc=1, device_id=at(row, 0), device_id_type=MESH)

    def take(when):
        @pl.when((span == 0) & when)
        def _():
            pl.semaphore_wait(free_sem, 1)

    exchange(0, values, partial)
    for k in range(1, 4):
        param_copy(k, segment ^ k).wait_recv()

    @pl.loop(0, layers)
    def _(layer):
        moves_at("a", 0, layer)
        receive(0, values)
        moves_at("r", 0, layer)
        give(layer > 0)
        activate(0, values, small[layer, 0:1], small[layer, 1:2])
        moves_at("b", 0, layer)
        partial = convolution(kernels.at[2 * layer], store_hidden)
        finish_sends(0, values)
        take(layer > 0)
        exchange(1, hidden, partial)
        moves_at("a", 1, layer)
        receive(1, hidden)
        moves_at("r", 1, layer)
        give(layer < layers - 1)
        activate(1, hidden, small[layer, 2:3], small[layer, 3:4])
        moves_at("b", 1, layer)
        partial = convolution(kernels.at[2 * layer + 1], store_values)
        finish_sends(1, hidden)

        @pl.when(layer < layers - 1)
        def _():
            take(layer >= 0)
            exchange(0, values, partial)

    for q in range(2):
        whole = values[q].astype(jnp.float32)
        for p in range(2):
            turned[q + 2 * p] = whole[:, p * height : (p + 1) * height].reshape(
                height * width, channels
            )
    for f in range(frames):
        for y in range(height):
            staged[f, y] = turned[f, pl.ds(y, width, stride=height)].astype(jnp.bfloat16)

    def outgoing(k, me, to):
        return pltpu.make_async_remote_copy(
            src_ref=staged.at[:, pl.ds(to * local_rows, local_rows)],
            dst_ref=out.at[0, :, :, pl.ds(pl.multiple_of(me * width, width), width)],
            send_sem=out_send.at[k],
            recv_sem=out_recv.at[me],
            device_id=at(to, span),
            device_id_type=MESH,
        )

    for k in range(1, count):
        outgoing(k, row, lax.rem(row + k, count)).start()
    own = pltpu.make_async_copy(
        staged.at[:, pl.ds(row * local_rows, local_rows)],
        out.at[0, :, :, pl.ds(pl.multiple_of(row * width, width), width)],
        own_sem,
    )
    own.start()
    own.wait()
    moves("end")
    for k in range(1, 4):
        param_copy(k, segment).wait_send()
    for k in range(1, count):
        other = lax.rem(row + k, count)
        outgoing(k, other, row).wait_recv()
        outgoing(k, row, other).wait_send()


def body(latents, conv_first, conv_second, gain_first, bias_first, gain_second, bias_second):
    micro, frames, local_rows, columns, channels = latents.shape
    count = lax.axis_size("rows")
    width = columns // count
    height = local_rows * count
    both = 2 * height
    dma = pltpu.SemaphoreType.DMA
    return pl.pallas_call(
        functools.partial(decode_kernel, count),
        out_shape=jax.ShapeDtypeStruct((1, frames, local_rows, columns, channels), jnp.bfloat16),
        in_specs=[pl.BlockSpec(memory_space=pltpu.HBM)] * 7,
        out_specs=pl.BlockSpec(memory_space=pltpu.VMEM),
        scratch_shapes=[
            pltpu.VMEM((frames, height, width, channels), jnp.bfloat16),
            pltpu.VMEM((frames, height * width, channels), jnp.float32),
            pltpu.VMEM((2, width, both, channels), jnp.bfloat16),
            pltpu.VMEM((2, width, both, channels), jnp.bfloat16),
            pltpu.VMEM((2, 2, width, both, channels), jnp.bfloat16),
            pltpu.VMEM((2, 2, 2, 2, both, channels), jnp.bfloat16),
            pltpu.VMEM((2, 2 * count, 8, channels), jnp.float32),
            pltpu.VMEM((4, 3, width + 2, both, channels), jnp.bfloat16),
            dma,
            dma((count,)),
            dma((count,)),
            dma((2, 2 * count)),
            dma((2, 2 * count)),
            dma((2, 2, 2)),
            dma((2, 2, 2)),
            dma((2,)),
            dma((2,)),
            dma((count,)),
            dma((count,)),
            pltpu.SemaphoreType.REGULAR,
            pltpu.VMEM((8,) + conv_first.shape[1:], jnp.bfloat16),
            pltpu.VMEM((4, 8, channels), jnp.float32),
            dma((4,)),
            dma((4,)),
            dma((8,)),
            dma((8, 2, 3)),
            dma((8, 3)),
            dma((8, 3)),
            dma((8, 3)),
            pltpu.VMEM((4, 1, channels), jnp.bfloat16),
            dma((4,)),
        ],
        compiler_params=pltpu.CompilerParams(
            collective_id=0, has_side_effects=True, vmem_limit_bytes=64 * 2**20 - 2**17
        ),
    )(latents, conv_first, conv_second, gain_first, bias_first, gain_second, bias_second)


def solution(mesh):
    in_specs = (
        P(None, "tm", "rows", None, None),
        P("segment", None, None, None, None, None),
        P("segment", None, None, None, None, None),
        P("segment", None),
        P("segment", None),
        P("segment", None),
        P("segment", None),
    )
    out_specs = P("segment", "tm", "rows", None, None)
    sizes = dict(mesh.shape)

    def run(latents, *params):
        micro, frames, height, columns, channels = latents.shape
        count = sizes["rows"]
        fits = (
            micro == sizes["segment"] == 4
            and params[0].shape == (4, 3, 3, 3, channels, channels)
            and count % 2 == 0
            and sizes["tm"] == 2
            and frames == 8
            and height % (8 * 1) == 0
            and columns % (count * ROWS) == 0
            and channels == 4 * GROUPS
        )
        inner = body if fits else plain_body
        return jax.shard_map(
            inner, mesh=mesh, in_specs=in_specs, out_specs=out_specs, check_vma=False
        )(latents, *params)

    return run
```

```python
import functools

import jax
import jax.numpy as jnp
from jax import lax
from jax.experimental import pallas as pl
from jax.experimental.pallas import tpu as pltpu
from jax.sharding import PartitionSpec as P

GROUPS = 32


EPS = 1e-06


def passed_along(value, axis, steps):
    count = lax.axis_size(axis)
    initial, last = (max(0, -steps), min(count, count - steps))
    return lax.ppermute(value, axis, [(source, source + steps) for source in range(initial, last)])


def padded_2(block, sides, width):
    for axis, dim in sides:
        count = lax.axis_size(axis)
        forward = [(i, i + 1) for i in range(count - 1)]
        backward = [(target, source) for source, target in forward]
        low = lax.ppermute(
            lax.slice_in_dim(block, block.shape[dim] - width, None, axis=dim), axis, forward
        )
        high = lax.ppermute(lax.slice_in_dim(block, 0, width, axis=dim), axis, backward)
        block = jnp.concatenate([low, block, high], axis=dim)
    return block


def normalize(values, norm_gain, norm_bias):
    frames, rows_here, columns, channels = values.shape
    width_group = channels // GROUPS
    grouped = values.astype(jnp.float32).reshape(frames, rows_here, columns, GROUPS, width_group)
    totals = lax.psum(
        (jnp.sum(grouped, axis=(0, 1, 2, 4)), jnp.sum(grouped * grouped, axis=(0, 1, 2, 4))), "rows"
    )
    members = frames * rows_here * lax.axis_size("rows") * columns * width_group
    average = totals[0] / members
    squares = totals[1] / members
    inverse = lax.rsqrt(squares - average * average + EPS)
    scaled = (grouped - average[:, None]) * inverse[:, None]
    scaled = scaled.reshape(values.shape) * norm_gain.astype(jnp.float32) + norm_bias.astype(
        jnp.float32
    )
    return jax.nn.silu(scaled).astype(jnp.bfloat16)


def convolve(active, kernel):
    previous = passed_along(active[-2:], "tm", 1)
    extended = jnp.concatenate([previous, active], axis=0)
    padded = padded_2(extended, (("rows", 1),), 1)
    padded = jnp.pad(padded, ((0, 0), (0, 0), (1, 1), (0, 0)))
    result = lax.conv_general_dilated(
        padded[None],
        kernel,
        (1, 1, 1),
        "VALID",
        dimension_numbers=("NDHWC", "DHWIO", "NDHWC"),
        preferred_element_type=jnp.float32,
    )
    return result[0]


def residual_block(values, params):
    first, second, gain_one, bias_one, gain_two, bias_two = params
    active = normalize(values, gain_one, bias_one)
    hidden = convolve(active, first).astype(jnp.bfloat16)
    active = normalize(hidden, gain_two, bias_two)
    return (values.astype(jnp.float32) + convolve(active, second)).astype(jnp.bfloat16)


def plain_body(latents, conv_first, conv_second, gain_first, bias_first, gain_second, bias_second):
    segments = lax.axis_size("segment")
    micro = latents.shape[0]
    per_segment = micro // segments
    position = lax.axis_index("segment")
    small = jnp.stack([gain_first, bias_first, gain_second, bias_second], axis=1)
    small = lax.all_gather(small, "segment", axis=0, tiled=True)
    first = lax.all_gather(conv_first, "segment", axis=0, tiled=True)
    second = lax.all_gather(conv_second, "segment", axis=0, tiled=True)
    outs = []
    for index in range(per_segment):
        values = lax.dynamic_index_in_dim(
            latents, position * per_segment + index, 0, keepdims=False
        )
        for layer in range(first.shape[0]):
            gains = small[layer]
            values = residual_block(
                values, (first[layer], second[layer], gains[0], gains[1], gains[2], gains[3])
            )
        outs.append(values)
    return jnp.stack(outs)


MESH = pl.DeviceIdType.MESH
ROWS = 16
STEPS = 4
PIECES = 4


def group_sums(values):
    lanes = values.shape[-1]
    lane = lax.broadcasted_iota(jnp.int32, values.shape, 1)
    values = values + jnp.where(
        lax.rem(lane, 2) == 0, pltpu.roll(values, lanes - 1, 1), pltpu.roll(values, 1, 1)
    )
    return values + jnp.where(
        lax.rem(lane, 4) < 2, pltpu.roll(values, lanes - 2, 1), pltpu.roll(values, 2, 1)
    )


def tap_block(weights, dt, dy, dx, channels):
    if dt < 0 or dt > 2:
        return jnp.zeros((channels, channels), jnp.bfloat16)
    return weights[dt, dy, dx]


def decode_kernel(
    count,
    latents,
    first,
    second,
    gain_first,
    bias_first,
    gain_second,
    bias_second,
    out,
    staged,
    turned,
    values,
    hidden,
    sibling,
    edges,
    stats,
    active,
    own_sem,
    in_send,
    in_recv,
    stat_send,
    stat_recv,
    edge_send,
    edge_recv,
    sib_send,
    sib_recv,
    out_send,
    out_recv,
    free_sem,
    kernels,
    small,
    param_send,
    param_recv,
    load_sem,
    w_send,
    w_recv,
    half_send,
    half_recv,
    raw_params,
    raw_sem,
):
    frames, height, width, channels = staged.shape
    local_rows = height // count
    both = 2 * height
    row = lax.axis_index("rows")
    segment = lax.axis_index("segment")
    span = lax.axis_index("tm")
    members = frames * height * width * count * (channels // GROUPS)

    def at(rows_index, tm_index):
        return {"rows": rows_index, "tm": tm_index}

    barrier = pltpu.get_barrier_semaphore()
    for k in range(count):
        other = lax.rem(row + k, count)
        if k:
            pl.semaphore_signal(barrier, inc=1, device_id=at(other, span), device_id_type=MESH)
        pl.semaphore_signal(barrier, inc=1, device_id=at(other, 1 - span), device_id_type=MESH)
    for k in range(1, 4):
        pl.semaphore_signal(
            barrier, inc=1, device_id={"segment": segment ^ k}, device_id_type=MESH
        )
    pl.semaphore_wait(barrier, 2 * count + 2)

    given = (first, second)
    layers = kernels.shape[0] // 2
    depth = channels // 2

    def tensor_part(ref, half, chunk, chunks):
        rows = pl.ds(pl.multiple_of(half * depth, depth), depth)
        size = 3 // chunks
        return ref.at[pl.ds(chunk * size, size), :, :, rows]

    def chunks_of(j):
        return 3 if j < 2 else 1

    def remote_half(j, chunk, source, to, slot):
        return pltpu.make_async_remote_copy(
            src_ref=tensor_part(source, span, chunk, chunks_of(j)),
            dst_ref=tensor_part(kernels.at[j], span, chunk, chunks_of(j)),
            send_sem=w_send.at[j, slot, chunk],
            recv_sem=w_recv.at[j, chunk],
            device_id={"rows": row ^ 1} if to is None else {"segment": to},
            device_id_type=MESH,
        )

    def core_half(j, chunk, half):
        return pltpu.make_async_remote_copy(
            src_ref=tensor_part(kernels.at[j], half, chunk, chunks_of(j)),
            dst_ref=tensor_part(kernels.at[j], half, chunk, chunks_of(j)),
            send_sem=half_send.at[j, chunk],
            recv_sem=half_recv.at[j, chunk],
            device_id={"tm": 1 - span},
            device_id_type=MESH,
        )

    routes = "ZZVXVVVV"

    def move(name):
        kind, j = name[0], int(name[1])
        route = routes[j]
        away = segment ^ (j // 2)
        source = given[j % 2].at[0]
        each = range(chunks_of(j))
        if route == "X":
            first_to = segment ^ 1
            second_to = pass_to = segment ^ 2
            passes = away == 1
        else:
            turn = lax.rem(row + span, 2) if route == "Z" else span
            first_to = segment ^ (1 + turn)
            second_to = pass_to = segment ^ (2 - turn)
            passes = away == 1 + turn
        here = kernels.at[j]
        if kind == "P":

            @pl.when(away == 0)
            def _():
                for c in each:
                    remote_half(j, c, source, first_to, 0).start()

        if kind == "Q":

            @pl.when(away == 0)
            def _():
                for c in each:
                    remote_half(j - 1, c, given[(j - 1) % 2].at[0], first_to, 0).wait_send()
                    remote_half(j, c, source, first_to, 0).start()

        if kind == "S":

            @pl.when(away == 0)
            def _():
                for c in each:
                    remote_half(j, c, source, second_to, 1).start()

        if kind == "F":

            @pl.when(passes)
            def _():
                for c in each:
                    remote_half(j, c, here, pass_to, 0).wait_recv()
                    remote_half(j, c, here, pass_to, 0).start()
                    if route == "Z":
                        remote_half(j, c, here, None, 1).start()
                    core_half(j, c, span).start()

        if kind == "R":

            @pl.when((away > 0) & jnp.logical_not(passes))
            def _():
                for c in each:
                    remote_half(j, c, here, pass_to, 0).wait_recv()
                    core_half(j, c, span).start()

        if kind == "G":

            @pl.when(away > 0)
            def _():
                for c in each:
                    core_half(j, c, 1 - span).wait_recv()

            @pl.when(away == 0)
            def _():
                pltpu.make_async_copy(source, kernels.at[j], load_sem.at[j]).wait()

        if kind == "W":

            @pl.when(away == 0)
            def _():
                for c in each:
                    if j > 0:
                        remote_half(j, c, source, first_to, 0).wait_send()
                    if route != "Z":
                        remote_half(j, c, source, second_to, 1).wait_send()

            @pl.when(passes)
            def _():
                for c in each:
                    remote_half(j, c, here, pass_to, 0).wait_send()
                    if route == "Z":
                        remote_half(j, c, here, None, 1).wait_send()

            @pl.when(away > 0)
            def _():
                for c in each:
                    core_half(j, c, span).wait_send()

    plan = {
        "start": ("P0", "P2", "P4", "P6"),
        "early": ("Q1", "F0"),
        "a0": ("P3", "F1", "R0"),
        "r0": ("F2", "S2", "S4"),
        "b0": ("G0",),
        "a1": ("S3", "S6", "F4", "R1"),
        "b1": ("G1",),
        "a2": ("F3", "P5", "R2", "F6"),
        "b2": ("G2",),
        "a3": ("S5", "P7", "R4", "R3"),
        "r3": ("F5",),
        "b3": ("G3",),
        "a4": ("S7", "R6"),
        "b4": ("G4",),
        "a5": ("F7", "R5"),
        "b5": ("G5",),
        "r6": ("R7",),
        "b6": ("G6",),
        "b7": ("G7",),
        "end": ("W0", "W1", "W2", "W3", "W4", "W5", "W6", "W7"),
    }

    def moves(point):
        for name in plan.get(point, ()):
            move(name)

    def moves_at(letter, which, layer):
        for known in range(layers):
            point = letter + str(2 * known + which)
            if point in plan:

                @pl.when(layer == known)
                def _(point=point):
                    moves(point)

    def incoming(k, me, to):
        return pltpu.make_async_remote_copy(
            src_ref=latents.at[segment, :, :, pl.ds(pl.multiple_of(to * width, width), width)],
            dst_ref=staged.at[:, pl.ds(me * local_rows, local_rows)],
            send_sem=in_send.at[k],
            recv_sem=in_recv.at[me],
            device_id=at(to, span),
            device_id_type=MESH,
        )

    moves("start")
    for k in range(1, count):
        incoming(k, row, lax.rem(row + k, count)).start()
    for j in range(2 * layers):

        @pl.when(segment == j // 2)
        def _(j=j):
            pltpu.make_async_copy(given[j % 2].at[0], kernels.at[j], load_sem.at[j]).start()

    index = lax.broadcasted_iota(jnp.int32, (8, channels), 0)
    raw = [
        pltpu.make_async_copy(ref, raw_params.at[k], raw_sem.at[k])
        for k, ref in enumerate((gain_first, bias_first, gain_second, bias_second))
    ]
    for copy in raw:
        copy.start()
    for copy in raw:
        copy.wait()
    packed = jnp.zeros((8, channels), jnp.float32)
    for k in range(4):
        packed = jnp.where(index == k, raw_params[k].astype(jnp.float32), packed)
    small[segment] = packed

    def param_copy(k, me):
        return pltpu.make_async_remote_copy(
            src_ref=small.at[me],
            dst_ref=small.at[me],
            send_sem=param_send.at[k],
            recv_sem=param_recv.at[me],
            device_id={"segment": segment ^ k},
            device_id_type=MESH,
        )

    for k in range(1, 4):
        param_copy(k, segment).start()
    own = pltpu.make_async_copy(
        latents.at[segment, :, :, pl.ds(pl.multiple_of(row * width, width), width)],
        staged.at[:, pl.ds(row * local_rows, local_rows)],
        own_sem,
    )
    own.start()
    moves("early")
    own.wait()
    for k in range(1, count):
        other = lax.rem(row + k, count)
        incoming(k, other, row).wait_recv()

    for f in range(frames):
        turned[f] = staged[f].astype(jnp.float32).reshape(height * width, channels)
    zero = jnp.zeros((height, channels), jnp.float32)

    def turn(x, carry):
        total, squares = carry
        for q in range(2):
            tile = jnp.concatenate(
                [turned[q + 2 * p, pl.ds(x, height, stride=width)] for p in range(2)], axis=0
            )
            values[q, x] = tile.astype(jnp.bfloat16)
            total = total + tile[:height] + tile[height:]
            tile = tile * tile
            squares = squares + tile[:height] + tile[height:]
        return total, squares

    partial = lax.fori_loop(0, width, turn, (zero, zero), unroll=4)
    for k in range(1, count):
        incoming(k, row, lax.rem(row + k, count)).wait_send()

    def stat_copy(par, k, me, to, tm_from, tm_to):
        slot = tm_from * count + me
        cross = 0 if tm_from is tm_to else count
        return pltpu.make_async_remote_copy(
            src_ref=stats.at[par, slot],
            dst_ref=stats.at[par, slot],
            send_sem=stat_send.at[par, k + cross],
            recv_sem=stat_recv.at[par, slot],
            device_id=at(to, tm_to),
            device_id_type=MESH,
        )

    def edge_copy(par, source, side, tm_from, tm_to, to):
        return pltpu.make_async_remote_copy(
            src_ref=source.at[:, width - 1 if side == 0 else 0],
            dst_ref=edges.at[par, side, tm_from],
            send_sem=edge_send.at[par, side, tm_to],
            recv_sem=edge_recv.at[par, side, tm_from],
            device_id=at(to, tm_to),
            device_id_type=MESH,
        )

    def sib_copy(par, source):
        return pltpu.make_async_remote_copy(
            src_ref=source,
            dst_ref=sibling.at[par],
            send_sem=sib_send.at[par],
            recv_sem=sib_recv.at[par],
            device_id=at(row, 1),
            device_id_type=MESH,
        )

    def each_send(par, source, act):
        for k in range(1, count):
            act(stat_copy(par, k, row, lax.rem(row + k, count), span, span))

        @pl.when(span == 0)
        def _():
            for k in range(count):
                act(stat_copy(par, k, row, lax.rem(row + k, count), 0, 1))

        for side, there in ((0, row < count - 1), (1, row > 0)):

            @pl.when(there)
            def _(side=side):
                to = row + 1 if side == 0 else row - 1
                act(edge_copy(par, source, side, span, span, to))

                @pl.when(span == 0)
                def _():
                    act(edge_copy(par, source, side, 0, 1, to))

        @pl.when(span == 0)
        def _():
            act(sib_copy(par, source))

    def exchange(par, source, partial):
        index = lax.broadcasted_iota(jnp.int32, (8, channels), 0)
        total = jnp.sum(partial[0], axis=0, keepdims=True)
        squares = jnp.sum(partial[1], axis=0, keepdims=True)
        stats[par, span * count + row] = jnp.where(
            index == 0, total, jnp.where(index == 1, squares, 0.0)
        )
        each_send(par, source, lambda copy: copy.start())

    def finish_sends(par, source):
        each_send(par, source, lambda copy: copy.wait_send())

    def receive(par, source):
        for side, there in ((0, row > 0), (1, row < count - 1)):

            @pl.when(there)
            def _(side=side):
                edge_copy(par, source, side, span, span, row).wait_recv()

                @pl.when(span == 1)
                def _():
                    edge_copy(par, source, side, 0, 1, row).wait_recv()

        @pl.when(span == 1)
        def _():
            sib_copy(par, source).wait_recv()
            for k in range(count):
                stat_copy(par, k, lax.rem(row + k, count), row, 0, 1).wait_recv()

        for k in range(1, count):
            stat_copy(par, k, lax.rem(row + k, count), row, span, span).wait_recv()

    def moments(par, base, gain):
        total = stats[par, base]
        for k in range(1, count):
            total = total + stats[par, base + k]
        total = group_sums(total) / members
        average = total[0:1]
        return average, lax.rsqrt(total[1:2] - average * average + EPS) * gain

    def layer_half(par, source, gain, bias, weights, store):
        mine = moments(par, span * count, gain)
        before = moments(par, 0, gain)
        later = span > 0
        index = lax.broadcasted_iota(jnp.int32, (1, height, channels), 1)

        def silu(tile, moment):
            half = ((tile - moment[0]) * moment[1] + bias) * 0.5
            return half + half * jnp.tanh(half)

        def shifted(a, dy):
            if dy == 0:
                return jnp.where(index == 0, 0.0, pltpu.roll(a, 1, 1))
            if dy == 2:
                return jnp.where(index == height - 1, 0.0, pltpu.roll(a, height - 1, 1))
            return a

        def put(q, x, size, tile, older, valid):
            a = silu(tile.astype(jnp.float32), mine).reshape(2 * size, height, channels)
            b = silu(older.astype(jnp.float32)[:, height:], before)
            b = jnp.where(later, b, 0.0)
            if valid is not None:
                a = jnp.where(valid, a, 0.0)
                b = jnp.where(valid, b, 0.0)
            for dy in range(3):
                now = shifted(a, dy).reshape(size, both, channels)
                old = shifted(b, dy)
                active[2 + q, dy, x : x + size] = now.astype(jnp.bfloat16)
                active[q, dy, x : x + size] = jnp.concatenate(
                    [old, now[:, :height]], axis=1
                ).astype(jnp.bfloat16)

        def columns_at(x, size):
            for q in range(2):
                put(
                    q, x + 1, size, source[q, x : x + size], sibling[par, q, x : x + size], None
                )

        def border(side):
            there = row > 0 if side == 0 else row < count - 1
            for q in range(2):
                put(
                    q,
                    0 if side == 0 else width + 1,
                    1,
                    edges[par, side, span, q][None],
                    edges[par, side, 0, q][None],
                    there,
                )

        def products(x, step):
            left, right = [], []
            for dy in range(3):
                for dx in range(3):
                    for k in (1, 2, 0, 3):
                        left.append(
                            active[k, dy, x + dx : x + dx + step].reshape(step * both, channels)
                        )
                        right.append(
                            jnp.concatenate(
                                [tap_block(weights, k - q, dy, dx, channels) for q in range(2)],
                                axis=1,
                            )
                        )
            result = jnp.dot(
                jnp.concatenate(left, axis=1),
                jnp.concatenate(right, axis=0),
                preferred_element_type=jnp.float32,
            )
            sums = []
            for q in range(2):
                tile = store(
                    q,
                    x,
                    step,
                    result[:, q * channels : (q + 1) * channels].reshape(step, both, channels),
                )
                tile = tile.astype(jnp.float32).reshape(-1, height, channels)
                sums.append((jnp.sum(tile, axis=0), jnp.sum(tile * tile, axis=0)))
            return [sums[0][i] + sums[1][i] for i in range(2)]

        step, piece = width // STEPS, width // PIECES
        ready, partial = 0, None
        border(0)
        for x in range(0, width, step):
            while ready < min(x + step + 1, width):
                columns_at(ready, piece)
                ready += piece
                if ready == width:
                    border(1)
            sums = products(x, step)
            partial = sums if partial is None else [partial[i] + sums[i] for i in range(2)]
        return tuple(partial)

    def store_hidden(q, x, step, tile):
        tile = tile.astype(jnp.bfloat16)
        hidden[q, x : x + step] = tile
        return tile

    def store_values(q, x, step, tile):
        tile = (values[q, x : x + step].astype(jnp.float32) + tile).astype(jnp.bfloat16)
        values[q, x : x + step] = tile
        return tile

    def give(when):
        @pl.when((span == 1) & when)
        def _():
            pl.semaphore_signal(free_sem, inc=1, device_id=at(row, 0), device_id_type=MESH)

    def take(when):
        @pl.when((span == 0) & when)
        def _():
            pl.semaphore_wait(free_sem, 1)

    exchange(0, values, partial)
    for k in range(1, 4):
        param_copy(k, segment ^ k).wait_recv()

    @pl.loop(0, layers)
    def _(layer):
        moves_at("a", 0, layer)
        receive(0, values)
        moves_at("r", 0, layer)
        give(layer > 0)
        moves_at("b", 0, layer)
        partial = layer_half(
            0,
            values,
            small[layer, 0:1],
            small[layer, 1:2],
            kernels.at[2 * layer],
            store_hidden,
        )
        take(layer > 0)
        exchange(1, hidden, partial)
        finish_sends(0, values)
        moves_at("a", 1, layer)
        receive(1, hidden)
        moves_at("r", 1, layer)
        give(layer < layers - 1)
        moves_at("b", 1, layer)
        partial = layer_half(
            1,
            hidden,
            small[layer, 2:3],
            small[layer, 3:4],
            kernels.at[2 * layer + 1],
            store_values,
        )

        @pl.when(layer < layers - 1)
        def _():
            take(layer >= 0)
            exchange(0, values, partial)

        finish_sends(1, hidden)

    for q in range(2):
        whole = values[q].astype(jnp.float32)
        for p in range(2):
            turned[q + 2 * p] = whole[:, p * height : (p + 1) * height].reshape(
                height * width, channels
            )
    def outgoing(k, me, to):
        return pltpu.make_async_remote_copy(
            src_ref=staged.at[:, pl.ds(to * local_rows, local_rows)],
            dst_ref=out.at[0, :, :, pl.ds(pl.multiple_of(me * width, width), width)],
            send_sem=out_send.at[k],
            recv_sem=out_recv.at[me],
            device_id=at(to, span),
            device_id_type=MESH,
        )

    def stage(to):
        for f in range(frames):
            for i in range(local_rows):
                y = to * local_rows + i
                staged[f, y] = turned[f, pl.ds(y, width, stride=height)].astype(jnp.bfloat16)

    for k in range(1, count):
        stage(lax.rem(row + k, count))
        outgoing(k, row, lax.rem(row + k, count)).start()
    stage(row)
    own = pltpu.make_async_copy(
        staged.at[:, pl.ds(row * local_rows, local_rows)],
        out.at[0, :, :, pl.ds(pl.multiple_of(row * width, width), width)],
        own_sem,
    )
    own.start()
    own.wait()
    moves("end")
    for k in range(1, 4):
        param_copy(k, segment).wait_send()
    for k in range(1, count):
        other = lax.rem(row + k, count)
        outgoing(k, other, row).wait_recv()
        outgoing(k, row, other).wait_send()


def body(latents, conv_first, conv_second, gain_first, bias_first, gain_second, bias_second):
    micro, frames, local_rows, columns, channels = latents.shape
    count = lax.axis_size("rows")
    width = columns // count
    height = local_rows * count
    both = 2 * height
    dma = pltpu.SemaphoreType.DMA
    return pl.pallas_call(
        functools.partial(decode_kernel, count),
        out_shape=jax.ShapeDtypeStruct((1, frames, local_rows, columns, channels), jnp.bfloat16),
        in_specs=[pl.BlockSpec(memory_space=pltpu.HBM)] * 7,
        out_specs=pl.BlockSpec(memory_space=pltpu.VMEM),
        scratch_shapes=[
            pltpu.VMEM((frames, height, width, channels), jnp.bfloat16),
            pltpu.VMEM((frames, height * width, channels), jnp.float32),
            pltpu.VMEM((2, width, both, channels), jnp.bfloat16),
            pltpu.VMEM((2, width, both, channels), jnp.bfloat16),
            pltpu.VMEM((2, 2, width, both, channels), jnp.bfloat16),
            pltpu.VMEM((2, 2, 2, 2, both, channels), jnp.bfloat16),
            pltpu.VMEM((2, 2 * count, 8, channels), jnp.float32),
            pltpu.VMEM((4, 3, width + 2, both, channels), jnp.bfloat16),
            dma,
            dma((count,)),
            dma((count,)),
            dma((2, 2 * count)),
            dma((2, 2 * count)),
            dma((2, 2, 2)),
            dma((2, 2, 2)),
            dma((2,)),
            dma((2,)),
            dma((count,)),
            dma((count,)),
            pltpu.SemaphoreType.REGULAR,
            pltpu.VMEM((8,) + conv_first.shape[1:], jnp.bfloat16),
            pltpu.VMEM((4, 8, channels), jnp.float32),
            dma((4,)),
            dma((4,)),
            dma((8,)),
            dma((8, 2, 3)),
            dma((8, 3)),
            dma((8, 3)),
            dma((8, 3)),
            pltpu.VMEM((4, 1, channels), jnp.bfloat16),
            dma((4,)),
        ],
        compiler_params=pltpu.CompilerParams(
            collective_id=0, has_side_effects=True, vmem_limit_bytes=64 * 2**20 - 2**17
        ),
    )(latents, conv_first, conv_second, gain_first, bias_first, gain_second, bias_second)


def solution(mesh):
    in_specs = (
        P(None, "tm", "rows", None, None),
        P("segment", None, None, None, None, None),
        P("segment", None, None, None, None, None),
        P("segment", None),
        P("segment", None),
        P("segment", None),
        P("segment", None),
    )
    out_specs = P("segment", "tm", "rows", None, None)
    sizes = dict(mesh.shape)

    def run(latents, *params):
        micro, frames, height, columns, channels = latents.shape
        count = sizes["rows"]
        fits = (
            micro == sizes["segment"] == 4
            and params[0].shape == (4, 3, 3, 3, channels, channels)
            and count % 2 == 0
            and sizes["tm"] == 2
            and frames == 8
            and height % (8 * 1) == 0
            and columns % (count * ROWS) == 0
            and channels == 4 * GROUPS
        )
        inner = body if fits else plain_body
        return jax.shard_map(
            inner, mesh=mesh, in_specs=in_specs, out_specs=out_specs, check_vma=False
        )(latents, *params)

    return run
```

```python
import functools

import jax
import jax.numpy as jnp
from jax import lax
from jax.experimental import pallas as pl
from jax.experimental.pallas import tpu as pltpu
from jax.sharding import PartitionSpec as P

GROUPS = 32


EPS = 1e-06


def passed_along(value, axis, steps):
    count = lax.axis_size(axis)
    initial, last = (max(0, -steps), min(count, count - steps))
    return lax.ppermute(value, axis, [(source, source + steps) for source in range(initial, last)])


def padded_2(block, sides, width):
    for axis, dim in sides:
        count = lax.axis_size(axis)
        forward = [(i, i + 1) for i in range(count - 1)]
        backward = [(target, source) for source, target in forward]
        low = lax.ppermute(
            lax.slice_in_dim(block, block.shape[dim] - width, None, axis=dim), axis, forward
        )
        high = lax.ppermute(lax.slice_in_dim(block, 0, width, axis=dim), axis, backward)
        block = jnp.concatenate([low, block, high], axis=dim)
    return block


def normalize(values, norm_gain, norm_bias):
    frames, rows_here, columns, channels = values.shape
    width_group = channels // GROUPS
    grouped = values.astype(jnp.float32).reshape(frames, rows_here, columns, GROUPS, width_group)
    totals = lax.psum(
        (jnp.sum(grouped, axis=(0, 1, 2, 4)), jnp.sum(grouped * grouped, axis=(0, 1, 2, 4))), "rows"
    )
    members = frames * rows_here * lax.axis_size("rows") * columns * width_group
    average = totals[0] / members
    squares = totals[1] / members
    inverse = lax.rsqrt(squares - average * average + EPS)
    scaled = (grouped - average[:, None]) * inverse[:, None]
    scaled = scaled.reshape(values.shape) * norm_gain.astype(jnp.float32) + norm_bias.astype(
        jnp.float32
    )
    return jax.nn.silu(scaled).astype(jnp.bfloat16)


def convolve(active, kernel):
    previous = passed_along(active[-2:], "tm", 1)
    extended = jnp.concatenate([previous, active], axis=0)
    padded = padded_2(extended, (("rows", 1),), 1)
    padded = jnp.pad(padded, ((0, 0), (0, 0), (1, 1), (0, 0)))
    result = lax.conv_general_dilated(
        padded[None],
        kernel,
        (1, 1, 1),
        "VALID",
        dimension_numbers=("NDHWC", "DHWIO", "NDHWC"),
        preferred_element_type=jnp.float32,
    )
    return result[0]


def residual_block(values, params):
    first, second, gain_one, bias_one, gain_two, bias_two = params
    active = normalize(values, gain_one, bias_one)
    hidden = convolve(active, first).astype(jnp.bfloat16)
    active = normalize(hidden, gain_two, bias_two)
    return (values.astype(jnp.float32) + convolve(active, second)).astype(jnp.bfloat16)


def plain_body(latents, conv_first, conv_second, gain_first, bias_first, gain_second, bias_second):
    segments = lax.axis_size("segment")
    micro = latents.shape[0]
    per_segment = micro // segments
    position = lax.axis_index("segment")
    small = jnp.stack([gain_first, bias_first, gain_second, bias_second], axis=1)
    small = lax.all_gather(small, "segment", axis=0, tiled=True)
    first = lax.all_gather(conv_first, "segment", axis=0, tiled=True)
    second = lax.all_gather(conv_second, "segment", axis=0, tiled=True)
    outs = []
    for index in range(per_segment):
        values = lax.dynamic_index_in_dim(
            latents, position * per_segment + index, 0, keepdims=False
        )
        for layer in range(first.shape[0]):
            gains = small[layer]
            values = residual_block(
                values, (first[layer], second[layer], gains[0], gains[1], gains[2], gains[3])
            )
        outs.append(values)
    return jnp.stack(outs)


MESH = pl.DeviceIdType.MESH
ROWS = 16
STEPS = 4
PIECES = 4


def group_sums(values):
    lanes = values.shape[-1]
    lane = lax.broadcasted_iota(jnp.int32, values.shape, 1)
    values = values + jnp.where(
        lax.rem(lane, 2) == 0, pltpu.roll(values, lanes - 1, 1), pltpu.roll(values, 1, 1)
    )
    return values + jnp.where(
        lax.rem(lane, 4) < 2, pltpu.roll(values, lanes - 2, 1), pltpu.roll(values, 2, 1)
    )


def tap_block(weights, dt, dy, dx, channels):
    if dt < 0 or dt > 2:
        return jnp.zeros((channels, channels), jnp.bfloat16)
    return weights[dt, dy, dx]


def decode_kernel(
    count,
    latents,
    first,
    second,
    gain_first,
    bias_first,
    gain_second,
    bias_second,
    out,
    staged,
    turned,
    values,
    hidden,
    sibling,
    edges,
    stats,
    active,
    own_sem,
    in_send,
    in_recv,
    stat_send,
    stat_recv,
    edge_send,
    edge_recv,
    sib_send,
    sib_recv,
    out_send,
    out_recv,
    free_sem,
    kernels,
    small,
    param_send,
    param_recv,
    load_sem,
    w_send,
    w_recv,
    half_send,
    half_recv,
    raw_params,
    raw_sem,
):
    frames, height, width, channels = staged.shape
    local_rows = height // count
    both = 2 * height
    row = lax.axis_index("rows")
    segment = lax.axis_index("segment")
    span = lax.axis_index("tm")
    members = frames * height * width * count * (channels // GROUPS)

    def at(rows_index, tm_index):
        return {"rows": rows_index, "tm": tm_index}

    barrier = pltpu.get_barrier_semaphore()
    for k in range(count):
        other = lax.rem(row + k, count)
        if k:
            pl.semaphore_signal(barrier, inc=1, device_id=at(other, span), device_id_type=MESH)
        pl.semaphore_signal(barrier, inc=1, device_id=at(other, 1 - span), device_id_type=MESH)
    for k in range(1, 4):
        pl.semaphore_signal(
            barrier, inc=1, device_id={"segment": segment ^ k}, device_id_type=MESH
        )
    pl.semaphore_wait(barrier, 2 * count + 2)

    given = (first, second)
    layers = kernels.shape[0] // 2
    for k in (0, 3):
        for dy in range(3):
            active[k, dy, width + 2] = jnp.zeros((both, channels), jnp.bfloat16)
    depth = channels // 2

    def tensor_part(ref, half, chunk, chunks):
        rows = pl.ds(pl.multiple_of(half * depth, depth), depth)
        size = 3 // chunks
        return ref.at[pl.ds(chunk * size, size), :, :, rows]

    def chunks_of(j):
        return 3 if j < 2 else 1

    def remote_half(j, chunk, source, to, slot):
        return pltpu.make_async_remote_copy(
            src_ref=tensor_part(source, span, chunk, chunks_of(j)),
            dst_ref=tensor_part(kernels.at[j], span, chunk, chunks_of(j)),
            send_sem=w_send.at[j, slot, chunk],
            recv_sem=w_recv.at[j, chunk],
            device_id={"rows": row ^ 1} if to is None else {"segment": to},
            device_id_type=MESH,
        )

    def core_half(j, chunk, half):
        return pltpu.make_async_remote_copy(
            src_ref=tensor_part(kernels.at[j], half, chunk, chunks_of(j)),
            dst_ref=tensor_part(kernels.at[j], half, chunk, chunks_of(j)),
            send_sem=half_send.at[j, chunk],
            recv_sem=half_recv.at[j, chunk],
            device_id={"tm": 1 - span},
            device_id_type=MESH,
        )

    routes = "ZZVXVVVV"

    def move(name):
        kind, j = name[0], int(name[1])
        route = routes[j]
        away = segment ^ (j // 2)
        source = given[j % 2].at[0]
        each = range(chunks_of(j))
        if route == "X":
            first_to = segment ^ 1
            second_to = pass_to = segment ^ 2
            passes = away == 1
        else:
            turn = lax.rem(row + span, 2) if route == "Z" else span
            first_to = segment ^ (1 + turn)
            second_to = pass_to = segment ^ (2 - turn)
            passes = away == 1 + turn
        here = kernels.at[j]
        if kind == "P":

            @pl.when(away == 0)
            def _():
                for c in each:
                    remote_half(j, c, source, first_to, 0).start()

        if kind == "Q":

            @pl.when(away == 0)
            def _():
                for c in each:
                    remote_half(j - 1, c, given[(j - 1) % 2].at[0], first_to, 0).wait_send()
                    remote_half(j, c, source, first_to, 0).start()

        if kind == "S":

            @pl.when(away == 0)
            def _():
                for c in each:
                    remote_half(j, c, source, second_to, 1).start()

        if kind == "F":

            @pl.when(passes)
            def _():
                for c in each:
                    remote_half(j, c, here, pass_to, 0).wait_recv()
                    remote_half(j, c, here, pass_to, 0).start()
                    if route == "Z":
                        remote_half(j, c, here, None, 1).start()
                    core_half(j, c, span).start()

        if kind == "R":

            @pl.when((away > 0) & jnp.logical_not(passes))
            def _():
                for c in each:
                    remote_half(j, c, here, pass_to, 0).wait_recv()
                    core_half(j, c, span).start()

        if kind == "G":

            @pl.when(away > 0)
            def _():
                for c in each:
                    core_half(j, c, 1 - span).wait_recv()

            @pl.when(away == 0)
            def _():
                pltpu.make_async_copy(source, kernels.at[j], load_sem.at[j]).wait()

        if kind == "W":

            @pl.when(away == 0)
            def _():
                for c in each:
                    if j > 0:
                        remote_half(j, c, source, first_to, 0).wait_send()
                    if route != "Z":
                        remote_half(j, c, source, second_to, 1).wait_send()

            @pl.when(passes)
            def _():
                for c in each:
                    remote_half(j, c, here, pass_to, 0).wait_send()
                    if route == "Z":
                        remote_half(j, c, here, None, 1).wait_send()

            @pl.when(away > 0)
            def _():
                for c in each:
                    core_half(j, c, span).wait_send()

    plan = {
        "start": ("P0", "P2", "P4", "P6"),
        "early": ("Q1", "F0"),
        "a0": ("P3", "F1", "R0"),
        "r0": ("F2", "S2", "S4"),
        "b0": ("G0",),
        "a1": ("S3", "S6", "F4", "R1"),
        "b1": ("G1",),
        "a2": ("F3", "P5", "R2", "F6"),
        "b2": ("G2",),
        "a3": ("S5", "P7", "R4", "R3"),
        "r3": ("F5",),
        "b3": ("G3",),
        "a4": ("S7", "R6"),
        "b4": ("G4",),
        "a5": ("F7", "R5"),
        "b5": ("G5",),
        "r6": ("R7",),
        "b6": ("G6",),
        "b7": ("G7",),
        "end": ("W0", "W1", "W2", "W3", "W4", "W5", "W6", "W7"),
    }

    def moves(point):
        for name in plan.get(point, ()):
            move(name)

    def moves_at(letter, which, layer):
        for known in range(layers):
            point = letter + str(2 * known + which)
            if point in plan:

                @pl.when(layer == known)
                def _(point=point):
                    moves(point)

    def incoming(k, me, to):
        return pltpu.make_async_remote_copy(
            src_ref=latents.at[segment, :, :, pl.ds(pl.multiple_of(to * width, width), width)],
            dst_ref=staged.at[:, pl.ds(me * local_rows, local_rows)],
            send_sem=in_send.at[k],
            recv_sem=in_recv.at[me],
            device_id=at(to, span),
            device_id_type=MESH,
        )

    moves("start")
    for k in range(1, count):
        incoming(k, row, lax.rem(row + k, count)).start()
    for j in range(2 * layers):

        @pl.when(segment == j // 2)
        def _(j=j):
            pltpu.make_async_copy(given[j % 2].at[0], kernels.at[j], load_sem.at[j]).start()

    index = lax.broadcasted_iota(jnp.int32, (8, channels), 0)
    raw = [
        pltpu.make_async_copy(ref, raw_params.at[k], raw_sem.at[k])
        for k, ref in enumerate((gain_first, bias_first, gain_second, bias_second))
    ]
    for copy in raw:
        copy.start()
    for copy in raw:
        copy.wait()
    packed = jnp.zeros((8, channels), jnp.float32)
    for k in range(4):
        packed = jnp.where(index == k, raw_params[k].astype(jnp.float32), packed)
    small[segment] = packed

    def param_copy(k, me):
        return pltpu.make_async_remote_copy(
            src_ref=small.at[me],
            dst_ref=small.at[me],
            send_sem=param_send.at[k],
            recv_sem=param_recv.at[me],
            device_id={"segment": segment ^ k},
            device_id_type=MESH,
        )

    for k in range(1, 4):
        param_copy(k, segment).start()
    own = pltpu.make_async_copy(
        latents.at[segment, :, :, pl.ds(pl.multiple_of(row * width, width), width)],
        staged.at[:, pl.ds(row * local_rows, local_rows)],
        own_sem,
    )
    own.start()
    moves("early")
    own.wait()
    for k in range(1, count):
        other = lax.rem(row + k, count)
        incoming(k, other, row).wait_recv()

    for f in range(frames):
        turned[f] = staged[f].astype(jnp.float32).reshape(height * width, channels)
    zero = jnp.zeros((height, channels), jnp.float32)

    def turn(x, carry):
        total, squares = carry
        for q in range(2):
            tile = jnp.concatenate(
                [turned[q + 2 * p, pl.ds(x, height, stride=width)] for p in range(2)], axis=0
            )
            values[q, x] = tile.astype(jnp.bfloat16)
            total = total + tile[:height] + tile[height:]
            tile = tile * tile
            squares = squares + tile[:height] + tile[height:]
        return total, squares

    partial = lax.fori_loop(0, width, turn, (zero, zero), unroll=4)
    for k in range(1, count):
        incoming(k, row, lax.rem(row + k, count)).wait_send()

    def stat_copy(par, k, me, to, tm_from, tm_to):
        slot = tm_from * count + me
        cross = 0 if tm_from is tm_to else count
        return pltpu.make_async_remote_copy(
            src_ref=stats.at[par, slot],
            dst_ref=stats.at[par, slot],
            send_sem=stat_send.at[par, k + cross],
            recv_sem=stat_recv.at[par, slot],
            device_id=at(to, tm_to),
            device_id_type=MESH,
        )

    def edge_copy(par, source, side, tm_from, tm_to, to):
        return pltpu.make_async_remote_copy(
            src_ref=source.at[:, width - 1 if side == 0 else 0],
            dst_ref=edges.at[par, side, tm_from],
            send_sem=edge_send.at[par, side, tm_to],
            recv_sem=edge_recv.at[par, side, tm_from],
            device_id=at(to, tm_to),
            device_id_type=MESH,
        )

    def sib_copy(par, source):
        return pltpu.make_async_remote_copy(
            src_ref=source,
            dst_ref=sibling.at[par],
            send_sem=sib_send.at[par],
            recv_sem=sib_recv.at[par],
            device_id=at(row, 1),
            device_id_type=MESH,
        )

    def each_send(par, source, act):
        for k in range(1, count):
            act(stat_copy(par, k, row, lax.rem(row + k, count), span, span))

        @pl.when(span == 0)
        def _():
            for k in range(count):
                act(stat_copy(par, k, row, lax.rem(row + k, count), 0, 1))

        for side, there in ((0, row < count - 1), (1, row > 0)):

            @pl.when(there)
            def _(side=side):
                to = row + 1 if side == 0 else row - 1
                act(edge_copy(par, source, side, span, span, to))

                @pl.when(span == 0)
                def _():
                    act(edge_copy(par, source, side, 0, 1, to))

        @pl.when(span == 0)
        def _():
            act(sib_copy(par, source))

    def exchange(par, source, partial):
        index = lax.broadcasted_iota(jnp.int32, (8, channels), 0)
        total = jnp.sum(partial[0], axis=0, keepdims=True)
        squares = jnp.sum(partial[1], axis=0, keepdims=True)
        stats[par, span * count + row] = jnp.where(
            index == 0, total, jnp.where(index == 1, squares, 0.0)
        )
        each_send(par, source, lambda copy: copy.start())

    def finish_sends(par, source):
        each_send(par, source, lambda copy: copy.wait_send())

    def receive(par, source):
        for side, there in ((0, row > 0), (1, row < count - 1)):

            @pl.when(there)
            def _(side=side):
                edge_copy(par, source, side, span, span, row).wait_recv()

                @pl.when(span == 1)
                def _():
                    edge_copy(par, source, side, 0, 1, row).wait_recv()

        @pl.when(span == 1)
        def _():
            sib_copy(par, source).wait_recv()
            for k in range(count):
                stat_copy(par, k, lax.rem(row + k, count), row, 0, 1).wait_recv()

        for k in range(1, count):
            stat_copy(par, k, lax.rem(row + k, count), row, span, span).wait_recv()

    def moments(par, base, gain):
        total = stats[par, base]
        for k in range(1, count):
            total = total + stats[par, base + k]
        total = group_sums(total) / members
        average = total[0:1]
        return average, lax.rsqrt(total[1:2] - average * average + EPS) * gain

    def layer_half(par, source, gain, bias, weights, store):
        mine = moments(par, span * count, gain)
        before = moments(par, 0, gain)
        later = span > 0
        index = lax.broadcasted_iota(jnp.int32, (1, height, channels), 1)

        def silu(tile, moment):
            half = ((tile - moment[0]) * moment[1] + bias) * 0.5
            return half + half * jnp.tanh(half)

        def shifted(a, dy):
            if dy == 0:
                return jnp.where(index == 0, 0.0, pltpu.roll(a, 1, 1))
            if dy == 2:
                return jnp.where(index == height - 1, 0.0, pltpu.roll(a, height - 1, 1))
            return a

        def put(q, x, size, tile, older, valid):
            a = silu(tile.astype(jnp.float32), mine).reshape(2 * size, height, channels)
            b = silu(older.astype(jnp.float32)[:, height:], before)
            b = jnp.where(later, b, 0.0)
            if valid is not None:
                a = jnp.where(valid, a, 0.0)
                b = jnp.where(valid, b, 0.0)
            for dy in range(3):
                now = shifted(a, dy).reshape(size, both, channels)
                old = shifted(b, dy)
                active[2 + q, dy, x : x + size] = now.astype(jnp.bfloat16)
                active[q, dy, x : x + size] = jnp.concatenate(
                    [old, now[:, :height]], axis=1
                ).astype(jnp.bfloat16)

        def columns_at(x, size):
            for q in range(2):
                put(
                    q, x + 1, size, source[q, x : x + size], sibling[par, q, x : x + size], None
                )

        def border(side):
            there = row > 0 if side == 0 else row < count - 1
            for q in range(2):
                put(
                    q,
                    0 if side == 0 else width + 1,
                    1,
                    edges[par, side, span, q][None],
                    edges[par, side, 0, q][None],
                    there,
                )

        def pixels(k, dy, x, step):
            return active[k, dy, x : x + step].reshape(step * both, channels)

        def lone(k, dt, x, step):
            left, right = [], []
            for dy in range(3):
                left += [pixels(k, dy, x, step + 1), pixels(k, dy, x + 2, step + 1)]
                for taps in ((0, 1), (2, None)):
                    right.append(
                        jnp.concatenate(
                            [
                                tap_block(weights, -1 if dx is None else dt, dy, dx, channels)
                                for dx in taps
                            ],
                            axis=1,
                        )
                    )
            part = jnp.dot(
                jnp.concatenate(left, axis=1),
                jnp.concatenate(right, axis=0),
                preferred_element_type=jnp.float32,
            )
            return part[: step * both, :channels] + part[both:, channels:]

        def products(x, step):
            left, right = [], []
            for dy in range(3):
                for dx in range(3):
                    for k in (1, 2):
                        left.append(pixels(k, dy, x + dx, step))
                        right.append(
                            jnp.concatenate(
                                [tap_block(weights, k - q, dy, dx, channels) for q in range(2)],
                                axis=1,
                            )
                        )
            shared = jnp.dot(
                jnp.concatenate(left, axis=1),
                jnp.concatenate(right, axis=0),
                preferred_element_type=jnp.float32,
            )
            result = [
                shared[:, :channels] + lone(0, 0, x, step),
                shared[:, channels:] + lone(3, 2, x, step),
            ]
            sums = []
            for q in range(2):
                tile = store(
                    q,
                    x,
                    step,
                    result[q].reshape(step, both, channels),
                )
                tile = tile.astype(jnp.float32).reshape(-1, height, channels)
                sums.append((jnp.sum(tile, axis=0), jnp.sum(tile * tile, axis=0)))
            return [sums[0][i] + sums[1][i] for i in range(2)]

        step, piece = width // STEPS, width // PIECES
        ready, partial = 0, None
        border(0)
        for x in range(0, width, step):
            while ready < min(x + step + 1, width):
                columns_at(ready, piece)
                ready += piece
                if ready == width:
                    border(1)
            sums = products(x, step)
            partial = sums if partial is None else [partial[i] + sums[i] for i in range(2)]
        return tuple(partial)

    def store_hidden(q, x, step, tile):
        tile = tile.astype(jnp.bfloat16)
        hidden[q, x : x + step] = tile
        return tile

    def store_values(q, x, step, tile):
        tile = (values[q, x : x + step].astype(jnp.float32) + tile).astype(jnp.bfloat16)
        values[q, x : x + step] = tile
        return tile

    def give(when):
        @pl.when((span == 1) & when)
        def _():
            pl.semaphore_signal(free_sem, inc=1, device_id=at(row, 0), device_id_type=MESH)

    def take(when):
        @pl.when((span == 0) & when)
        def _():
            pl.semaphore_wait(free_sem, 1)

    exchange(0, values, partial)
    for k in range(1, 4):
        param_copy(k, segment ^ k).wait_recv()

    @pl.loop(0, layers)
    def _(layer):
        moves_at("a", 0, layer)
        receive(0, values)
        moves_at("r", 0, layer)
        give(layer > 0)
        moves_at("b", 0, layer)
        partial = layer_half(
            0,
            values,
            small[layer, 0:1],
            small[layer, 1:2],
            kernels.at[2 * layer],
            store_hidden,
        )
        take(layer > 0)
        exchange(1, hidden, partial)
        finish_sends(0, values)
        moves_at("a", 1, layer)
        receive(1, hidden)
        moves_at("r", 1, layer)
        give(layer < layers - 1)
        moves_at("b", 1, layer)
        partial = layer_half(
            1,
            hidden,
            small[layer, 2:3],
            small[layer, 3:4],
            kernels.at[2 * layer + 1],
            store_values,
        )

        @pl.when(layer < layers - 1)
        def _():
            take(layer >= 0)
            exchange(0, values, partial)

        finish_sends(1, hidden)

    for q in range(2):
        whole = values[q].astype(jnp.float32)
        for p in range(2):
            turned[q + 2 * p] = whole[:, p * height : (p + 1) * height].reshape(
                height * width, channels
            )
    def outgoing(k, me, to):
        return pltpu.make_async_remote_copy(
            src_ref=staged.at[:, pl.ds(to * local_rows, local_rows)],
            dst_ref=out.at[0, :, :, pl.ds(pl.multiple_of(me * width, width), width)],
            send_sem=out_send.at[k],
            recv_sem=out_recv.at[me],
            device_id=at(to, span),
            device_id_type=MESH,
        )

    def stage(to):
        for f in range(frames):
            for i in range(local_rows):
                y = to * local_rows + i
                staged[f, y] = turned[f, pl.ds(y, width, stride=height)].astype(jnp.bfloat16)

    for k in range(1, count):
        stage(lax.rem(row + k, count))
        outgoing(k, row, lax.rem(row + k, count)).start()
    stage(row)
    own = pltpu.make_async_copy(
        staged.at[:, pl.ds(row * local_rows, local_rows)],
        out.at[0, :, :, pl.ds(pl.multiple_of(row * width, width), width)],
        own_sem,
    )
    own.start()
    own.wait()
    moves("end")
    for k in range(1, 4):
        param_copy(k, segment).wait_send()
    for k in range(1, count):
        other = lax.rem(row + k, count)
        outgoing(k, other, row).wait_recv()
        outgoing(k, row, other).wait_send()


def body(latents, conv_first, conv_second, gain_first, bias_first, gain_second, bias_second):
    micro, frames, local_rows, columns, channels = latents.shape
    count = lax.axis_size("rows")
    width = columns // count
    height = local_rows * count
    both = 2 * height
    dma = pltpu.SemaphoreType.DMA
    return pl.pallas_call(
        functools.partial(decode_kernel, count),
        out_shape=jax.ShapeDtypeStruct((1, frames, local_rows, columns, channels), jnp.bfloat16),
        in_specs=[pl.BlockSpec(memory_space=pltpu.HBM)] * 7,
        out_specs=pl.BlockSpec(memory_space=pltpu.VMEM),
        scratch_shapes=[
            pltpu.VMEM((frames, height, width, channels), jnp.bfloat16),
            pltpu.VMEM((frames, height * width, channels), jnp.float32),
            pltpu.VMEM((2, width, both, channels), jnp.bfloat16),
            pltpu.VMEM((2, width, both, channels), jnp.bfloat16),
            pltpu.VMEM((2, 2, width, both, channels), jnp.bfloat16),
            pltpu.VMEM((2, 2, 2, 2, both, channels), jnp.bfloat16),
            pltpu.VMEM((2, 2 * count, 8, channels), jnp.float32),
            pltpu.VMEM((4, 3, width + 3, both, channels), jnp.bfloat16),
            dma,
            dma((count,)),
            dma((count,)),
            dma((2, 2 * count)),
            dma((2, 2 * count)),
            dma((2, 2, 2)),
            dma((2, 2, 2)),
            dma((2,)),
            dma((2,)),
            dma((count,)),
            dma((count,)),
            pltpu.SemaphoreType.REGULAR,
            pltpu.VMEM((8,) + conv_first.shape[1:], jnp.bfloat16),
            pltpu.VMEM((4, 8, channels), jnp.float32),
            dma((4,)),
            dma((4,)),
            dma((8,)),
            dma((8, 2, 3)),
            dma((8, 3)),
            dma((8, 3)),
            dma((8, 3)),
            pltpu.VMEM((4, 1, channels), jnp.bfloat16),
            dma((4,)),
        ],
        compiler_params=pltpu.CompilerParams(
            collective_id=0, has_side_effects=True, vmem_limit_bytes=64 * 2**20 - 2**17
        ),
    )(latents, conv_first, conv_second, gain_first, bias_first, gain_second, bias_second)


def solution(mesh):
    in_specs = (
        P(None, "tm", "rows", None, None),
        P("segment", None, None, None, None, None),
        P("segment", None, None, None, None, None),
        P("segment", None),
        P("segment", None),
        P("segment", None),
        P("segment", None),
    )
    out_specs = P("segment", "tm", "rows", None, None)
    sizes = dict(mesh.shape)

    def run(latents, *params):
        micro, frames, height, columns, channels = latents.shape
        count = sizes["rows"]
        fits = (
            micro == sizes["segment"] == 4
            and params[0].shape == (4, 3, 3, 3, channels, channels)
            and count % 2 == 0
            and sizes["tm"] == 2
            and frames == 8
            and height % (8 * 1) == 0
            and columns % (count * ROWS) == 0
            and channels == 4 * GROUPS
        )
        inner = body if fits else plain_body
        return jax.shard_map(
            inner, mesh=mesh, in_specs=in_specs, out_specs=out_specs, check_vma=False
        )(latents, *params)

    return run
```

```python
import functools

import jax
import jax.numpy as jnp
from jax import lax
from jax.experimental import pallas as pl
from jax.experimental.pallas import tpu as pltpu
from jax.sharding import PartitionSpec as P

GROUPS = 32


EPS = 1e-06


def passed_along(value, axis, steps):
    count = lax.axis_size(axis)
    initial, last = (max(0, -steps), min(count, count - steps))
    return lax.ppermute(value, axis, [(source, source + steps) for source in range(initial, last)])


def padded_2(block, sides, width):
    for axis, dim in sides:
        count = lax.axis_size(axis)
        forward = [(i, i + 1) for i in range(count - 1)]
        backward = [(target, source) for source, target in forward]
        low = lax.ppermute(
            lax.slice_in_dim(block, block.shape[dim] - width, None, axis=dim), axis, forward
        )
        high = lax.ppermute(lax.slice_in_dim(block, 0, width, axis=dim), axis, backward)
        block = jnp.concatenate([low, block, high], axis=dim)
    return block


def normalize(values, norm_gain, norm_bias):
    frames, rows_here, columns, channels = values.shape
    width_group = channels // GROUPS
    grouped = values.astype(jnp.float32).reshape(frames, rows_here, columns, GROUPS, width_group)
    totals = lax.psum(
        (jnp.sum(grouped, axis=(0, 1, 2, 4)), jnp.sum(grouped * grouped, axis=(0, 1, 2, 4))), "rows"
    )
    members = frames * rows_here * lax.axis_size("rows") * columns * width_group
    average = totals[0] / members
    squares = totals[1] / members
    inverse = lax.rsqrt(squares - average * average + EPS)
    scaled = (grouped - average[:, None]) * inverse[:, None]
    scaled = scaled.reshape(values.shape) * norm_gain.astype(jnp.float32) + norm_bias.astype(
        jnp.float32
    )
    return jax.nn.silu(scaled).astype(jnp.bfloat16)


def convolve(active, kernel):
    previous = passed_along(active[-2:], "tm", 1)
    extended = jnp.concatenate([previous, active], axis=0)
    padded = padded_2(extended, (("rows", 1),), 1)
    padded = jnp.pad(padded, ((0, 0), (0, 0), (1, 1), (0, 0)))
    result = lax.conv_general_dilated(
        padded[None],
        kernel,
        (1, 1, 1),
        "VALID",
        dimension_numbers=("NDHWC", "DHWIO", "NDHWC"),
        preferred_element_type=jnp.float32,
    )
    return result[0]


def residual_block(values, params):
    first, second, gain_one, bias_one, gain_two, bias_two = params
    active = normalize(values, gain_one, bias_one)
    hidden = convolve(active, first).astype(jnp.bfloat16)
    active = normalize(hidden, gain_two, bias_two)
    return (values.astype(jnp.float32) + convolve(active, second)).astype(jnp.bfloat16)


def plain_body(latents, conv_first, conv_second, gain_first, bias_first, gain_second, bias_second):
    segments = lax.axis_size("segment")
    micro = latents.shape[0]
    per_segment = micro // segments
    position = lax.axis_index("segment")
    small = jnp.stack([gain_first, bias_first, gain_second, bias_second], axis=1)
    small = lax.all_gather(small, "segment", axis=0, tiled=True)
    first = lax.all_gather(conv_first, "segment", axis=0, tiled=True)
    second = lax.all_gather(conv_second, "segment", axis=0, tiled=True)
    outs = []
    for index in range(per_segment):
        values = lax.dynamic_index_in_dim(
            latents, position * per_segment + index, 0, keepdims=False
        )
        for layer in range(first.shape[0]):
            gains = small[layer]
            values = residual_block(
                values, (first[layer], second[layer], gains[0], gains[1], gains[2], gains[3])
            )
        outs.append(values)
    return jnp.stack(outs)


MESH = pl.DeviceIdType.MESH
ROWS = 16
STEPS = 4
PIECES = 4


def group_sums(values):
    lanes = values.shape[-1]
    lane = lax.broadcasted_iota(jnp.int32, values.shape, 1)
    values = values + jnp.where(
        lax.rem(lane, 2) == 0, pltpu.roll(values, lanes - 1, 1), pltpu.roll(values, 1, 1)
    )
    return values + jnp.where(
        lax.rem(lane, 4) < 2, pltpu.roll(values, lanes - 2, 1), pltpu.roll(values, 2, 1)
    )


def tap_block(weights, dt, dy, dx, channels):
    if dt < 0 or dt > 2:
        return jnp.zeros((channels, channels), jnp.bfloat16)
    return weights[dt, dy, dx]


def decode_kernel(
    count,
    latents,
    first,
    second,
    gain_first,
    bias_first,
    gain_second,
    bias_second,
    out,
    staged,
    turned,
    values,
    hidden,
    sibling,
    edges,
    stats,
    active,
    own_sem,
    in_send,
    in_recv,
    stat_send,
    stat_recv,
    edge_send,
    edge_recv,
    sib_send,
    sib_recv,
    out_send,
    out_recv,
    free_sem,
    kernels,
    small,
    param_send,
    param_recv,
    load_sem,
    w_send,
    w_recv,
    half_send,
    half_recv,
    raw_params,
    raw_sem,
):
    frames, height, width, channels = staged.shape
    local_rows = height // count
    both = 2 * height
    row = lax.axis_index("rows")
    segment = lax.axis_index("segment")
    span = lax.axis_index("tm")
    members = frames * height * width * count * (channels // GROUPS)

    def at(rows_index, tm_index):
        return {"rows": rows_index, "tm": tm_index}

    barrier = pltpu.get_barrier_semaphore()
    for k in range(count):
        other = lax.rem(row + k, count)
        if k:
            pl.semaphore_signal(barrier, inc=1, device_id=at(other, span), device_id_type=MESH)
        pl.semaphore_signal(barrier, inc=1, device_id=at(other, 1 - span), device_id_type=MESH)
    for k in range(1, 4):
        pl.semaphore_signal(
            barrier, inc=1, device_id={"segment": segment ^ k}, device_id_type=MESH
        )
    pl.semaphore_wait(barrier, 2 * count + 2)

    given = (first, second)
    layers = kernels.shape[0] // 2
    for k in (0, 3):
        for dy in range(3):
            active[k, dy, width + 2] = jnp.zeros((both, channels), jnp.bfloat16)
    depth = channels // 2

    def tensor_part(ref, half, chunk, chunks):
        rows = pl.ds(pl.multiple_of(half * depth, depth), depth)
        size = 3 // chunks
        return ref.at[pl.ds(chunk * size, size), :, :, rows]

    def chunks_of(j):
        return 3 if j < 4 else 1

    def remote_half(j, chunk, source, to, slot):
        return pltpu.make_async_remote_copy(
            src_ref=tensor_part(source, span, chunk, chunks_of(j)),
            dst_ref=tensor_part(kernels.at[j], span, chunk, chunks_of(j)),
            send_sem=w_send.at[j, slot, chunk],
            recv_sem=w_recv.at[j, chunk],
            device_id={"rows": row ^ 1} if to is None else {"segment": to},
            device_id_type=MESH,
        )

    def core_half(j, chunk, half):
        return pltpu.make_async_remote_copy(
            src_ref=tensor_part(kernels.at[j], half, chunk, chunks_of(j)),
            dst_ref=tensor_part(kernels.at[j], half, chunk, chunks_of(j)),
            send_sem=half_send.at[j, chunk],
            recv_sem=half_recv.at[j, chunk],
            device_id={"tm": 1 - span},
            device_id_type=MESH,
        )

    routes = "ZZVXVVVV"

    def move(name):
        kind, j = name[0], int(name[1])
        route = routes[j]
        away = segment ^ (j // 2)
        source = given[j % 2].at[0]
        each = range(chunks_of(j)) if len(name) == 2 else (int(name[2]),)
        if route == "X":
            first_to = segment ^ 1
            second_to = pass_to = segment ^ 2
            passes = away == 1
        else:
            turn = lax.rem(row + span, 2) if route == "Z" else span
            first_to = segment ^ (1 + turn)
            second_to = pass_to = segment ^ (2 - turn)
            passes = away == 1 + turn
        here = kernels.at[j]
        if kind == "P":

            @pl.when(away == 0)
            def _():
                for c in each:
                    remote_half(j, c, source, first_to, 0).start()

        if kind == "Q":

            @pl.when(away == 0)
            def _():
                for c in each:
                    remote_half(j - 1, c, given[(j - 1) % 2].at[0], first_to, 0).wait_send()
                    remote_half(j, c, source, first_to, 0).start()

        if kind == "S":

            @pl.when(away == 0)
            def _():
                for c in each:
                    remote_half(j, c, source, second_to, 1).start()

        if kind == "F":

            @pl.when(passes)
            def _():
                for c in each:
                    remote_half(j, c, here, pass_to, 0).wait_recv()
                    remote_half(j, c, here, pass_to, 0).start()
                    if route == "Z":
                        remote_half(j, c, here, None, 1).start()
                    core_half(j, c, span).start()

        if kind == "R":

            @pl.when((away > 0) & jnp.logical_not(passes))
            def _():
                for c in each:
                    remote_half(j, c, here, pass_to, 0).wait_recv()
                    core_half(j, c, span).start()

        if kind == "G":

            @pl.when(away > 0)
            def _():
                for c in each:
                    core_half(j, c, 1 - span).wait_recv()

            @pl.when(away == 0)
            def _():
                pltpu.make_async_copy(source, kernels.at[j], load_sem.at[j]).wait()

        if kind == "W":

            @pl.when(away == 0)
            def _():
                for c in each:
                    if j > 0:
                        remote_half(j, c, source, first_to, 0).wait_send()
                    if route != "Z":
                        remote_half(j, c, source, second_to, 1).wait_send()

            @pl.when(passes)
            def _():
                for c in each:
                    remote_half(j, c, here, pass_to, 0).wait_send()
                    if route == "Z":
                        remote_half(j, c, here, None, 1).wait_send()

            @pl.when(away > 0)
            def _():
                for c in each:
                    core_half(j, c, span).wait_send()

    plan = {
        "start": ("P0", "P2", "P4", "P6"),
        "early": ("Q1", "F0"),
        "a0": ("F1", "R0",),
        "r0": ("F2", "S2", "S4"),
        "b0": ("G0",),
        "a1": ("S3", "S6", "F4", "R1"),
        "b1": ("G1",),
        "a2": ("F32", "P5", "R2", "F6",),
        "b2": ("G2",),
        "a3": ("S5", "P7", "R4", "R3"),
        "r3": ("F5",),
        "b3": ("G3",),
        "a4": ("S7", "R6"),
        "b4": ("G4",),
        "a5": ("F7", "R5"),
        "b5": ("G5",),
        "r6": ("R7",),
        "b6": ("G6",),
        "b7": ("G7",),
        "mid": ("P3",),
        "r1": ("F30", "F31",),
        "end": ("W0", "W1", "W2", "W3", "W4", "W5", "W6", "W7"),
    }

    def moves(point):
        for name in plan.get(point, ()):
            move(name)

    def moves_at(letter, which, layer):
        for known in range(layers):
            point = letter + str(2 * known + which)
            if point in plan:

                @pl.when(layer == known)
                def _(point=point):
                    moves(point)

    def incoming(k, me, to):
        return pltpu.make_async_remote_copy(
            src_ref=latents.at[segment, :, :, pl.ds(pl.multiple_of(to * width, width), width)],
            dst_ref=staged.at[:, pl.ds(me * local_rows, local_rows)],
            send_sem=in_send.at[k],
            recv_sem=in_recv.at[me],
            device_id=at(to, span),
            device_id_type=MESH,
        )

    moves("start")
    for k in range(1, count):
        incoming(k, row, lax.rem(row + k, count)).start()
    for j in range(2 * layers):

        @pl.when(segment == j // 2)
        def _(j=j):
            pltpu.make_async_copy(given[j % 2].at[0], kernels.at[j], load_sem.at[j]).start()

    index = lax.broadcasted_iota(jnp.int32, (8, channels), 0)
    raw = [
        pltpu.make_async_copy(ref, raw_params.at[k], raw_sem.at[k])
        for k, ref in enumerate((gain_first, bias_first, gain_second, bias_second))
    ]
    for copy in raw:
        copy.start()
    for copy in raw:
        copy.wait()
    packed = jnp.zeros((8, channels), jnp.float32)
    for k in range(4):
        packed = jnp.where(index == k, raw_params[k].astype(jnp.float32), packed)
    small[segment] = packed

    def param_copy(k, me):
        return pltpu.make_async_remote_copy(
            src_ref=small.at[me],
            dst_ref=small.at[me],
            send_sem=param_send.at[k],
            recv_sem=param_recv.at[me],
            device_id={"segment": segment ^ k},
            device_id_type=MESH,
        )

    for k in range(1, 4):
        param_copy(k, segment).start()
    own = pltpu.make_async_copy(
        latents.at[segment, :, :, pl.ds(pl.multiple_of(row * width, width), width)],
        staged.at[:, pl.ds(row * local_rows, local_rows)],
        own_sem,
    )
    own.start()
    moves("early")
    own.wait()
    for k in range(1, count):
        other = lax.rem(row + k, count)
        incoming(k, other, row).wait_recv()
    moves("mid")

    for f in range(frames):
        turned[f, : height * width] = (
            staged[f].astype(jnp.float32).reshape(height * width, channels)
        )
    zero = jnp.zeros((height, channels), jnp.float32)

    def turn(x, carry):
        total, squares = carry
        for q in range(2):
            tile = jnp.concatenate(
                [turned[q + 2 * p, pl.ds(x, height, stride=width)] for p in range(2)], axis=0
            )
            values[q, x] = tile.astype(jnp.bfloat16)
            total = total + tile[:height] + tile[height:]
            tile = tile * tile
            squares = squares + tile[:height] + tile[height:]
        return total, squares

    partial = lax.fori_loop(0, width, turn, (zero, zero), unroll=4)
    for k in range(1, count):
        incoming(k, row, lax.rem(row + k, count)).wait_send()

    def stat_copy(par, k, me, to, tm_from, tm_to):
        slot = tm_from * count + me
        cross = 0 if tm_from is tm_to else count
        return pltpu.make_async_remote_copy(
            src_ref=stats.at[par, slot],
            dst_ref=stats.at[par, slot],
            send_sem=stat_send.at[par, k + cross],
            recv_sem=stat_recv.at[par, slot],
            device_id=at(to, tm_to),
            device_id_type=MESH,
        )

    def edge_copy(par, source, side, tm_from, tm_to, to):
        return pltpu.make_async_remote_copy(
            src_ref=source.at[:, width - 1 if side == 0 else 0],
            dst_ref=edges.at[par, side, tm_from],
            send_sem=edge_send.at[par, side, tm_to],
            recv_sem=edge_recv.at[par, side, tm_from],
            device_id=at(to, tm_to),
            device_id_type=MESH,
        )

    def sib_copy(par, source):
        return pltpu.make_async_remote_copy(
            src_ref=source,
            dst_ref=sibling.at[par],
            send_sem=sib_send.at[par],
            recv_sem=sib_recv.at[par],
            device_id=at(row, 1),
            device_id_type=MESH,
        )

    def each_send(par, source, act):
        for k in range(1, count):
            act(stat_copy(par, k, row, lax.rem(row + k, count), span, span))

        @pl.when(span == 0)
        def _():
            for k in range(count):
                act(stat_copy(par, k, row, lax.rem(row + k, count), 0, 1))

        for side, there in ((0, row < count - 1), (1, row > 0)):

            @pl.when(there)
            def _(side=side):
                to = row + 1 if side == 0 else row - 1
                act(edge_copy(par, source, side, span, span, to))

                @pl.when(span == 0)
                def _():
                    act(edge_copy(par, source, side, 0, 1, to))

        @pl.when(span == 0)
        def _():
            act(sib_copy(par, source))

    def exchange(par, source, partial):
        index = lax.broadcasted_iota(jnp.int32, (8, channels), 0)
        total = jnp.sum(partial[0], axis=0, keepdims=True)
        squares = jnp.sum(partial[1], axis=0, keepdims=True)
        stats[par, span * count + row] = jnp.where(
            index == 0, total, jnp.where(index == 1, squares, 0.0)
        )
        each_send(par, source, lambda copy: copy.start())

    def finish_sends(par, source):
        each_send(par, source, lambda copy: copy.wait_send())

    def receive(par, source):
        for side, there in ((0, row > 0), (1, row < count - 1)):

            @pl.when(there)
            def _(side=side):
                edge_copy(par, source, side, span, span, row).wait_recv()

                @pl.when(span == 1)
                def _():
                    edge_copy(par, source, side, 0, 1, row).wait_recv()

        @pl.when(span == 1)
        def _():
            sib_copy(par, source).wait_recv()
            for k in range(count):
                stat_copy(par, k, lax.rem(row + k, count), row, 0, 1).wait_recv()

        for k in range(1, count):
            stat_copy(par, k, lax.rem(row + k, count), row, span, span).wait_recv()

    def moments(par, base, gain):
        total = stats[par, base]
        for k in range(1, count):
            total = total + stats[par, base + k]
        total = group_sums(total) / members
        average = total[0:1]
        return average, lax.rsqrt(total[1:2] - average * average + EPS) * gain

    def layer_half(par, source, gain, bias, weights, store):
        mine = moments(par, span * count, gain)
        before = moments(par, 0, gain)
        later = span > 0
        index = lax.broadcasted_iota(jnp.int32, (1, height, channels), 1)

        def silu(tile, moment):
            half = ((tile - moment[0]) * moment[1] + bias) * 0.5
            return half + half * jnp.tanh(half)

        def shifted(a, dy):
            if dy == 0:
                return jnp.where(index == 0, 0.0, pltpu.roll(a, 1, 1))
            if dy == 2:
                return jnp.where(index == height - 1, 0.0, pltpu.roll(a, height - 1, 1))
            return a

        def put(q, x, size, tile, older, valid):
            a = silu(tile.astype(jnp.float32), mine).reshape(2 * size, height, channels)
            b = silu(older.astype(jnp.float32)[:, height:], before)
            b = jnp.where(later, b, 0.0)
            if valid is not None:
                a = jnp.where(valid, a, 0.0)
                b = jnp.where(valid, b, 0.0)
            for dy in range(3):
                now = shifted(a, dy).reshape(size, both, channels)
                old = shifted(b, dy)
                active[2 + q, dy, x : x + size] = now.astype(jnp.bfloat16)
                active[q, dy, x : x + size] = jnp.concatenate(
                    [old, now[:, :height]], axis=1
                ).astype(jnp.bfloat16)

        def columns_at(x, size):
            for q in range(2):
                put(
                    q, x + 1, size, source[q, x : x + size], sibling[par, q, x : x + size], None
                )

        def border(side):
            there = row > 0 if side == 0 else row < count - 1
            for q in range(2):
                put(
                    q,
                    0 if side == 0 else width + 1,
                    1,
                    edges[par, side, span, q][None],
                    edges[par, side, 0, q][None],
                    there,
                )

        def pixels(k, dy, x, step):
            return active[k, dy, x : x + step].reshape(step * both, channels)

        def lone(k, dt, x, step):
            left, right = [], []
            for dy in range(3):
                left += [pixels(k, dy, x, step + 1), pixels(k, dy, x + 2, step + 1)]
                for taps in ((0, 1), (2, None)):
                    right.append(
                        jnp.concatenate(
                            [
                                tap_block(weights, -1 if dx is None else dt, dy, dx, channels)
                                for dx in taps
                            ],
                            axis=1,
                        )
                    )
            part = jnp.dot(
                jnp.concatenate(left, axis=1),
                jnp.concatenate(right, axis=0),
                preferred_element_type=jnp.float32,
            )
            return part[: step * both, :channels] + part[both:, channels:]

        def products(x, step):
            left, right = [], []
            for dy in range(3):
                for dx in range(3):
                    for k in (1, 2):
                        left.append(pixels(k, dy, x + dx, step))
                        right.append(
                            jnp.concatenate(
                                [tap_block(weights, k - q, dy, dx, channels) for q in range(2)],
                                axis=1,
                            )
                        )
            shared = jnp.dot(
                jnp.concatenate(left, axis=1),
                jnp.concatenate(right, axis=0),
                preferred_element_type=jnp.float32,
            )
            result = [
                shared[:, :channels] + lone(0, 0, x, step),
                shared[:, channels:] + lone(3, 2, x, step),
            ]
            sums = []
            for q in range(2):
                tile = store(
                    q,
                    x,
                    step,
                    result[q].reshape(step, both, channels),
                )
                tile = tile.astype(jnp.float32).reshape(-1, height, channels)
                sums.append((jnp.sum(tile, axis=0), jnp.sum(tile * tile, axis=0)))
            return [sums[0][i] + sums[1][i] for i in range(2)]

        step, piece = width // STEPS, width // PIECES
        ready, partial = 0, None
        border(0)
        for x in range(0, width, step):
            while ready < min(x + step + 1, width):
                columns_at(ready, piece)
                ready += piece
                if ready == width:
                    border(1)
            sums = products(x, step)
            partial = sums if partial is None else [partial[i] + sums[i] for i in range(2)]
        return tuple(partial)

    def store_hidden(q, x, step, tile):
        tile = tile.astype(jnp.bfloat16)
        hidden[q, x : x + step] = tile
        return tile

    def store_values(q, x, step, tile):
        tile = (values[q, x : x + step].astype(jnp.float32) + tile).astype(jnp.bfloat16)
        values[q, x : x + step] = tile
        return tile

    def give(when):
        @pl.when((span == 1) & when)
        def _():
            pl.semaphore_signal(free_sem, inc=1, device_id=at(row, 0), device_id_type=MESH)

    def take(when):
        @pl.when((span == 0) & when)
        def _():
            pl.semaphore_wait(free_sem, 1)

    exchange(0, values, partial)
    for k in range(1, 4):
        param_copy(k, segment ^ k).wait_recv()

    @pl.loop(0, layers)
    def _(layer):
        moves_at("a", 0, layer)
        receive(0, values)
        moves_at("r", 0, layer)
        give(layer > 0)
        moves_at("b", 0, layer)
        partial = layer_half(
            0,
            values,
            small[layer, 0:1],
            small[layer, 1:2],
            kernels.at[2 * layer],
            store_hidden,
        )
        take(layer > 0)
        exchange(1, hidden, partial)
        finish_sends(0, values)
        moves_at("a", 1, layer)
        receive(1, hidden)
        moves_at("r", 1, layer)
        give(layer < layers - 1)
        moves_at("b", 1, layer)
        partial = layer_half(
            1,
            hidden,
            small[layer, 2:3],
            small[layer, 3:4],
            kernels.at[2 * layer + 1],
            store_values,
        )

        @pl.when(layer < layers - 1)
        def _():
            take(layer >= 0)
            exchange(0, values, partial)

        finish_sends(1, hidden)

    for q in range(2):
        whole = values[q].astype(jnp.float32)
        for p in range(2):
            turned[q + 2 * p, : height * width] = whole[
                :, p * height : (p + 1) * height
            ].reshape(height * width, channels)
    def outgoing(k, me, to):
        return pltpu.make_async_remote_copy(
            src_ref=staged.at[:, pl.ds(to * local_rows, local_rows)],
            dst_ref=out.at[0, :, :, pl.ds(pl.multiple_of(me * width, width), width)],
            send_sem=out_send.at[k],
            recv_sem=out_recv.at[me],
            device_id=at(to, span),
            device_id_type=MESH,
        )

    def stage(to):
        for f in range(frames):
            for i in range(local_rows):
                y = to * local_rows + i
                staged[f, y] = turned[f, pl.ds(y, width, stride=height)].astype(jnp.bfloat16)

    for k in range(1, count):
        stage(lax.rem(row + k, count))
        outgoing(k, row, lax.rem(row + k, count)).start()
    stage(row)
    own = pltpu.make_async_copy(
        staged.at[:, pl.ds(row * local_rows, local_rows)],
        out.at[0, :, :, pl.ds(pl.multiple_of(row * width, width), width)],
        own_sem,
    )
    own.start()
    own.wait()
    moves("end")
    for k in range(1, 4):
        param_copy(k, segment).wait_send()
    for k in range(1, count):
        other = lax.rem(row + k, count)
        outgoing(k, other, row).wait_recv()
        outgoing(k, row, other).wait_send()


def body(latents, conv_first, conv_second, gain_first, bias_first, gain_second, bias_second):
    micro, frames, local_rows, columns, channels = latents.shape
    count = lax.axis_size("rows")
    width = columns // count
    height = local_rows * count
    both = 2 * height
    dma = pltpu.SemaphoreType.DMA
    return pl.pallas_call(
        functools.partial(decode_kernel, count),
        out_shape=jax.ShapeDtypeStruct((1, frames, local_rows, columns, channels), jnp.bfloat16),
        in_specs=[pl.BlockSpec(memory_space=pltpu.HBM)] * 7,
        out_specs=pl.BlockSpec(memory_space=pltpu.VMEM),
        scratch_shapes=[
            pltpu.VMEM((frames, height, width, channels), jnp.bfloat16),
            pltpu.VMEM((frames, height * width + height + width, channels), jnp.float32),
            pltpu.VMEM((2, width, both, channels), jnp.bfloat16),
            pltpu.VMEM((2, width, both, channels), jnp.bfloat16),
            pltpu.VMEM((2, 2, width, both, channels), jnp.bfloat16),
            pltpu.VMEM((2, 2, 2, 2, both, channels), jnp.bfloat16),
            pltpu.VMEM((2, 2 * count, 8, channels), jnp.float32),
            pltpu.VMEM((4, 3, width + 3, both, channels), jnp.bfloat16),
            dma,
            dma((count,)),
            dma((count,)),
            dma((2, 2 * count)),
            dma((2, 2 * count)),
            dma((2, 2, 2)),
            dma((2, 2, 2)),
            dma((2,)),
            dma((2,)),
            dma((count,)),
            dma((count,)),
            pltpu.SemaphoreType.REGULAR,
            pltpu.VMEM((8,) + conv_first.shape[1:], jnp.bfloat16),
            pltpu.VMEM((4, 8, channels), jnp.float32),
            dma((4,)),
            dma((4,)),
            dma((8,)),
            dma((8, 2, 3)),
            dma((8, 3)),
            dma((8, 3)),
            dma((8, 3)),
            pltpu.VMEM((4, 1, channels), jnp.bfloat16),
            dma((4,)),
        ],
        compiler_params=pltpu.CompilerParams(
            collective_id=0, has_side_effects=True, vmem_limit_bytes=64 * 2**20 - 2**17
        ),
    )(latents, conv_first, conv_second, gain_first, bias_first, gain_second, bias_second)


def solution(mesh):
    in_specs = (
        P(None, "tm", "rows", None, None),
        P("segment", None, None, None, None, None),
        P("segment", None, None, None, None, None),
        P("segment", None),
        P("segment", None),
        P("segment", None),
        P("segment", None),
    )
    out_specs = P("segment", "tm", "rows", None, None)
    sizes = dict(mesh.shape)

    def run(latents, *params):
        micro, frames, height, columns, channels = latents.shape
        count = sizes["rows"]
        fits = (
            micro == sizes["segment"] == 4
            and params[0].shape == (4, 3, 3, 3, channels, channels)
            and count % 2 == 0
            and sizes["tm"] == 2
            and frames == 8
            and height % (8 * 1) == 0
            and columns % (count * ROWS) == 0
            and channels == 4 * GROUPS
        )
        inner = body if fits else plain_body
        return jax.shard_map(
            inner, mesh=mesh, in_specs=in_specs, out_specs=out_specs, check_vma=False
        )(latents, *params)

    return run
```

```python
import functools

import jax
import jax.numpy as jnp
from jax import lax
from jax.experimental import pallas as pl
from jax.experimental.pallas import tpu as pltpu
from jax.sharding import PartitionSpec as P

GROUPS = 32


EPS = 1e-06


def passed_along(value, axis, steps):
    count = lax.axis_size(axis)
    initial, last = (max(0, -steps), min(count, count - steps))
    return lax.ppermute(value, axis, [(source, source + steps) for source in range(initial, last)])


def padded_2(block, sides, width):
    for axis, dim in sides:
        count = lax.axis_size(axis)
        forward = [(i, i + 1) for i in range(count - 1)]
        backward = [(target, source) for source, target in forward]
        low = lax.ppermute(
            lax.slice_in_dim(block, block.shape[dim] - width, None, axis=dim), axis, forward
        )
        high = lax.ppermute(lax.slice_in_dim(block, 0, width, axis=dim), axis, backward)
        block = jnp.concatenate([low, block, high], axis=dim)
    return block


def normalize(values, norm_gain, norm_bias):
    frames, rows_here, columns, channels = values.shape
    width_group = channels // GROUPS
    grouped = values.astype(jnp.float32).reshape(frames, rows_here, columns, GROUPS, width_group)
    totals = lax.psum(
        (jnp.sum(grouped, axis=(0, 1, 2, 4)), jnp.sum(grouped * grouped, axis=(0, 1, 2, 4))), "rows"
    )
    members = frames * rows_here * lax.axis_size("rows") * columns * width_group
    average = totals[0] / members
    squares = totals[1] / members
    inverse = lax.rsqrt(squares - average * average + EPS)
    scaled = (grouped - average[:, None]) * inverse[:, None]
    scaled = scaled.reshape(values.shape) * norm_gain.astype(jnp.float32) + norm_bias.astype(
        jnp.float32
    )
    return jax.nn.silu(scaled).astype(jnp.bfloat16)


def convolve(active, kernel):
    previous = passed_along(active[-2:], "tm", 1)
    extended = jnp.concatenate([previous, active], axis=0)
    padded = padded_2(extended, (("rows", 1),), 1)
    padded = jnp.pad(padded, ((0, 0), (0, 0), (1, 1), (0, 0)))
    result = lax.conv_general_dilated(
        padded[None],
        kernel,
        (1, 1, 1),
        "VALID",
        dimension_numbers=("NDHWC", "DHWIO", "NDHWC"),
        preferred_element_type=jnp.float32,
    )
    return result[0]


def residual_block(values, params):
    first, second, gain_one, bias_one, gain_two, bias_two = params
    active = normalize(values, gain_one, bias_one)
    hidden = convolve(active, first).astype(jnp.bfloat16)
    active = normalize(hidden, gain_two, bias_two)
    return (values.astype(jnp.float32) + convolve(active, second)).astype(jnp.bfloat16)


def plain_body(latents, conv_first, conv_second, gain_first, bias_first, gain_second, bias_second):
    segments = lax.axis_size("segment")
    micro = latents.shape[0]
    per_segment = micro // segments
    position = lax.axis_index("segment")
    small = jnp.stack([gain_first, bias_first, gain_second, bias_second], axis=1)
    small = lax.all_gather(small, "segment", axis=0, tiled=True)
    first = lax.all_gather(conv_first, "segment", axis=0, tiled=True)
    second = lax.all_gather(conv_second, "segment", axis=0, tiled=True)
    outs = []
    for index in range(per_segment):
        values = lax.dynamic_index_in_dim(
            latents, position * per_segment + index, 0, keepdims=False
        )
        for layer in range(first.shape[0]):
            gains = small[layer]
            values = residual_block(
                values, (first[layer], second[layer], gains[0], gains[1], gains[2], gains[3])
            )
        outs.append(values)
    return jnp.stack(outs)


MESH = pl.DeviceIdType.MESH
ROWS = 16
STEPS = 4
PIECES = 4


def group_sums(values):
    lanes = values.shape[-1]
    lane = lax.broadcasted_iota(jnp.int32, values.shape, 1)
    values = values + jnp.where(
        lax.rem(lane, 2) == 0, pltpu.roll(values, lanes - 1, 1), pltpu.roll(values, 1, 1)
    )
    return values + jnp.where(
        lax.rem(lane, 4) < 2, pltpu.roll(values, lanes - 2, 1), pltpu.roll(values, 2, 1)
    )


def tap_block(weights, dt, dy, dx, channels):
    if dt < 0 or dt > 2:
        return jnp.zeros((channels, channels), jnp.bfloat16)
    return weights[dt, dy, dx]


def decode_kernel(
    count,
    latents,
    first,
    second,
    gain_first,
    bias_first,
    gain_second,
    bias_second,
    out,
    staged,
    turned,
    values,
    hidden,
    sibling,
    edges,
    stats,
    active,
    own_sem,
    in_send,
    in_recv,
    stat_send,
    stat_recv,
    edge_send,
    edge_recv,
    sib_send,
    sib_recv,
    out_send,
    out_recv,
    free_sem,
    kernels,
    small,
    param_send,
    param_recv,
    load_sem,
    w_send,
    w_recv,
    half_send,
    half_recv,
    raw_params,
    raw_sem,
):
    frames, height, width, channels = staged.shape
    local_rows = height // count
    both = 2 * height
    row = lax.axis_index("rows")
    segment = lax.axis_index("segment")
    span = lax.axis_index("tm")
    members = frames * height * width * count * (channels // GROUPS)

    def at(rows_index, tm_index):
        return {"rows": rows_index, "tm": tm_index}

    barrier = pltpu.get_barrier_semaphore()
    for k in range(count):
        other = lax.rem(row + k, count)
        if k:
            pl.semaphore_signal(barrier, inc=1, device_id=at(other, span), device_id_type=MESH)
        pl.semaphore_signal(barrier, inc=1, device_id=at(other, 1 - span), device_id_type=MESH)
    for k in range(1, 4):
        pl.semaphore_signal(
            barrier, inc=1, device_id={"segment": segment ^ k}, device_id_type=MESH
        )
    pl.semaphore_wait(barrier, 2 * count + 2)

    given = (first, second)
    layers = kernels.shape[0] // 2
    for k in (0, 3):
        for dy in range(3):
            active[k, dy, width + 2] = jnp.zeros((both, channels), jnp.bfloat16)
    depth = channels // 2

    def tensor_part(ref, half, chunk, chunks):
        rows = pl.ds(pl.multiple_of(half * depth, depth), depth)
        size = 3 // chunks
        return ref.at[pl.ds(chunk * size, size), :, :, rows]

    def chunks_of(j):
        return 3 if j < 4 else 1

    def remote_half(j, chunk, source, to, slot):
        return pltpu.make_async_remote_copy(
            src_ref=tensor_part(source, span, chunk, chunks_of(j)),
            dst_ref=tensor_part(kernels.at[j], span, chunk, chunks_of(j)),
            send_sem=w_send.at[j, slot, chunk],
            recv_sem=w_recv.at[j, chunk],
            device_id={"rows": row ^ 1} if to is None else {"segment": to},
            device_id_type=MESH,
        )

    def core_half(j, chunk, half):
        return pltpu.make_async_remote_copy(
            src_ref=tensor_part(kernels.at[j], half, chunk, chunks_of(j)),
            dst_ref=tensor_part(kernels.at[j], half, chunk, chunks_of(j)),
            send_sem=half_send.at[j, chunk],
            recv_sem=half_recv.at[j, chunk],
            device_id={"tm": 1 - span},
            device_id_type=MESH,
        )

    routes = "ZZVXVVVV"

    def move(name):
        kind, j = name[0], int(name[1])
        route = routes[j]
        away = segment ^ (j // 2)
        source = given[j % 2].at[0]
        each = range(chunks_of(j)) if len(name) == 2 else (int(name[2]),)
        if route == "X":
            first_to = segment ^ 1
            second_to = pass_to = segment ^ 2
            passes = away == 1
        else:
            turn = lax.rem(row + span, 2) if route == "Z" else span
            first_to = segment ^ (1 + turn)
            second_to = pass_to = segment ^ (2 - turn)
            passes = away == 1 + turn
        here = kernels.at[j]
        if kind == "P":

            @pl.when(away == 0)
            def _():
                for c in each:
                    remote_half(j, c, source, first_to, 0).start()

        if kind == "Q":

            @pl.when(away == 0)
            def _():
                for c in each:
                    remote_half(j - 1, c, given[(j - 1) % 2].at[0], first_to, 0).wait_send()
                    remote_half(j, c, source, first_to, 0).start()

        if kind == "S":

            @pl.when(away == 0)
            def _():
                for c in each:
                    remote_half(j, c, source, second_to, 1).start()

        if kind == "F":

            @pl.when(passes)
            def _():
                for c in each:
                    remote_half(j, c, here, pass_to, 0).wait_recv()
                    remote_half(j, c, here, pass_to, 0).start()
                    if route == "Z":
                        remote_half(j, c, here, None, 1).start()
                    core_half(j, c, span).start()

        if kind == "R":

            @pl.when((away > 0) & jnp.logical_not(passes))
            def _():
                for c in each:
                    remote_half(j, c, here, pass_to, 0).wait_recv()
                    core_half(j, c, span).start()

        if kind == "G":

            @pl.when(away > 0)
            def _():
                for c in each:
                    core_half(j, c, 1 - span).wait_recv()

            @pl.when(away == 0)
            def _():
                pltpu.make_async_copy(source, kernels.at[j], load_sem.at[j]).wait()

        if kind == "W":

            @pl.when(away == 0)
            def _():
                for c in each:
                    if j > 0:
                        remote_half(j, c, source, first_to, 0).wait_send()
                    if route != "Z":
                        remote_half(j, c, source, second_to, 1).wait_send()

            @pl.when(passes)
            def _():
                for c in each:
                    remote_half(j, c, here, pass_to, 0).wait_send()
                    if route == "Z":
                        remote_half(j, c, here, None, 1).wait_send()

            @pl.when(away > 0)
            def _():
                for c in each:
                    core_half(j, c, span).wait_send()

    plan = {
        "start": ("P0", "P2", "P4", "P6"),
        "early": ("Q1", "F0"),
        "a0": ("F1", "R0",),
        "r0": ("F2", "S2", "S4"),
        "b0": ("G0",),
        "a1": ("S3", "F4", "F30", "R1",),
        "b1": ("G1",),
        "a2": ("F32", "P5", "R2", "F6",),
        "b2": ("G2",),
        "a3": ("S5", "P7", "R4", "R3"),
        "r3": ("F5",),
        "b3": ("G3",),
        "a4": ("S7", "R6"),
        "b4": ("G4",),
        "a5": ("F7", "R5"),
        "b5": ("G5",),
        "r6": ("R7",),
        "b6": ("G6",),
        "b7": ("G7",),
        "mid": ("P3",),
        "r1": ("S6", "F31",),
        "end": ("W0", "W1", "W2", "W3", "W4", "W5", "W6", "W7"),
    }

    def moves(point):
        for name in plan.get(point, ()):
            move(name)

    def moves_at(letter, which, layer):
        for known in range(layers):
            point = letter + str(2 * known + which)
            if point in plan:

                @pl.when(layer == known)
                def _(point=point):
                    moves(point)

    def incoming(k, me, to):
        return pltpu.make_async_remote_copy(
            src_ref=latents.at[segment, :, :, pl.ds(pl.multiple_of(to * width, width), width)],
            dst_ref=staged.at[:, pl.ds(me * local_rows, local_rows)],
            send_sem=in_send.at[k],
            recv_sem=in_recv.at[me],
            device_id=at(to, span),
            device_id_type=MESH,
        )

    moves("start")
    for k in range(1, count):
        incoming(k, row, lax.rem(row + k, count)).start()
    for j in range(2 * layers):

        @pl.when(segment == j // 2)
        def _(j=j):
            pltpu.make_async_copy(given[j % 2].at[0], kernels.at[j], load_sem.at[j]).start()

    index = lax.broadcasted_iota(jnp.int32, (8, channels), 0)
    raw = [
        pltpu.make_async_copy(ref, raw_params.at[k], raw_sem.at[k])
        for k, ref in enumerate((gain_first, bias_first, gain_second, bias_second))
    ]
    for copy in raw:
        copy.start()
    for copy in raw:
        copy.wait()
    packed = jnp.zeros((8, channels), jnp.float32)
    for k in range(4):
        packed = jnp.where(index == k, raw_params[k].astype(jnp.float32), packed)
    small[segment] = packed

    def param_copy(k, me):
        return pltpu.make_async_remote_copy(
            src_ref=small.at[me],
            dst_ref=small.at[me],
            send_sem=param_send.at[k],
            recv_sem=param_recv.at[me],
            device_id={"segment": segment ^ k},
            device_id_type=MESH,
        )

    for k in range(1, 4):
        param_copy(k, segment).start()
    own = pltpu.make_async_copy(
        latents.at[segment, :, :, pl.ds(pl.multiple_of(row * width, width), width)],
        staged.at[:, pl.ds(row * local_rows, local_rows)],
        own_sem,
    )
    own.start()
    moves("early")
    own.wait()
    for k in range(1, count):
        other = lax.rem(row + k, count)
        incoming(k, other, row).wait_recv()
    moves("mid")

    for f in range(frames):
        turned[f, : height * width] = (
            staged[f].astype(jnp.float32).reshape(height * width, channels)
        )
    zero = jnp.zeros((height, channels), jnp.float32)

    def turn(x, carry):
        total, squares = carry
        for q in range(2):
            tile = jnp.concatenate(
                [turned[q + 2 * p, pl.ds(x, height, stride=width)] for p in range(2)], axis=0
            )
            values[q, x] = tile.astype(jnp.bfloat16)
            total = total + tile[:height] + tile[height:]
            tile = tile * tile
            squares = squares + tile[:height] + tile[height:]
        return total, squares

    partial = lax.fori_loop(0, width, turn, (zero, zero), unroll=16)

    def stat_copy(par, k, me, to, tm_from, tm_to):
        slot = tm_from * count + me
        cross = 0 if tm_from is tm_to else count
        return pltpu.make_async_remote_copy(
            src_ref=stats.at[par, slot],
            dst_ref=stats.at[par, slot],
            send_sem=stat_send.at[par, k + cross],
            recv_sem=stat_recv.at[par, slot],
            device_id=at(to, tm_to),
            device_id_type=MESH,
        )

    def edge_copy(par, source, side, tm_from, tm_to, to):
        return pltpu.make_async_remote_copy(
            src_ref=source.at[:, width - 1 if side == 0 else 0],
            dst_ref=edges.at[par, side, tm_from],
            send_sem=edge_send.at[par, side, tm_to],
            recv_sem=edge_recv.at[par, side, tm_from],
            device_id=at(to, tm_to),
            device_id_type=MESH,
        )

    def sib_copy(par, source):
        return pltpu.make_async_remote_copy(
            src_ref=source,
            dst_ref=sibling.at[par],
            send_sem=sib_send.at[par],
            recv_sem=sib_recv.at[par],
            device_id=at(row, 1),
            device_id_type=MESH,
        )

    def each_send(par, source, act):
        for k in range(1, count):
            act(stat_copy(par, k, row, lax.rem(row + k, count), span, span))

        @pl.when(span == 0)
        def _():
            for k in range(count):
                act(stat_copy(par, k, row, lax.rem(row + k, count), 0, 1))

        for side, there in ((0, row < count - 1), (1, row > 0)):

            @pl.when(there)
            def _(side=side):
                to = row + 1 if side == 0 else row - 1
                act(edge_copy(par, source, side, span, span, to))

                @pl.when(span == 0)
                def _():
                    act(edge_copy(par, source, side, 0, 1, to))

        @pl.when(span == 0)
        def _():
            act(sib_copy(par, source))

    def exchange(par, source, partial):
        index = lax.broadcasted_iota(jnp.int32, (8, channels), 0)
        total = jnp.sum(partial[0], axis=0, keepdims=True)
        squares = jnp.sum(partial[1], axis=0, keepdims=True)
        stats[par, span * count + row] = jnp.where(
            index == 0, total, jnp.where(index == 1, squares, 0.0)
        )
        each_send(par, source, lambda copy: copy.start())

    def finish_sends(par, source):
        each_send(par, source, lambda copy: copy.wait_send())

    def receive(par, source):
        for side, there in ((0, row > 0), (1, row < count - 1)):

            @pl.when(there)
            def _(side=side):
                edge_copy(par, source, side, span, span, row).wait_recv()

                @pl.when(span == 1)
                def _():
                    edge_copy(par, source, side, 0, 1, row).wait_recv()

        @pl.when(span == 1)
        def _():
            sib_copy(par, source).wait_recv()
            for k in range(count):
                stat_copy(par, k, lax.rem(row + k, count), row, 0, 1).wait_recv()

        for k in range(1, count):
            stat_copy(par, k, lax.rem(row + k, count), row, span, span).wait_recv()

    def moments(par, base, gain):
        total = stats[par, base]
        for k in range(1, count):
            total = total + stats[par, base + k]
        total = group_sums(total) / members
        average = total[0:1]
        return average, lax.rsqrt(total[1:2] - average * average + EPS) * gain

    def layer_half(par, source, gain, bias, weights, store):
        mine = moments(par, span * count, gain)
        before = moments(par, 0, gain)
        later = span > 0
        index = lax.broadcasted_iota(jnp.int32, (1, height, channels), 1)

        def silu(tile, moment):
            half = ((tile - moment[0]) * moment[1] + bias) * 0.5
            return half + half * jnp.tanh(half)

        def shifted(a, dy):
            if dy == 0:
                return jnp.where(index == 0, 0.0, pltpu.roll(a, 1, 1))
            if dy == 2:
                return jnp.where(index == height - 1, 0.0, pltpu.roll(a, height - 1, 1))
            return a

        def put(q, x, size, tile, older, valid):
            a = silu(tile.astype(jnp.float32), mine).reshape(2 * size, height, channels)
            b = silu(older.astype(jnp.float32)[:, height:], before)
            b = jnp.where(later, b, 0.0)
            if valid is not None:
                a = jnp.where(valid, a, 0.0)
                b = jnp.where(valid, b, 0.0)
            for dy in range(3):
                now = shifted(a, dy).reshape(size, both, channels)
                old = shifted(b, dy)
                active[2 + q, dy, x : x + size] = now.astype(jnp.bfloat16)
                active[q, dy, x : x + size] = jnp.concatenate(
                    [old, now[:, :height]], axis=1
                ).astype(jnp.bfloat16)

        def columns_at(x, size):
            for q in range(2):
                put(
                    q, x + 1, size, source[q, x : x + size], sibling[par, q, x : x + size], None
                )

        def border(side):
            there = row > 0 if side == 0 else row < count - 1
            for q in range(2):
                put(
                    q,
                    0 if side == 0 else width + 1,
                    1,
                    edges[par, side, span, q][None],
                    edges[par, side, 0, q][None],
                    there,
                )

        def pixels(k, dy, x, step):
            return active[k, dy, x : x + step].reshape(step * both, channels)

        def lone(k, dt, x, step):
            left, right = [], []
            for dy in range(3):
                left += [pixels(k, dy, x, step + 1), pixels(k, dy, x + 2, step + 1)]
                for taps in ((0, 1), (2, None)):
                    right.append(
                        jnp.concatenate(
                            [
                                tap_block(weights, -1 if dx is None else dt, dy, dx, channels)
                                for dx in taps
                            ],
                            axis=1,
                        )
                    )
            part = jnp.dot(
                jnp.concatenate(left, axis=1),
                jnp.concatenate(right, axis=0),
                preferred_element_type=jnp.float32,
            )
            return part[: step * both, :channels] + part[both:, channels:]

        def products(x, step):
            left, right = [], []
            for dy in range(3):
                for dx in range(3):
                    for k in (1, 2):
                        left.append(pixels(k, dy, x + dx, step))
                        right.append(
                            jnp.concatenate(
                                [tap_block(weights, k - q, dy, dx, channels) for q in range(2)],
                                axis=1,
                            )
                        )
            shared = jnp.dot(
                jnp.concatenate(left, axis=1),
                jnp.concatenate(right, axis=0),
                preferred_element_type=jnp.float32,
            )
            result = [
                shared[:, :channels] + lone(0, 0, x, step),
                shared[:, channels:] + lone(3, 2, x, step),
            ]
            sums = []
            for q in range(2):
                tile = store(
                    q,
                    x,
                    step,
                    result[q].reshape(step, both, channels),
                )
                tile = tile.astype(jnp.float32).reshape(-1, height, channels)
                sums.append((jnp.sum(tile, axis=0), jnp.sum(tile * tile, axis=0)))
            return [sums[0][i] + sums[1][i] for i in range(2)]

        step, piece = width // STEPS, width // PIECES
        ready, partial = 0, None
        border(0)
        for x in range(0, width, step):
            while ready < min(x + step + 1, width):
                columns_at(ready, piece)
                ready += piece
                if ready == width:
                    border(1)
            sums = products(x, step)
            partial = sums if partial is None else [partial[i] + sums[i] for i in range(2)]
        return tuple(partial)

    def store_hidden(q, x, step, tile):
        tile = tile.astype(jnp.bfloat16)
        hidden[q, x : x + step] = tile
        return tile

    def store_values(q, x, step, tile):
        tile = (values[q, x : x + step].astype(jnp.float32) + tile).astype(jnp.bfloat16)
        values[q, x : x + step] = tile
        return tile

    def give(when):
        @pl.when((span == 1) & when)
        def _():
            pl.semaphore_signal(free_sem, inc=1, device_id=at(row, 0), device_id_type=MESH)

    def take(when):
        @pl.when((span == 0) & when)
        def _():
            pl.semaphore_wait(free_sem, 1)

    exchange(0, values, partial)
    for k in range(1, count):
        incoming(k, row, lax.rem(row + k, count)).wait_send()
    for k in range(1, 4):
        param_copy(k, segment ^ k).wait_recv()

    @pl.loop(0, layers)
    def _(layer):
        moves_at("a", 0, layer)
        receive(0, values)
        moves_at("r", 0, layer)
        give(layer > 0)
        moves_at("b", 0, layer)
        partial = layer_half(
            0,
            values,
            small[layer, 0:1],
            small[layer, 1:2],
            kernels.at[2 * layer],
            store_hidden,
        )
        take(layer > 0)
        exchange(1, hidden, partial)
        finish_sends(0, values)
        moves_at("a", 1, layer)
        receive(1, hidden)
        moves_at("r", 1, layer)
        give(layer < layers - 1)
        moves_at("b", 1, layer)
        partial = layer_half(
            1,
            hidden,
            small[layer, 2:3],
            small[layer, 3:4],
            kernels.at[2 * layer + 1],
            store_values,
        )

        @pl.when(layer < layers - 1)
        def _():
            take(layer >= 0)
            exchange(0, values, partial)

        finish_sends(1, hidden)

    for q in range(2):
        whole = values[q].astype(jnp.float32)
        for p in range(2):
            turned[q + 2 * p, : height * width] = whole[
                :, p * height : (p + 1) * height
            ].reshape(height * width, channels)
    def outgoing(k, me, to):
        return pltpu.make_async_remote_copy(
            src_ref=staged.at[:, pl.ds(to * local_rows, local_rows)],
            dst_ref=out.at[0, :, :, pl.ds(pl.multiple_of(me * width, width), width)],
            send_sem=out_send.at[k],
            recv_sem=out_recv.at[me],
            device_id=at(to, span),
            device_id_type=MESH,
        )

    def stage(to):
        for f in range(frames):
            for i in range(local_rows):
                y = to * local_rows + i
                staged[f, y] = turned[f, pl.ds(y, width, stride=height)].astype(jnp.bfloat16)

    for k in range(1, count):
        stage(lax.rem(row + k, count))
        outgoing(k, row, lax.rem(row + k, count)).start()
    stage(row)
    own = pltpu.make_async_copy(
        staged.at[:, pl.ds(row * local_rows, local_rows)],
        out.at[0, :, :, pl.ds(pl.multiple_of(row * width, width), width)],
        own_sem,
    )
    own.start()
    own.wait()
    moves("end")
    for k in range(1, 4):
        param_copy(k, segment).wait_send()
    for k in range(1, count):
        other = lax.rem(row + k, count)
        outgoing(k, other, row).wait_recv()
        outgoing(k, row, other).wait_send()


def body(latents, conv_first, conv_second, gain_first, bias_first, gain_second, bias_second):
    micro, frames, local_rows, columns, channels = latents.shape
    count = lax.axis_size("rows")
    width = columns // count
    height = local_rows * count
    both = 2 * height
    dma = pltpu.SemaphoreType.DMA
    return pl.pallas_call(
        functools.partial(decode_kernel, count),
        out_shape=jax.ShapeDtypeStruct((1, frames, local_rows, columns, channels), jnp.bfloat16),
        in_specs=[pl.BlockSpec(memory_space=pltpu.HBM)] * 7,
        out_specs=pl.BlockSpec(memory_space=pltpu.VMEM),
        scratch_shapes=[
            pltpu.VMEM((frames, height, width, channels), jnp.bfloat16),
            pltpu.VMEM((frames, height * width + height + width, channels), jnp.float32),
            pltpu.VMEM((2, width, both, channels), jnp.bfloat16),
            pltpu.VMEM((2, width, both, channels), jnp.bfloat16),
            pltpu.VMEM((2, 2, width, both, channels), jnp.bfloat16),
            pltpu.VMEM((2, 2, 2, 2, both, channels), jnp.bfloat16),
            pltpu.VMEM((2, 2 * count, 8, channels), jnp.float32),
            pltpu.VMEM((4, 3, width + 3, both, channels), jnp.bfloat16),
            dma,
            dma((count,)),
            dma((count,)),
            dma((2, 2 * count)),
            dma((2, 2 * count)),
            dma((2, 2, 2)),
            dma((2, 2, 2)),
            dma((2,)),
            dma((2,)),
            dma((count,)),
            dma((count,)),
            pltpu.SemaphoreType.REGULAR,
            pltpu.VMEM((8,) + conv_first.shape[1:], jnp.bfloat16),
            pltpu.VMEM((4, 8, channels), jnp.float32),
            dma((4,)),
            dma((4,)),
            dma((8,)),
            dma((8, 2, 3)),
            dma((8, 3)),
            dma((8, 3)),
            dma((8, 3)),
            pltpu.VMEM((4, 1, channels), jnp.bfloat16),
            dma((4,)),
        ],
        compiler_params=pltpu.CompilerParams(
            collective_id=0, has_side_effects=True, vmem_limit_bytes=64 * 2**20 - 2**17
        ),
    )(latents, conv_first, conv_second, gain_first, bias_first, gain_second, bias_second)


def solution(mesh):
    in_specs = (
        P(None, "tm", "rows", None, None),
        P("segment", None, None, None, None, None),
        P("segment", None, None, None, None, None),
        P("segment", None),
        P("segment", None),
        P("segment", None),
        P("segment", None),
    )
    out_specs = P("segment", "tm", "rows", None, None)
    sizes = dict(mesh.shape)

    def run(latents, *params):
        micro, frames, height, columns, channels = latents.shape
        count = sizes["rows"]
        fits = (
            micro == sizes["segment"] == 4
            and params[0].shape == (4, 3, 3, 3, channels, channels)
            and count % 2 == 0
            and sizes["tm"] == 2
            and frames == 8
            and height % (8 * 1) == 0
            and columns % (count * ROWS) == 0
            and channels == 4 * GROUPS
        )
        inner = body if fits else plain_body
        return jax.shard_map(
            inner, mesh=mesh, in_specs=in_specs, out_specs=out_specs, check_vma=False
        )(latents, *params)

    return run
```

```python
import functools

import jax
import jax.numpy as jnp
from jax import lax
from jax.experimental import pallas as pl
from jax.experimental.pallas import tpu as pltpu
from jax.sharding import PartitionSpec as P

GROUPS = 32


EPS = 1e-06


def passed_along(value, axis, steps):
    count = lax.axis_size(axis)
    initial, last = (max(0, -steps), min(count, count - steps))
    return lax.ppermute(value, axis, [(source, source + steps) for source in range(initial, last)])


def padded_2(block, sides, width):
    for axis, dim in sides:
        count = lax.axis_size(axis)
        forward = [(i, i + 1) for i in range(count - 1)]
        backward = [(target, source) for source, target in forward]
        low = lax.ppermute(
            lax.slice_in_dim(block, block.shape[dim] - width, None, axis=dim), axis, forward
        )
        high = lax.ppermute(lax.slice_in_dim(block, 0, width, axis=dim), axis, backward)
        block = jnp.concatenate([low, block, high], axis=dim)
    return block


def normalize(values, norm_gain, norm_bias):
    frames, rows_here, columns, channels = values.shape
    width_group = channels // GROUPS
    grouped = values.astype(jnp.float32).reshape(frames, rows_here, columns, GROUPS, width_group)
    totals = lax.psum(
        (jnp.sum(grouped, axis=(0, 1, 2, 4)), jnp.sum(grouped * grouped, axis=(0, 1, 2, 4))), "rows"
    )
    members = frames * rows_here * lax.axis_size("rows") * columns * width_group
    average = totals[0] / members
    squares = totals[1] / members
    inverse = lax.rsqrt(squares - average * average + EPS)
    scaled = (grouped - average[:, None]) * inverse[:, None]
    scaled = scaled.reshape(values.shape) * norm_gain.astype(jnp.float32) + norm_bias.astype(
        jnp.float32
    )
    return jax.nn.silu(scaled).astype(jnp.bfloat16)


def convolve(active, kernel):
    previous = passed_along(active[-2:], "tm", 1)
    extended = jnp.concatenate([previous, active], axis=0)
    padded = padded_2(extended, (("rows", 1),), 1)
    padded = jnp.pad(padded, ((0, 0), (0, 0), (1, 1), (0, 0)))
    result = lax.conv_general_dilated(
        padded[None],
        kernel,
        (1, 1, 1),
        "VALID",
        dimension_numbers=("NDHWC", "DHWIO", "NDHWC"),
        preferred_element_type=jnp.float32,
    )
    return result[0]


def residual_block(values, params):
    first, second, gain_one, bias_one, gain_two, bias_two = params
    active = normalize(values, gain_one, bias_one)
    hidden = convolve(active, first).astype(jnp.bfloat16)
    active = normalize(hidden, gain_two, bias_two)
    return (values.astype(jnp.float32) + convolve(active, second)).astype(jnp.bfloat16)


def plain_body(latents, conv_first, conv_second, gain_first, bias_first, gain_second, bias_second):
    segments = lax.axis_size("segment")
    micro = latents.shape[0]
    per_segment = micro // segments
    position = lax.axis_index("segment")
    small = jnp.stack([gain_first, bias_first, gain_second, bias_second], axis=1)
    small = lax.all_gather(small, "segment", axis=0, tiled=True)
    first = lax.all_gather(conv_first, "segment", axis=0, tiled=True)
    second = lax.all_gather(conv_second, "segment", axis=0, tiled=True)
    outs = []
    for index in range(per_segment):
        values = lax.dynamic_index_in_dim(
            latents, position * per_segment + index, 0, keepdims=False
        )
        for layer in range(first.shape[0]):
            gains = small[layer]
            values = residual_block(
                values, (first[layer], second[layer], gains[0], gains[1], gains[2], gains[3])
            )
        outs.append(values)
    return jnp.stack(outs)


MESH = pl.DeviceIdType.MESH
ROWS = 16
STEPS = 4
PIECES = 4


def group_sums(values):
    lanes = values.shape[-1]
    lane = lax.broadcasted_iota(jnp.int32, values.shape, 1)
    values = values + jnp.where(
        lax.rem(lane, 2) == 0, pltpu.roll(values, lanes - 1, 1), pltpu.roll(values, 1, 1)
    )
    return values + jnp.where(
        lax.rem(lane, 4) < 2, pltpu.roll(values, lanes - 2, 1), pltpu.roll(values, 2, 1)
    )


def tap_block(weights, dt, dy, dx, channels):
    if dt < 0 or dt > 2:
        return jnp.zeros((channels, channels), jnp.bfloat16)
    return weights[dt, dy, dx]


def decode_kernel(
    count,
    latents,
    first,
    second,
    gain_first,
    bias_first,
    gain_second,
    bias_second,
    out,
    staged,
    turned,
    values,
    hidden,
    sibling,
    edges,
    stats,
    active,
    own_sem,
    in_send,
    in_recv,
    stat_send,
    stat_recv,
    edge_send,
    edge_recv,
    sib_send,
    sib_recv,
    out_send,
    out_recv,
    free_sem,
    kernels,
    small,
    param_send,
    param_recv,
    load_sem,
    w_send,
    w_recv,
    half_send,
    half_recv,
    raw_params,
    raw_sem,
):
    frames, height, width, channels = staged.shape
    local_rows = height // count
    both = 2 * height
    row = lax.axis_index("rows")
    segment = lax.axis_index("segment")
    span = lax.axis_index("tm")
    members = frames * height * width * count * (channels // GROUPS)

    def at(rows_index, tm_index):
        return {"rows": rows_index, "tm": tm_index}

    barrier = pltpu.get_barrier_semaphore()
    for k in range(count):
        other = lax.rem(row + k, count)
        if k:
            pl.semaphore_signal(barrier, inc=1, device_id=at(other, span), device_id_type=MESH)
        pl.semaphore_signal(barrier, inc=1, device_id=at(other, 1 - span), device_id_type=MESH)
    for k in range(1, 4):
        pl.semaphore_signal(
            barrier, inc=1, device_id={"segment": segment ^ k}, device_id_type=MESH
        )
    pl.semaphore_wait(barrier, 2 * count + 2)

    given = (first, second)
    layers = kernels.shape[0] // 2
    for k in (0, 3):
        for dy in range(3):
            active[k, dy, width + 2] = jnp.zeros((both, channels), jnp.bfloat16)
    depth = channels // 2

    def tensor_part(ref, half, chunk, chunks):
        rows = pl.ds(pl.multiple_of(half * depth, depth), depth)
        size = 3 // chunks
        return ref.at[pl.ds(chunk * size, size), :, :, rows]

    def chunks_of(j):
        return 3 if j < 4 else 1

    def remote_half(j, chunk, source, to, slot):
        return pltpu.make_async_remote_copy(
            src_ref=tensor_part(source, span, chunk, chunks_of(j)),
            dst_ref=tensor_part(kernels.at[j], span, chunk, chunks_of(j)),
            send_sem=w_send.at[j, slot, chunk],
            recv_sem=w_recv.at[j, chunk],
            device_id={"rows": row ^ 1} if to is None else {"segment": to},
            device_id_type=MESH,
        )

    def core_half(j, chunk, half):
        return pltpu.make_async_remote_copy(
            src_ref=tensor_part(kernels.at[j], half, chunk, chunks_of(j)),
            dst_ref=tensor_part(kernels.at[j], half, chunk, chunks_of(j)),
            send_sem=half_send.at[j, chunk],
            recv_sem=half_recv.at[j, chunk],
            device_id={"tm": 1 - span},
            device_id_type=MESH,
        )

    routes = "ZZVXVVVV"

    def move(name):
        kind, j = name[0], int(name[1])
        route = routes[j]
        away = segment ^ (j // 2)
        source = given[j % 2].at[0]
        each = range(chunks_of(j)) if len(name) == 2 else (int(name[2]),)
        if route == "X":
            first_to = segment ^ 1
            second_to = pass_to = segment ^ 2
            passes = away == 1
        else:
            turn = lax.rem(row + span, 2) if route == "Z" else span
            first_to = segment ^ (1 + turn)
            second_to = pass_to = segment ^ (2 - turn)
            passes = away == 1 + turn
        here = kernels.at[j]
        if kind == "P":

            @pl.when(away == 0)
            def _():
                for c in each:
                    remote_half(j, c, source, first_to, 0).start()

        if kind == "Q":

            @pl.when(away == 0)
            def _():
                for c in each:
                    remote_half(j - 1, c, given[(j - 1) % 2].at[0], first_to, 0).wait_send()
                    remote_half(j, c, source, first_to, 0).start()

        if kind == "S":

            @pl.when(away == 0)
            def _():
                for c in each:
                    remote_half(j, c, source, second_to, 1).start()

        if kind == "F":

            @pl.when(passes)
            def _():
                for c in each:
                    remote_half(j, c, here, pass_to, 0).wait_recv()
                    remote_half(j, c, here, pass_to, 0).start()
                    if route == "Z":
                        remote_half(j, c, here, None, 1).start()
                    core_half(j, c, span).start()

        if kind == "R":

            @pl.when((away > 0) & jnp.logical_not(passes))
            def _():
                for c in each:
                    remote_half(j, c, here, pass_to, 0).wait_recv()
                    core_half(j, c, span).start()

        if kind == "G":

            @pl.when(away > 0)
            def _():
                for c in each:
                    core_half(j, c, 1 - span).wait_recv()

            @pl.when(away == 0)
            def _():
                pltpu.make_async_copy(source, kernels.at[j], load_sem.at[j]).wait()

        if kind == "W":

            @pl.when(away == 0)
            def _():
                for c in each:
                    if j > 0:
                        remote_half(j, c, source, first_to, 0).wait_send()
                    if route != "Z":
                        remote_half(j, c, source, second_to, 1).wait_send()

            @pl.when(passes)
            def _():
                for c in each:
                    remote_half(j, c, here, pass_to, 0).wait_send()
                    if route == "Z":
                        remote_half(j, c, here, None, 1).wait_send()

            @pl.when(away > 0)
            def _():
                for c in each:
                    core_half(j, c, span).wait_send()

    plan = {
        "start": ("P0", "P2", "P4", "P6"),
        "early": ("Q1", "F0"),
        "a0": ("F1", "R0",),
        "r0": ("F2", "S2", "S4"),
        "b0": ("G0",),
        "a1": ("S3", "F4", "F30", "R1",),
        "b1": ("G1",),
        "a2": ("P7", "F32", "R2", "F6",),
        "b2": ("G2",),
        "a3": ("F5", "R4", "R3",),
        "b3": ("G3",),
        "a4": ("F7", "R6",),
        "b4": ("G4",),
        "a5": ("R5",),
        "b5": ("G5",),
        "r6": ("R7",),
        "b6": ("G6",),
        "b7": ("G7",),
        "mid": ("P3",),
        "r1": ("P5", "S6", "F31",),
        "r2": ("S5",),
        "r3": ("S7",),
        "end": ("W0", "W1", "W2", "W3", "W4", "W5", "W6", "W7"),
    }

    def moves(point):
        for name in plan.get(point, ()):
            move(name)

    def moves_at(letter, which, layer):
        for known in range(layers):
            point = letter + str(2 * known + which)
            if point in plan:

                @pl.when(layer == known)
                def _(point=point):
                    moves(point)

    def incoming(k, me, to):
        return pltpu.make_async_remote_copy(
            src_ref=latents.at[segment, :, :, pl.ds(pl.multiple_of(to * width, width), width)],
            dst_ref=staged.at[:, pl.ds(me * local_rows, local_rows)],
            send_sem=in_send.at[k],
            recv_sem=in_recv.at[me],
            device_id=at(to, span),
            device_id_type=MESH,
        )

    moves("start")
    for k in range(1, count):
        incoming(k, row, lax.rem(row + k, count)).start()
    for j in range(2 * layers):

        @pl.when(segment == j // 2)
        def _(j=j):
            pltpu.make_async_copy(given[j % 2].at[0], kernels.at[j], load_sem.at[j]).start()

    index = lax.broadcasted_iota(jnp.int32, (8, channels), 0)
    raw = [
        pltpu.make_async_copy(ref, raw_params.at[k], raw_sem.at[k])
        for k, ref in enumerate((gain_first, bias_first, gain_second, bias_second))
    ]
    for copy in raw:
        copy.start()
    for copy in raw:
        copy.wait()
    packed = jnp.zeros((8, channels), jnp.float32)
    for k in range(4):
        packed = jnp.where(index == k, raw_params[k].astype(jnp.float32), packed)
    small[segment] = packed

    def param_copy(k, me):
        return pltpu.make_async_remote_copy(
            src_ref=small.at[me],
            dst_ref=small.at[me],
            send_sem=param_send.at[k],
            recv_sem=param_recv.at[me],
            device_id={"segment": segment ^ k},
            device_id_type=MESH,
        )

    for k in range(1, 4):
        param_copy(k, segment).start()
    own = pltpu.make_async_copy(
        latents.at[segment, :, :, pl.ds(pl.multiple_of(row * width, width), width)],
        staged.at[:, pl.ds(row * local_rows, local_rows)],
        own_sem,
    )
    own.start()
    moves("early")
    own.wait()
    for k in range(1, count):
        other = lax.rem(row + k, count)
        incoming(k, other, row).wait_recv()
    moves("mid")

    for f in range(frames):
        turned[f, : height * width] = (
            staged[f].astype(jnp.float32).reshape(height * width, channels)
        )
    zero = jnp.zeros((height, channels), jnp.float32)

    def turn(x, carry):
        total, squares = carry
        for q in range(2):
            tile = jnp.concatenate(
                [turned[q + 2 * p, pl.ds(x, height, stride=width)] for p in range(2)], axis=0
            )
            values[q, x] = tile.astype(jnp.bfloat16)
            total = total + tile[:height] + tile[height:]
            tile = tile * tile
            squares = squares + tile[:height] + tile[height:]
        return total, squares

    partial = lax.fori_loop(0, width, turn, (zero, zero), unroll=16)

    def stat_copy(par, k, me, to, tm_from, tm_to):
        slot = tm_from * count + me
        cross = 0 if tm_from is tm_to else count
        return pltpu.make_async_remote_copy(
            src_ref=stats.at[par, slot],
            dst_ref=stats.at[par, slot],
            send_sem=stat_send.at[par, k + cross],
            recv_sem=stat_recv.at[par, slot],
            device_id=at(to, tm_to),
            device_id_type=MESH,
        )

    def edge_copy(par, source, side, tm_from, tm_to, to):
        return pltpu.make_async_remote_copy(
            src_ref=source.at[:, width - 1 if side == 0 else 0],
            dst_ref=edges.at[par, side, tm_from],
            send_sem=edge_send.at[par, side, tm_to],
            recv_sem=edge_recv.at[par, side, tm_from],
            device_id=at(to, tm_to),
            device_id_type=MESH,
        )

    def sib_copy(par, source):
        return pltpu.make_async_remote_copy(
            src_ref=source,
            dst_ref=sibling.at[par],
            send_sem=sib_send.at[par],
            recv_sem=sib_recv.at[par],
            device_id=at(row, 1),
            device_id_type=MESH,
        )

    def each_send(par, source, act):
        for k in range(1, count):
            act(stat_copy(par, k, row, lax.rem(row + k, count), span, span))

        @pl.when(span == 0)
        def _():
            for k in range(count):
                act(stat_copy(par, k, row, lax.rem(row + k, count), 0, 1))

        for side, there in ((0, row < count - 1), (1, row > 0)):

            @pl.when(there)
            def _(side=side):
                to = row + 1 if side == 0 else row - 1
                act(edge_copy(par, source, side, span, span, to))

                @pl.when(span == 0)
                def _():
                    act(edge_copy(par, source, side, 0, 1, to))

        @pl.when(span == 0)
        def _():
            act(sib_copy(par, source))

    def exchange(par, source, partial):
        index = lax.broadcasted_iota(jnp.int32, (8, channels), 0)
        total = jnp.sum(partial[0], axis=0, keepdims=True)
        squares = jnp.sum(partial[1], axis=0, keepdims=True)
        stats[par, span * count + row] = jnp.where(
            index == 0, total, jnp.where(index == 1, squares, 0.0)
        )
        each_send(par, source, lambda copy: copy.start())

    def finish_sends(par, source):
        each_send(par, source, lambda copy: copy.wait_send())

    def receive(par, source):
        for side, there in ((0, row > 0), (1, row < count - 1)):

            @pl.when(there)
            def _(side=side):
                edge_copy(par, source, side, span, span, row).wait_recv()

                @pl.when(span == 1)
                def _():
                    edge_copy(par, source, side, 0, 1, row).wait_recv()

        @pl.when(span == 1)
        def _():
            sib_copy(par, source).wait_recv()
            for k in range(count):
                stat_copy(par, k, lax.rem(row + k, count), row, 0, 1).wait_recv()

        for k in range(1, count):
            stat_copy(par, k, lax.rem(row + k, count), row, span, span).wait_recv()

    def moments(par, base, gain):
        total = stats[par, base]
        for k in range(1, count):
            total = total + stats[par, base + k]
        total = group_sums(total) / members
        average = total[0:1]
        return average, lax.rsqrt(total[1:2] - average * average + EPS) * gain

    def layer_half(par, source, gain, bias, weights, store):
        mine = moments(par, span * count, gain)
        before = moments(par, 0, gain)
        later = span > 0
        index = lax.broadcasted_iota(jnp.int32, (1, height, channels), 1)

        def silu(tile, moment):
            half = ((tile - moment[0]) * moment[1] + bias) * 0.5
            return half + half * jnp.tanh(half)

        def shifted(a, dy):
            if dy == 0:
                return jnp.where(index == 0, 0.0, pltpu.roll(a, 1, 1))
            if dy == 2:
                return jnp.where(index == height - 1, 0.0, pltpu.roll(a, height - 1, 1))
            return a

        def put(q, x, size, tile, older, valid):
            a = silu(tile.astype(jnp.float32), mine).reshape(2 * size, height, channels)
            b = silu(older.astype(jnp.float32)[:, height:], before)
            b = jnp.where(later, b, 0.0)
            if valid is not None:
                a = jnp.where(valid, a, 0.0)
                b = jnp.where(valid, b, 0.0)
            for dy in range(3):
                now = shifted(a, dy).reshape(size, both, channels)
                old = shifted(b, dy)
                active[2 + q, dy, x : x + size] = now.astype(jnp.bfloat16)
                active[q, dy, x : x + size] = jnp.concatenate(
                    [old, now[:, :height]], axis=1
                ).astype(jnp.bfloat16)

        def columns_at(x, size):
            for q in range(2):
                put(
                    q, x + 1, size, source[q, x : x + size], sibling[par, q, x : x + size], None
                )

        def border(side):
            there = row > 0 if side == 0 else row < count - 1
            for q in range(2):
                put(
                    q,
                    0 if side == 0 else width + 1,
                    1,
                    edges[par, side, span, q][None],
                    edges[par, side, 0, q][None],
                    there,
                )

        def pixels(k, dy, x, step):
            return active[k, dy, x : x + step].reshape(step * both, channels)

        def lone(k, dt, x, step):
            left, right = [], []
            for dy in range(3):
                left += [pixels(k, dy, x, step + 1), pixels(k, dy, x + 2, step + 1)]
                for taps in ((0, 1), (2, None)):
                    right.append(
                        jnp.concatenate(
                            [
                                tap_block(weights, -1 if dx is None else dt, dy, dx, channels)
                                for dx in taps
                            ],
                            axis=1,
                        )
                    )
            part = jnp.dot(
                jnp.concatenate(left, axis=1),
                jnp.concatenate(right, axis=0),
                preferred_element_type=jnp.float32,
            )
            return part[: step * both, :channels] + part[both:, channels:]

        def products(x, step):
            left, right = [], []
            for dy in range(3):
                for dx in range(3):
                    for k in (1, 2):
                        left.append(pixels(k, dy, x + dx, step))
                        right.append(
                            jnp.concatenate(
                                [tap_block(weights, k - q, dy, dx, channels) for q in range(2)],
                                axis=1,
                            )
                        )
            shared = jnp.dot(
                jnp.concatenate(left, axis=1),
                jnp.concatenate(right, axis=0),
                preferred_element_type=jnp.float32,
            )
            result = [
                shared[:, :channels] + lone(0, 0, x, step),
                shared[:, channels:] + lone(3, 2, x, step),
            ]
            sums = []
            for q in range(2):
                tile = store(
                    q,
                    x,
                    step,
                    result[q].reshape(step, both, channels),
                )
                tile = tile.astype(jnp.float32).reshape(-1, height, channels)
                sums.append((jnp.sum(tile, axis=0), jnp.sum(tile * tile, axis=0)))
            return [sums[0][i] + sums[1][i] for i in range(2)]

        step, piece = width // STEPS, width // PIECES
        ready, partial = 0, None
        border(0)
        for x in range(0, width, step):
            while ready < min(x + step + 1, width):
                columns_at(ready, piece)
                ready += piece
                if ready == width:
                    border(1)
            sums = products(x, step)
            partial = sums if partial is None else [partial[i] + sums[i] for i in range(2)]
        return tuple(partial)

    def store_hidden(q, x, step, tile):
        tile = tile.astype(jnp.bfloat16)
        hidden[q, x : x + step] = tile
        return tile

    def store_values(q, x, step, tile):
        tile = (values[q, x : x + step].astype(jnp.float32) + tile).astype(jnp.bfloat16)
        values[q, x : x + step] = tile
        return tile

    def give(when):
        @pl.when((span == 1) & when)
        def _():
            pl.semaphore_signal(free_sem, inc=1, device_id=at(row, 0), device_id_type=MESH)

    def take(when):
        @pl.when((span == 0) & when)
        def _():
            pl.semaphore_wait(free_sem, 1)

    exchange(0, values, partial)
    for k in range(1, count):
        incoming(k, row, lax.rem(row + k, count)).wait_send()
    for k in range(1, 4):
        param_copy(k, segment ^ k).wait_recv()

    @pl.loop(0, layers)
    def _(layer):
        moves_at("a", 0, layer)
        receive(0, values)
        moves_at("r", 0, layer)
        give(layer > 0)
        moves_at("b", 0, layer)
        partial = layer_half(
            0,
            values,
            small[layer, 0:1],
            small[layer, 1:2],
            kernels.at[2 * layer],
            store_hidden,
        )
        take(layer > 0)
        exchange(1, hidden, partial)
        finish_sends(0, values)
        moves_at("a", 1, layer)
        receive(1, hidden)
        moves_at("r", 1, layer)
        give(layer < layers - 1)
        moves_at("b", 1, layer)
        partial = layer_half(
            1,
            hidden,
            small[layer, 2:3],
            small[layer, 3:4],
            kernels.at[2 * layer + 1],
            store_values,
        )

        @pl.when(layer < layers - 1)
        def _():
            take(layer >= 0)
            exchange(0, values, partial)

        finish_sends(1, hidden)

    for q in range(2):
        whole = values[q].astype(jnp.float32)
        for p in range(2):
            turned[q + 2 * p, : height * width] = whole[
                :, p * height : (p + 1) * height
            ].reshape(height * width, channels)
    def outgoing(k, me, to):
        return pltpu.make_async_remote_copy(
            src_ref=staged.at[:, pl.ds(to * local_rows, local_rows)],
            dst_ref=out.at[0, :, :, pl.ds(pl.multiple_of(me * width, width), width)],
            send_sem=out_send.at[k],
            recv_sem=out_recv.at[me],
            device_id=at(to, span),
            device_id_type=MESH,
        )

    def stage(to):
        for f in range(frames):
            for i in range(local_rows):
                y = to * local_rows + i
                staged[f, y] = turned[f, pl.ds(y, width, stride=height)].astype(jnp.bfloat16)

    for k in range(1, count):
        stage(lax.rem(row + k, count))
        outgoing(k, row, lax.rem(row + k, count)).start()
    stage(row)
    own = pltpu.make_async_copy(
        staged.at[:, pl.ds(row * local_rows, local_rows)],
        out.at[0, :, :, pl.ds(pl.multiple_of(row * width, width), width)],
        own_sem,
    )
    own.start()
    own.wait()
    moves("end")
    for k in range(1, 4):
        param_copy(k, segment).wait_send()
    for k in range(1, count):
        other = lax.rem(row + k, count)
        outgoing(k, other, row).wait_recv()
        outgoing(k, row, other).wait_send()


def body(latents, conv_first, conv_second, gain_first, bias_first, gain_second, bias_second):
    micro, frames, local_rows, columns, channels = latents.shape
    count = lax.axis_size("rows")
    width = columns // count
    height = local_rows * count
    both = 2 * height
    dma = pltpu.SemaphoreType.DMA
    return pl.pallas_call(
        functools.partial(decode_kernel, count),
        out_shape=jax.ShapeDtypeStruct((1, frames, local_rows, columns, channels), jnp.bfloat16),
        in_specs=[pl.BlockSpec(memory_space=pltpu.HBM)] * 7,
        out_specs=pl.BlockSpec(memory_space=pltpu.VMEM),
        scratch_shapes=[
            pltpu.VMEM((frames, height, width, channels), jnp.bfloat16),
            pltpu.VMEM((frames, height * width + height + width, channels), jnp.float32),
            pltpu.VMEM((2, width, both, channels), jnp.bfloat16),
            pltpu.VMEM((2, width, both, channels), jnp.bfloat16),
            pltpu.VMEM((2, 2, width, both, channels), jnp.bfloat16),
            pltpu.VMEM((2, 2, 2, 2, both, channels), jnp.bfloat16),
            pltpu.VMEM((2, 2 * count, 8, channels), jnp.float32),
            pltpu.VMEM((4, 3, width + 3, both, channels), jnp.bfloat16),
            dma,
            dma((count,)),
            dma((count,)),
            dma((2, 2 * count)),
            dma((2, 2 * count)),
            dma((2, 2, 2)),
            dma((2, 2, 2)),
            dma((2,)),
            dma((2,)),
            dma((count,)),
            dma((count,)),
            pltpu.SemaphoreType.REGULAR,
            pltpu.VMEM((8,) + conv_first.shape[1:], jnp.bfloat16),
            pltpu.VMEM((4, 8, channels), jnp.float32),
            dma((4,)),
            dma((4,)),
            dma((8,)),
            dma((8, 2, 3)),
            dma((8, 3)),
            dma((8, 3)),
            dma((8, 3)),
            pltpu.VMEM((4, 1, channels), jnp.bfloat16),
            dma((4,)),
        ],
        compiler_params=pltpu.CompilerParams(
            collective_id=0, has_side_effects=True, vmem_limit_bytes=64 * 2**20 - 2**17
        ),
    )(latents, conv_first, conv_second, gain_first, bias_first, gain_second, bias_second)


def solution(mesh):
    in_specs = (
        P(None, "tm", "rows", None, None),
        P("segment", None, None, None, None, None),
        P("segment", None, None, None, None, None),
        P("segment", None),
        P("segment", None),
        P("segment", None),
        P("segment", None),
    )
    out_specs = P("segment", "tm", "rows", None, None)
    sizes = dict(mesh.shape)

    def run(latents, *params):
        micro, frames, height, columns, channels = latents.shape
        count = sizes["rows"]
        fits = (
            micro == sizes["segment"] == 4
            and params[0].shape == (4, 3, 3, 3, channels, channels)
            and count % 2 == 0
            and sizes["tm"] == 2
            and frames == 8
            and height % (8 * 1) == 0
            and columns % (count * ROWS) == 0
            and channels == 4 * GROUPS
        )
        inner = body if fits else plain_body
        return jax.shard_map(
            inner, mesh=mesh, in_specs=in_specs, out_specs=out_specs, check_vma=False
        )(latents, *params)

    return run
```
